32 devices in a mesh: dp: 8 (over z, x), mp: 4 (over y, core).
Axes of the slice: x: 2, y: 2, z: 4, core: 2. Of those that a mesh axis runs over, the one named last changes fastest.
Arguments:
- tokens: bfloat16 [32768, 512], P(('dp', 'mp')), may hold values from -6 to 6
- gain_mix: bfloat16 [512], P(('dp', 'mp')), may hold values from 0.25 to 1.75
- gain_mlp: bfloat16 [512], P(('dp', 'mp')), may hold values from 0.25 to 1.75
- forget_weight: bfloat16 [512, 1024], P(('dp', 'mp')), may hold values from -0.25 to 0.25
- input_weight: bfloat16 [512, 1024], P(('dp', 'mp')), may hold values from -0.25 to 0.25
- candidate_weight: bfloat16 [512, 1024], P(('dp', 'mp')), may hold values from -0.25 to 0.25
- input_gate_bias: bfloat16 [1024], P(('dp', 'mp')), may hold values from -11 to -3
- output_weight: bfloat16 [1024, 512], P(('dp', 'mp')), may hold values from -1 to 1
- up_weight: bfloat16 [512, 2048], P('dp', 'mp'), may hold values from -0.25 to 0.25
- down_weight: bfloat16 [2048, 512], P('mp', 'dp'), may hold values from -0.1875 to 0.1875
- cotangent: bfloat16 [32768, 512], P(('dp', 'mp')), may hold values from -6 to 6
Outputs:
- block_out: bfloat16 [32768, 512], P(('dp', 'mp'))
- tokens_grad: float32 [32768, 512], P(('dp', 'mp'))
- gain_mix_grad: float32 [512], P(('dp', 'mp'))
- gain_mlp_grad: float32 [512], P(('dp', 'mp'))
- forget_grad: float32 [512, 1024], P(('dp', 'mp'))
- input_grad: float32 [512, 1024], P(('dp', 'mp'))
- cand_grad: float32 [512, 1024], P(('dp', 'mp'))
- bias_grad: float32 [1024], P(('dp', 'mp'))
- out_grad: float32 [1024, 512], P(('dp', 'mp'))
- up_grad: float32 [512, 2048], P('dp', 'mp')
- down_grad: float32 [2048, 512], P('mp', 'dp')
The draws below stay inside these ranges and needn't reach their ends.
All inputs are finite; a program needn't handle non-finite values.
Results may differ from the reference program's by a relative error of at most 0.011.
Values may be sent and summed in bfloat16 or wider, within the bound.
No kernel may reach another device: no remote copies, remote signals or barrier semaphores. Data moves between devices by JAX's collectives and lax.ppermute only.
A program may use at most 192 MiB of HBM per device.

```python
import jax
import jax.numpy as jnp
from jax import lax

D = 512
H = 1024
F = 2048
LEN = 1024
TOKENS = 32768


def draw_input_gate_bias(key, part):
    key = jax.random.fold_in(key, 7)
    lower, upper = (-10.0, -3.0)
    values = jax.random.uniform(key, (H,), jnp.float32, lower, upper)
    return values.astype(jnp.bfloat16)


def spiked(values, stream_key, source, target, parts, factor):
    def block_of(dim):
        return (jnp.arange(values.shape[dim]) // (values.shape[dim] // parts)).reshape((-1,) + (1,) * (values.ndim - 1 - dim))

    first = jax.random.permutation(stream_key, parts)[block_of(target)]
    far = (block_of(target) + parts // 2) % parts
    return jnp.where((block_of(source) == first) | (block_of(source) == far), factor * values, values)


def level_of(rng, dims, pieces, smallest, high):
    level, own = 1.0, jax.random.fold_in(rng, 6)
    for dim, shards_of in pieces:
        heights = jnp.exp(jax.random.uniform(jax.random.fold_in(own, dim), (shards_of,), jnp.float32, smallest / len(pieces), high / len(pieces)))
        level = level * jnp.repeat(heights, dims[dim] // shards_of).reshape([-1 if axis == dim else 1 for axis in range(len(dims))])
    return level


def noise(rng, extent, width, limit, shards=(), held_as=jnp.bfloat16):
    drawn = width * jax.random.normal(rng, extent, jnp.float32)
    if shards:
        drawn = drawn * level_of(rng, extent, shards, -0.22, 0.18)
    return jnp.clip(drawn, -limit, limit).astype(held_as)


def heavy_noise(key, extent, scale, limit, split, heavy, kind=jnp.bfloat16):
    values = scale * jax.random.normal(key, extent, jnp.float32)
    if split:
        values = values * level_of(key, extent, split, -0.22, 0.18)
    return jnp.clip(spiked(values, jax.random.fold_in(key, 3), *heavy), -limit, limit).astype(kind)


def setup_inputs(seed: int = 0) -> dict:
    keys = jax.random.split(jax.random.key(seed), 12)
    tokens = heavy_noise(keys[0], (TOKENS, D), 1.0, 6.0, ((0, 32),), (0, 1, 32, 2.75))
    gain_mix = jnp.clip(1.0 + 0.15 * jax.random.normal(keys[1], (D,), jnp.float32), 0.25, 1.75).astype(jnp.bfloat16)
    gain_mlp = jnp.clip(1.0 + 0.15 * jax.random.normal(keys[2], (D,), jnp.float32), 0.25, 1.75).astype(jnp.bfloat16)
    forget_weight = noise(keys[3], (D, H), D ** -0.5, 0.25, ((0, 32),))
    input_weight = noise(keys[4], (D, H), D ** -0.5, 0.25, ((0, 32),))
    candidate_weight = noise(keys[5], (D, H), D ** -0.5, 0.25, ((0, 32),))
    input_gate_bias = draw_input_gate_bias(jax.random.fold_in(keys[11], 71), 0)
    output_weight = noise(keys[7], (H, D), (H // 32) ** -0.5, 1.0, ((0, 32),))
    up_weight = noise(keys[8], (D, F), D ** -0.5, 0.25, ((0, 8), (1, 4)))
    down_weight = noise(keys[9], (F, D), (F // 2) ** -0.5, 0.1875, ((0, 4), (1, 8)))
    cotangent = noise(keys[10], (TOKENS, D), 1.0, 6.0, ((0, 32),))
    return {"tokens": tokens, "gain_mix": gain_mix, "gain_mlp": gain_mlp, "forget_weight": forget_weight, "input_weight": input_weight, "candidate_weight": candidate_weight, "input_gate_bias": input_gate_bias, "output_weight": output_weight, "up_weight": up_weight, "down_weight": down_weight, "cotangent": cotangent}


EPSILON = 1e-06

@jax.custom_vjp
def reduced_precision(v):
    return lax.optimization_barrier(v.astype(jnp.bfloat16)).astype(jnp.float32)

@jax.custom_vjp
def reduced_backward(v):
    return v

def low_keep(v):
    return (reduced_precision(v), None)

def low_pass(kept, grad):
    return (grad,)

def back_keep(v):
    return (v, None)

def back_low(kept, grad):
    return (reduced_precision(grad),)
reduced_precision.defvjp(low_keep, low_pass)
reduced_backward.defvjp(back_keep, back_low)

def combine_steps(earlier, later):
    return (earlier[0] * later[0], later[0] * earlier[1] + later[1])

def rms_rows(values):
    return values * lax.rsqrt(lax.optimization_barrier(jnp.mean(values * values, axis=-1, keepdims=True)) + EPSILON)

def forward(block, gain_mix, gain_mlp, forget_weight, input_weight, candidate_weight, input_gate_bias, output_weight, up_weight, down_weight):
    highest_precision = lax.Precision.HIGHEST
    first_normed_input = reduced_precision(rms_rows(block) * gain_mix)
    forget_gate = reduced_backward(jnp.einsum('fzi,ij->fzj', first_normed_input, forget_weight, precision=highest_precision))
    input_gate = reduced_backward(jnp.einsum('fzi,ij->fzj', first_normed_input, input_weight, precision=highest_precision) + input_gate_bias)
    candidate_rows = reduced_backward(jnp.einsum('fzi,ij->fzj', first_normed_input, candidate_weight, precision=highest_precision))
    forget = jax.nn.sigmoid(jax.nn.log_sigmoid(forget_gate) - jax.nn.log_sigmoid(input_gate))
    hidden_state = lax.associative_scan(combine_steps, (forget, (1.0 - forget) * candidate_rows), axis=1)[1]
    mixer_output = reduced_backward(jnp.einsum('omp,pj->omj', reduced_precision(hidden_state), output_weight, precision=highest_precision))
    residual_rows = block + mixer_output
    second_normed_input = reduced_precision(rms_rows(residual_rows) * gain_mlp)
    preactivation = reduced_backward(jnp.einsum('axj,jr->axr', second_normed_input, up_weight, precision=highest_precision))
    activation_rows = reduced_precision(jax.nn.gelu(preactivation, approximate=True))
    return residual_rows + jnp.einsum('zhc,cr->zhr', activation_rows, down_weight, precision=highest_precision)

def reference(tokens, gain_mix, gain_mlp, forget_weight, input_weight, candidate_weight, input_gate_bias, output_weight, up_weight, down_weight, cotangent):
    params = tuple((item.astype(jnp.float32) for item in (gain_mix, gain_mlp, forget_weight, input_weight, candidate_weight, input_gate_bias, output_weight, up_weight, down_weight)))
    nseq = TOKENS // LEN
    group = 4 if nseq % 4 == 0 else 2 if nseq % 2 == 0 else 1
    blocks = tokens.astype(jnp.float32).reshape(nseq // group, group, LEN, D)
    cots = cotangent.astype(jnp.float32).reshape(nseq // group, group, LEN, D)

    def step(totals, pair):
        block, cot = pair
        result, pull = jax.vjp(forward, block, *params)
        grads = pull(cot)
        totals = tuple((acc + item for acc, item in zip(totals, grads[1:])))
        return (totals, (result.astype(jnp.bfloat16), grads[0]))
    start_totals = tuple((jnp.zeros(item.shape, jnp.float32) for item in params))
    totals, (outputs, tok_grads) = lax.scan(step, start_totals, (blocks, cots))
    return (outputs.reshape(TOKENS, D), tok_grads.reshape(TOKENS, D), totals[0], totals[1], totals[2], totals[3], totals[4], totals[5], totals[6], totals[7], totals[8])
```

```python
import functools

import jax
import jax.numpy as jnp
import numpy as np
from jax import lax
from jax.experimental import pallas as pl
from jax.experimental.pallas import tpu as pltpu
from jax.sharding import PartitionSpec as P

LEN = 1024
EPSILON = 1e-06
AXES = ("dp", "mp")
SLOTS = 32
CHUNKS = 8
LANES = 256
BF = jnp.bfloat16
F32 = jnp.float32
VMEM_LIMIT = 60 * 1024 * 1024
C0 = 0.7978845608028654
C1 = C0 * 0.044715


def params():
    return pltpu.CompilerParams(vmem_limit_bytes=VMEM_LIMIT)


def dot(a, b, dims=((1,), (0,))):
    return lax.dot_general(a, b, (dims, ((), ())), preferred_element_type=F32)


def whole(shape):
    return pl.BlockSpec(shape, lambda *_: (0,) * len(shape), pipeline_mode=pl.Buffered(1))


def aligned(start, size):
    return pl.ds(pl.multiple_of(start, size), size)


def spread(small, offset, piece, width):
    lane = lax.broadcasted_iota(jnp.int32, (LANES, width), 0)
    column = lax.broadcasted_iota(jnp.int32, (LANES, width), 1)
    pick = (lane == offset + column % piece).astype(BF)
    placed = dot(small.astype(BF), pick)
    row = lax.broadcasted_iota(jnp.int32, (SLOTS, width), 0)
    col = lax.broadcasted_iota(jnp.int32, (SLOTS, width), 1)
    return jnp.sum(jnp.where(col // piece == row, placed, 0.0), axis=0, keepdims=True)


def collect(vector, offset, piece):
    width = vector.shape[1]
    row = lax.broadcasted_iota(jnp.int32, (SLOTS, width), 0)
    col = lax.broadcasted_iota(jnp.int32, (SLOTS, width), 1)
    kept = jnp.where(col // piece == row, vector, 0.0).astype(BF)
    column = lax.broadcasted_iota(jnp.int32, (width, LANES), 0)
    lane = lax.broadcasted_iota(jnp.int32, (width, LANES), 1)
    pick = (lane == offset + column % piece).astype(BF)
    return dot(kept, pick)


def mixer_forward(dev_ref, x_ref, g0, g1, g2, g3, hb_ref, f_ref, u1_ref, u2_ref, w_ref, xn_ref, gain_ref,
                  small, kf_s, ki_s, kc_s, c1_s, bias_s):
    step = pl.program_id(0)
    parts = (g0, g1, g2, g3)
    per = SLOTS // 4
    nblk = (g0.shape[1] - 16) // 48
    tail = 48 * nblk

    @pl.when(step == 0)
    def _():
        for s in range(SLOTS):
            d = dev_ref[s]
            row = parts[s // per][s % per, tail : tail + 16, :].astype(F32)
            small[pl.ds(d, 1), :] = row[0:1, :]
        values = small[...]
        width = x_ref.shape[1]
        piece = width // SLOTS
        chans = nblk * LANES
        gmix = spread(values, 0, piece, width)
        gmlp = spread(values, piece, piece, width)
        bias = spread(values, 2 * piece, chans // SLOTS, chans)
        gain_ref[0:1, :] = gmix
        gain_ref[1:2, :] = gmlp
        for b in range(nblk):
            bias_s[b, 0:1, :] = bias[:, b * LANES : (b + 1) * LANES]

        def rows(i, _):
            at = aligned(i * 128, 128)
            v = x_ref[at, :].astype(F32)
            scale = lax.rsqrt(jnp.mean(v * v, axis=-1, keepdims=True) + EPSILON)
            xn_ref[at, :] = ((v * scale) * gmix).astype(BF)
            return 0

        lax.fori_loop(0, x_ref.shape[0] // 128, rows, 0)

    for s in range(SLOTS):
        d = dev_ref[s]
        for w in range(3):
            src = aligned((w * nblk + step) * 16, 16)
            w_ref[w, aligned(d * 16, 16), :] = parts[s // per][s % per, src, :]

    xn = xn_ref[...]
    kf_s[...] = dot(xn, w_ref[0])
    ki_s[...] = dot(xn, w_ref[1])
    kc_s[...] = dot(xn, w_ref[2])
    bias = bias_s[step, 0:1, :]
    zeros = jnp.zeros((CHUNKS, LANES), F32)
    tile = 4 * CHUNKS
    count = x_ref.shape[0] // tile

    def first(i, carry):
        h, prod = carry
        at = aligned(i * tile, tile)
        kf = kf_s[at, :]
        ki = ki_s[at, :] + bias
        kc = kc_s[at, :]
        p = jnp.exp(-jnp.abs(kf))
        q = jnp.exp(-jnp.abs(ki))
        w = jnp.minimum(ki, 0.0) - jnp.minimum(kf, 0.0)
        e = jnp.exp(-jnp.abs(w))
        onep = 1.0 + p
        oneq = 1.0 + q
        low = w <= 0.0
        a = jnp.where(low, oneq, e * oneq)
        b = jnp.where(low, e * onep, onep)
        inv = 1.0 / (a + b)
        forget = a * inv
        other = b * inv
        both = forget * other
        f_ref[at, :] = forget
        drive = other * kc
        ki_s[at, :] = drive
        kf_s[at, :] = both * jnp.where(kf >= 0.0, p, 1.0) / onep
        c1_s[at, :] = -both * jnp.where(ki >= 0.0, q, 1.0) / oneq
        for k in range(4):
            part = slice(k * CHUNKS, (k + 1) * CHUNKS)
            h = forget[part] * h + drive[part]
            prod = prod * forget[part]
        return h, prod

    last, prod = lax.fori_loop(0, count, first, (zeros, zeros + 1.0))
    sub = lax.broadcasted_iota(jnp.int32, (CHUNKS, LANES), 0)
    start = zeros
    for s in range(CHUNKS - 1):
        moved = pltpu.roll(last + prod * start, 1, 0)
        start = jnp.where(sub == s + 1, moved, start)

    def second(i, h):
        at = aligned(i * tile, tile)
        forget = f_ref[at, :]
        drive = ki_s[at, :]
        kc = kc_s[at, :]
        before, after = [], []
        for k in range(4):
            part = slice(k * CHUNKS, (k + 1) * CHUNKS)
            before.append(h)
            h = forget[part] * h + drive[part]
            after.append(h)
        diff = jnp.concatenate(before, axis=0) - kc
        hb_ref[at, :] = jnp.concatenate(after, axis=0).astype(BF)
        u1_ref[at, :] = (kf_s[at, :] * diff).astype(BF)
        u2_ref[at, :] = (c1_s[at, :] * diff).astype(BF)
        return h

    lax.fori_loop(0, count, second, start)


def feed_forward(dev_ref, slot_ref, cols_ref, hb_ref, x_ref, dy_ref, gain_ref, g0, g1, g2, g3,
                 out_ref, dy1_ref, dmix_ref, wo_ref, small_ref, keep_ref, send_ref,
                 buf, sems, y1_s, xn_s, xnt_s, dyt_s, acc_s, dxn_s, up_s, dn_s, upg_s, dng_s):
    step = pl.program_id(0)
    parts = (g0, g1, g2, g3)
    per = SLOTS // 4
    tokens, width = x_ref.shape
    hid = up_s.shape[1]
    shard = buf.shape[1] - 32
    half = shard // 2
    rows_of = width // half
    copies = [pltpu.make_async_copy(parts[i], buf.at[pl.ds(i * per, per)], sems.at[i]) for i in range(4)]

    @pl.when(step == 0)
    def _():
        for c in copies:
            c.start()
        for c in copies:
            c.wait()
        for s in range(SLOTS):
            wo_ref[aligned(dev_ref[s] * 32, 32), :] = buf[s, shard : shard + 32, :]

        def rows(i, _):
            at = aligned(i * 256, 256)
            y1 = x_ref[at, :].astype(F32) + dot(hb_ref[at, :], wo_ref[...])
            y1_s[at, :] = y1
            scale = lax.rsqrt(jnp.mean(y1 * y1, axis=-1, keepdims=True) + EPSILON)
            xn = ((y1 * scale) * gain_ref[1:2, :]).astype(BF)
            xn_s[at, :] = xn
            xnt_s[:, aligned(i * 256, 256)] = xn.T
            dyt_s[:, aligned(i * 256, 256)] = dy_ref[at, :].T
            return 0

        lax.fori_loop(0, tokens // 256, rows, 0)
        acc_s[...] = jnp.zeros_like(acc_s)
        dxn_s[...] = jnp.zeros_like(dxn_s)

    block = cols_ref[step]
    for r in range(rows_of):
        s = slot_ref[r * 4 + block]
        up_s[r * half : (r + 1) * half, :] = buf[s, 0:half, :]
        dn_s[r * half : (r + 1) * half, :] = buf[s, half : 2 * half, :]

    upg_s[...] = jnp.zeros_like(upg_s)
    dng_s[...] = jnp.zeros_like(dng_s)

    def rows(i, _):
        at = aligned(i * 256, 256)
        xn = xn_s[at, :]
        pre = dot(xn, up_s[...])
        dact = dot(dy_ref[at, :], dn_s[...])
        sq = pre * pre
        gate = 0.5 + 0.5 * jnp.tanh(pre * (C0 + C1 * sq))
        value = pre * gate
        act = value.astype(BF)
        slope = gate + value * (1.0 - gate) * (2.0 * C0 + 6.0 * C1 * sq)
        dpre = (slope * dact).astype(BF)
        acc_s[at, :] += dot(act, dn_s[...], ((1,), (1,)))
        dxn_s[at, :] += dot(dpre, up_s[...], ((1,), (1,)))
        upg_s[...] += dot(xnt_s[:, at], dpre)
        dng_s[...] += dot(dyt_s[:, at], act)
        return 0

    lax.fori_loop(0, tokens // 256, rows, 0)

    def give(target, base):
        for r in range(rows_of):
            s = slot_ref[r * 4 + block] - base
            target[s, 0:half, :] = upg_s[r * half : (r + 1) * half, :].astype(BF)
            target[s, half : 2 * half, :] = dng_s[r * half : (r + 1) * half, :].astype(BF)

    @pl.when(step < 2)
    def _():
        give(send_ref, SLOTS // 2)

    @pl.when(step >= 2)
    def _():
        give(keep_ref, 0)

    @pl.when(step == 3)
    def _():
        gain = gain_ref[1:2, :]

        def rows(i, total):
            at = aligned(i * 128, 128)
            y1 = y1_s[at, :]
            scale = lax.rsqrt(jnp.mean(y1 * y1, axis=-1, keepdims=True) + EPSILON)
            n2 = y1 * scale
            out_ref[at, :] = (y1 + acc_s[at, :]).astype(BF)
            dxn = dxn_s[at, :]
            dn = dxn * gain
            dy1 = dy_ref[at, :].astype(F32) + scale * (dn - n2 * jnp.mean(dn * n2, axis=-1, keepdims=True))
            dy1_ref[at, :] = dy1
            dmix_ref[at, :] = dy1.astype(BF)
            return total + jnp.sum(dxn * n2, axis=0, keepdims=True)

        total = lax.fori_loop(0, tokens // 128, rows, jnp.zeros((1, width), F32))
        small_ref[...] = collect(total, 0, width // SLOTS)
        chans = hb_ref.shape[1]
        for b in range(chans // width):
            upg_s[...] = dot(hb_ref[:, b * width : (b + 1) * width], dmix_ref[...], ((0,), (0,)))
            per_b = width // 32
            for r in range(per_b):
                s = slot_ref[b * per_b + r]
                piece = upg_s[r * 32 : (r + 1) * 32, :].astype(BF)

                @pl.when(s < SLOTS // 2)
                def _():
                    keep_ref[s, shard : shard + 32, :] = piece

                @pl.when(s >= SLOTS // 2)
                def _():
                    send_ref[s - SLOTS // 2, shard : shard + 32, :] = piece


def mixer_backward(dev_ref, dmix_ref, xn_ref, small_ref, wo_ref, f_ref, u1_ref, u2_ref,
                   df_ref, di_ref, dc_ref, keep_ref, send_ref, xnt_s, dh_s, bias_s):
    step = pl.program_id(0)
    tokens, width = xn_ref.shape
    nblk = (keep_ref.shape[1] - 16) // 48
    tail = 48 * nblk
    half = SLOTS // 2

    @pl.when(step == 0)
    def _():
        xnt_s[...] = xn_ref[...].T

    dh_s[...] = dot(dmix_ref[...], wo_ref[...], ((1,), (1,)))
    zeros = jnp.zeros((CHUNKS, LANES), F32)
    tile = 4 * CHUNKS
    count = tokens // tile

    def first(i, carry):
        g, prod, decay = carry
        at = aligned((count - 1 - i) * tile, tile)
        dh = dh_s[at, :]
        forget = f_ref[at, :]
        for k in reversed(range(4)):
            part = slice(k * CHUNKS, (k + 1) * CHUNKS)
            g = dh[part] + decay * g
            prod = prod * decay
            decay = forget[part]
        return g, prod, decay

    ones = zeros + 1.0
    head, prod, decay = lax.fori_loop(0, count, first, (zeros, ones, ones))
    sub = lax.broadcasted_iota(jnp.int32, (CHUNKS, LANES), 0)
    start = zeros
    for s in reversed(range(1, CHUNKS)):
        moved = pltpu.roll(decay * (head + prod * start), CHUNKS - 1, 0)
        start = jnp.where(sub == s - 1, moved, start)

    def second(i, carry):
        g, decay, total = carry
        at = aligned((count - 1 - i) * tile, tile)
        dh = dh_s[at, :]
        forget = f_ref[at, :]
        parts = [None] * 4
        for k in reversed(range(4)):
            part = slice(k * CHUNKS, (k + 1) * CHUNKS)
            g = dh[part] + decay * g
            decay = forget[part]
            parts[k] = g
        grad = jnp.concatenate(parts, axis=0)
        df_ref[at, :] = (u1_ref[at, :].astype(F32) * grad).astype(BF)
        di = (u2_ref[at, :].astype(F32) * grad).astype(BF)
        di_ref[at, :] = di
        dc_ref[at, :] = ((1.0 - forget) * grad).astype(BF)
        di = di.astype(F32)
        for k in range(4):
            total = total + di[k * CHUNKS : (k + 1) * CHUNKS]
        return g, decay, total

    _, _, total = lax.fori_loop(0, count, second, (start, ones, zeros))
    bias_s[step, 0:1, :] = jnp.sum(total, axis=0, keepdims=True)

    for w, ref in enumerate((df_ref, di_ref, dc_ref)):
        grad = dot(xnt_s[...], ref[...]).astype(BF)
        dh_s[0:width, :] = grad.astype(F32)
        dst = aligned((w * nblk + step) * 16, 16)
        for s in range(SLOTS):
            d = dev_ref[s]
            target = keep_ref if s < half else send_ref
            target[s % half, dst, :] = dh_s[aligned(d * 16, 16), :].astype(BF)

    @pl.when(step == pl.num_programs(0) - 1)
    def _():
        bias = jnp.concatenate([bias_s[b, 0:1, :] for b in range(nblk)], axis=1)
        piece = width // SLOTS
        dh_s[0:SLOTS, :] = small_ref[...] + collect(bias, 2 * piece, nblk * LANES // SLOTS)
        row = lax.broadcasted_iota(jnp.int32, (16, LANES), 0)
        for s in range(SLOTS):
            target = keep_ref if s < half else send_ref
            values = dh_s[pl.ds(dev_ref[s], 1), :]
            target[s % half, tail : tail + 16, :] = jnp.where(row == 0, values, 0.0).astype(BF)


def input_gradient(x_ref, dy1_ref, gain_ref, df_ref, di_ref, dc_ref, w_ref, out_ref):
    dxn = dot(df_ref[...], w_ref[0], ((1,), (1,)))
    dxn = dxn + dot(di_ref[...], w_ref[1], ((1,), (1,)))
    dxn = dxn + dot(dc_ref[...], w_ref[2], ((1,), (1,)))
    v = x_ref[...].astype(F32)
    scale = lax.rsqrt(jnp.mean(v * v, axis=-1, keepdims=True) + EPSILON)
    n1 = v * scale
    dn = dxn * gain_ref[0:1, :]
    out_ref[...] = dy1_ref[...] + scale * (dn - n1 * jnp.mean(dn * n1, axis=-1, keepdims=True))


def order_table():
    table = np.zeros((SLOTS, SLOTS), np.int32)
    for me in range(SLOTS):
        core, y, x, z = me & 1, me >> 1 & 1, me >> 2 & 1, me >> 3
        for slot in range(SLOTS):
            oc, second, first, oz = slot >> 4, slot >> 3 & 1, slot >> 2 & 1, slot & 3
            c2 = core ^ oc
            x2 = x ^ (first if c2 == 0 else second)
            y2 = y ^ (second if c2 == 0 else first)
            table[me, slot] = ((z ^ oz) * 2 + x2) * 4 + y2 * 2 + c2
    return table


def flip(x0, y0, z0, c0, x1, y1, z1, c1):
    pairs = []
    for me in range(SLOTS):
        x, y, z, c = (x1, y1, z1, c1) if me & 1 else (x0, y0, z0, c0)
        pairs.append((me, me ^ (z << 3 | x << 2 | y << 1 | c)))
    return pairs


Z = [None] + [flip(0, 0, k, 0, 0, 0, k, 0) for k in (1, 2, 3)]
FIRST = flip(1, 0, 0, 0, 0, 1, 0, 0)
SECOND = flip(0, 1, 0, 0, 1, 0, 0, 0)
CORE = flip(0, 0, 0, 1, 0, 0, 0, 1)


def send(value, pairs):
    return lax.ppermute(value, AXES, pairs)


def gather(piece):
    four = jnp.stack([piece] + [send(piece, Z[k]) for k in (1, 2, 3)])
    eight = jnp.concatenate([four, send(four, FIRST)])
    more = send(eight, SECOND)
    return eight, more, send(eight, CORE), send(more, CORE)


def add(a, b):
    return (a.astype(F32) + b.astype(F32)).astype(BF)


def reduce_scatter(keep, away):
    got = send(away, CORE)
    high = add(keep[8:], got[8:])
    low = add(keep[:8], got[:8])
    got = send(high, SECOND)
    high = add(low[4:], got[4:])
    low = add(low[:4], got[:4])
    got = send(high, FIRST)
    four = add(low, got)
    parts = [send(four[k], Z[k]) for k in (1, 2, 3)]
    total = four[0].astype(F32)
    for part in parts:
        total = total + part.astype(F32)
    return total


def pack_mixer(forget_weight, input_weight, candidate_weight, small):
    def cut(w):
        blocks = w.shape[1] // LANES
        return w.reshape(16, blocks, LANES).transpose(1, 0, 2).reshape(blocks * 16, LANES)

    row = jnp.concatenate([small, jnp.zeros((LANES - small.shape[0],), small.dtype)])
    tail = jnp.concatenate([row[None], jnp.zeros((15, LANES), small.dtype)])
    return jnp.concatenate([cut(forget_weight), cut(input_weight), cut(candidate_weight), tail])


def local(fast, tokens, gain_mix, gain_mlp, forget_weight, input_weight, candidate_weight, input_gate_bias,
          output_weight, up_weight, down_weight, cotangent):
    rows, width = tokens.shape
    chans = forget_weight.shape[1]
    nblk = chans // LANES
    shard = width // SLOTS

    def permute(v):
        return v.reshape(CHUNKS, rows // CHUNKS, width).transpose(1, 0, 2).reshape(rows, width)

    def restore(v):
        return v.reshape(rows // CHUNKS, CHUNKS, width).transpose(1, 0, 2).reshape(rows, width)

    if fast:
        me = lax.axis_index(AXES)
        table = order_table()
        dev = lax.dynamic_index_in_dim(jnp.asarray(table), me, keepdims=False)
        slot = lax.dynamic_index_in_dim(jnp.asarray(np.argsort(table, axis=1).astype(np.int32)), me, keepdims=False)
        mine, core = me // 2 % 2, me % 2
        cols = jnp.stack([1 - core, 3 - core, core, 2 + core]).astype(jnp.int32)
        small = jnp.concatenate([gain_mix, gain_mlp, input_gate_bias])
        mixer = gather(pack_mixer(forget_weight, input_weight, candidate_weight, small))
        ffn = gather(jnp.concatenate([up_weight, down_weight.T, output_weight]))
    else:
        dev = slot = jnp.arange(SLOTS, dtype=jnp.int32)
        cols = jnp.arange(4, dtype=jnp.int32)

        def full(v, axis=0, names=AXES):
            return lax.all_gather(v, names, axis=axis, tiled=True)

        gm, gl, gb = full(gain_mix), full(gain_mlp), full(input_gate_bias)
        weights = [full(w) for w in (forget_weight, input_weight, candidate_weight)]
        smalls = jnp.concatenate([v.reshape(SLOTS, -1) for v in (gm, gl, gb)], axis=1)
        packed = jnp.stack(
            [pack_mixer(*[w[s * 16 : (s + 1) * 16] for w in weights], smalls[s]) for s in range(SLOTS)]
        )
        up = full(full(up_weight, 0, "dp"), 1, "mp")
        down = full(full(down_weight, 1, "dp"), 0, "mp")
        hid = up.shape[1] // 4

        def blocks(w):
            return w.reshape(8, width // 8, 4, hid).transpose(0, 2, 1, 3).reshape(SLOTS, width // 8, hid)

        both = jnp.concatenate([blocks(up), blocks(down.T), full(output_weight).reshape(SLOTS, -1, width)], axis=1)
        mixer = tuple(packed[k * 8 : (k + 1) * 8] for k in range(4))
        ffn = tuple(both[k * 8 : (k + 1) * 8] for k in range(4))

    xp = permute(tokens)
    dyp = permute(cotangent)
    r1 = mixer[0].shape[1]
    r2 = ffn[0].shape[1]
    hid = ffn[0].shape[2]
    smem = pl.BlockSpec(memory_space=pltpu.SMEM)
    anyspace = pl.BlockSpec(memory_space=pl.ANY)
    column = pl.BlockSpec((rows, LANES), lambda i: (0, i))

    hb, forget, u1, u2, w3, xn1, gains = pl.pallas_call(
        mixer_forward,
        grid=(nblk,),
        in_specs=[smem, whole((rows, width))] + [whole((8, r1, LANES))] * 4,
        out_specs=[column] * 4 + [pl.BlockSpec((3, width, LANES), lambda i: (0, 0, i)), whole((rows, width)), whole((2, width))],
        out_shape=[
            jax.ShapeDtypeStruct((rows, chans), BF),
            jax.ShapeDtypeStruct((rows, chans), F32),
            jax.ShapeDtypeStruct((rows, chans), BF),
            jax.ShapeDtypeStruct((rows, chans), BF),
            jax.ShapeDtypeStruct((3, width, chans), BF),
            jax.ShapeDtypeStruct((rows, width), BF),
            jax.ShapeDtypeStruct((2, width), F32),
        ],
        scratch_shapes=[pltpu.VMEM((SLOTS, LANES), F32)] + [pltpu.VMEM((rows, LANES), F32)] * 4 + [pltpu.VMEM((nblk, 8, LANES), F32)],
        compiler_params=params(),
        cost_estimate=pl.CostEstimate(flops=6 * rows * width * chans, bytes_accessed=16 << 20, transcendentals=6 * rows * chans),
        name="mixer_forward",
    )(dev, xp, *mixer)

    block_out, dy1, dmix, wo, gmlp_small, keep1, send1 = pl.pallas_call(
        feed_forward,
        grid=(4,),
        in_specs=[smem, smem, smem, whole((rows, chans)), whole((rows, width)), whole((rows, width)), whole((2, width))] + [anyspace] * 4,
        out_specs=[whole((rows, width))] * 3
        + [whole((chans, width)), whole((SLOTS, LANES)), whole((SLOTS // 2, r2, hid)), whole((SLOTS // 2, r2, hid))],
        out_shape=[
            jax.ShapeDtypeStruct((rows, width), BF),
            jax.ShapeDtypeStruct((rows, width), F32),
            jax.ShapeDtypeStruct((rows, width), BF),
            jax.ShapeDtypeStruct((chans, width), BF),
            jax.ShapeDtypeStruct((SLOTS, LANES), F32),
            jax.ShapeDtypeStruct((SLOTS // 2, r2, hid), BF),
            jax.ShapeDtypeStruct((SLOTS // 2, r2, hid), BF),
        ],
        scratch_shapes=[
            pltpu.VMEM((SLOTS, r2, hid), BF),
            pltpu.SemaphoreType.DMA((4,)),
            pltpu.VMEM((rows, width), F32),
            pltpu.VMEM((rows, width), BF),
            pltpu.VMEM((width, rows), BF),
            pltpu.VMEM((width, rows), BF),
            pltpu.VMEM((rows, width), F32),
            pltpu.VMEM((rows, width), F32),
            pltpu.VMEM((width, hid), BF),
            pltpu.VMEM((width, hid), BF),
            pltpu.VMEM((width, hid), F32),
            pltpu.VMEM((width, hid), F32),
        ],
        compiler_params=params(),
        cost_estimate=pl.CostEstimate(flops=2 * rows * width * (24 * hid + 2 * chans), bytes_accessed=24 << 20, transcendentals=4 * rows * hid),
        name="feed_forward",
    )(dev, slot, cols, hb, xp, dyp, gains, *ffn)

    df, di, dc, keep2, send2 = pl.pallas_call(
        mixer_backward,
        grid=(nblk,),
        in_specs=[smem, whole((rows, width)), whole((rows, width)), whole((SLOTS, LANES)),
                  pl.BlockSpec((LANES, width), lambda i: (i, 0)), column, column, column],
        out_specs=[column] * 3 + [whole((SLOTS // 2, r1, LANES))] * 2,
        out_shape=[jax.ShapeDtypeStruct((rows, chans), BF)] * 3 + [jax.ShapeDtypeStruct((SLOTS // 2, r1, LANES), BF)] * 2,
        scratch_shapes=[pltpu.VMEM((width, rows), BF), pltpu.VMEM((rows, LANES), F32), pltpu.VMEM((nblk, 8, LANES), F32)],
        compiler_params=params(),
        cost_estimate=pl.CostEstimate(flops=8 * rows * width * chans, bytes_accessed=24 << 20, transcendentals=0),
        name="mixer_backward",
    )(dev, dmix, xn1, gmlp_small, wo, forget, u1, u2)

    tile = 256
    tokens_grad = pl.pallas_call(
        input_gradient,
        grid=(rows // tile,),
        in_specs=[pl.BlockSpec((tile, width), lambda i: (i, 0))] * 2 + [whole((2, width))]
        + [pl.BlockSpec((tile, chans), lambda i: (i, 0))] * 3 + [whole((3, width, chans))],
        out_specs=pl.BlockSpec((tile, width), lambda i: (i, 0)),
        out_shape=jax.ShapeDtypeStruct((rows, width), F32),
        compiler_params=params(),
        cost_estimate=pl.CostEstimate(flops=6 * rows * width * chans, bytes_accessed=16 << 20, transcendentals=0),
        name="input_gradient",
    )(xp, dy1, gains, df, di, dc, w3)

    half = (r2 - 32) // 2

    def uncut(v):
        return v.reshape(nblk, 16, LANES).transpose(1, 0, 2).reshape(16, chans)

    if fast:
        ffn_total = reduce_scatter(keep1, send1)
        up_grad, down_grad, out_grad = ffn_total[:half], ffn_total[half : 2 * half].T, ffn_total[2 * half :]
        total = reduce_scatter(keep2, send2)
        step = nblk * 16
        grads = [uncut(total[k * step : (k + 1) * step]) for k in range(3)]
        last = total[3 * step]
        gmlp_grad = last[:shard]
        bias_grad = last[2 * shard : 2 * shard + chans // SLOTS]
    else:
        pieces = jnp.concatenate([keep1, send1])

        def summed(v, axis=0, names=AXES):
            return lax.psum_scatter(v, names, scatter_dimension=axis, tiled=True)

        def joined(w):
            return w.reshape(8, 4, half, hid).transpose(0, 2, 1, 3).reshape(8 * half, 4 * hid).astype(F32)

        up_grad = summed(summed(joined(pieces[:, :half]), 0, "dp"), 1, "mp")
        down_grad = summed(summed(joined(pieces[:, half : 2 * half]).T, 1, "dp"), 0, "mp")
        out_grad = summed(pieces[:, 2 * half :].reshape(chans, width).astype(F32))
        pieces = jnp.concatenate([keep2, send2]).astype(F32)
        step = nblk * 16
        grads = []
        for k in range(3):
            w = pieces[:, k * step : (k + 1) * step].reshape(SLOTS, nblk, 16, LANES).transpose(0, 2, 1, 3)
            grads.append(summed(w.reshape(width, chans)))
        last = pieces[:, 3 * step]
        gmlp_grad = summed(last[:, :shard].reshape(-1))
        bias_grad = summed(last[:, 2 * shard : 2 * shard + chans // SLOTS].reshape(-1))

    dots = sum(
        jnp.sum(w.astype(F32) * g, axis=1) for w, g in zip((forget_weight, input_weight, candidate_weight), grads)
    )
    gmix_grad = dots / gain_mix.astype(F32)
    return (restore(block_out), restore(tokens_grad), gmix_grad, gmlp_grad, grads[0], grads[1], grads[2], bias_grad,
            out_grad, up_grad, down_grad)


def solution(mesh):
    fast = mesh.shape["dp"] == 8 and mesh.shape["mp"] == 4
    every = P(AXES, None)
    in_specs = (every, P(AXES), P(AXES), every, every, every, P(AXES), every, P("dp", "mp"), P("mp", "dp"), every)
    out_specs = (every, every, P(AXES), P(AXES), every, every, every, P(AXES), every, P("dp", "mp"), P("mp", "dp"))
    return jax.shard_map(
        functools.partial(local, fast), mesh=mesh, in_specs=in_specs, out_specs=out_specs, check_vma=False
    )
```

```python
import functools

import jax
import jax.numpy as jnp
import numpy as np
from jax import lax
from jax.experimental import pallas as pl
from jax.experimental.pallas import tpu as pltpu
from jax.sharding import PartitionSpec as P

LEN = 1024
EPSILON = 1e-06
AXES = ("dp", "mp")
SLOTS = 32
CHUNKS = 8
LANES = 256
GROUP = 8
BF = jnp.bfloat16
F32 = jnp.float32
VMEM_LIMIT = 60 * 1024 * 1024
C0 = 0.7978845608028654
C1 = C0 * 0.044715


def params():
    return pltpu.CompilerParams(vmem_limit_bytes=VMEM_LIMIT)


def dot(a, b, dims=((1,), (0,))):
    return lax.dot_general(a, b, (dims, ((), ())), preferred_element_type=F32)


def whole(shape):
    return pl.BlockSpec(shape, lambda *_: (0,) * len(shape), pipeline_mode=pl.Buffered(1))


def aligned(start, size):
    return pl.ds(pl.multiple_of(start, size), size)


def spread(small, offset, piece, width):
    lane = lax.broadcasted_iota(jnp.int32, (LANES, width), 0)
    column = lax.broadcasted_iota(jnp.int32, (LANES, width), 1)
    pick = (lane == offset + column % piece).astype(BF)
    placed = dot(small.astype(BF), pick)
    row = lax.broadcasted_iota(jnp.int32, (SLOTS, width), 0)
    col = lax.broadcasted_iota(jnp.int32, (SLOTS, width), 1)
    return jnp.sum(jnp.where(col // piece == row, placed, 0.0), axis=0, keepdims=True)


def collect(vector, offset, piece):
    width = vector.shape[1]
    row = lax.broadcasted_iota(jnp.int32, (SLOTS, width), 0)
    col = lax.broadcasted_iota(jnp.int32, (SLOTS, width), 1)
    kept = jnp.where(col // piece == row, vector, 0.0).astype(BF)
    column = lax.broadcasted_iota(jnp.int32, (width, LANES), 0)
    lane = lax.broadcasted_iota(jnp.int32, (width, LANES), 1)
    pick = (lane == offset + column % piece).astype(BF)
    return dot(kept, pick)


def pack_mixer(forget_ref, input_ref, cand_ref, small_ref, out_ref):
    blocks = forget_ref.shape[1] // LANES
    for b in range(blocks):
        for w, ref in enumerate((forget_ref, input_ref, cand_ref)):
            at = (b * 3 + w) * 16
            out_ref[at : at + 16, :] = ref[:, b * LANES : (b + 1) * LANES]
    row = lax.broadcasted_iota(jnp.int32, (16, LANES), 0)
    out_ref[48 * blocks :, :] = jnp.where(row == 0, small_ref[...].astype(F32), 0.0).astype(BF)


def mixer_prepare(dev_ref, parts, x_ref, xn_ref, xnt_ref, gain_ref, bias_s, small):
    per = SLOTS // 4
    tail = parts[0].shape[1] - 16
    for s in range(SLOTS):
        row = parts[s // per][s % per, tail : tail + 16, :].astype(F32)
        small[pl.ds(dev_ref[s], 1), :] = row[0:1, :]
    values = small[...]
    width, chans = x_ref.shape[1], bias_s.shape[1]
    piece = width // SLOTS
    gmix = spread(values, 0, piece, width)
    gain_ref[0:1, :] = gmix
    gain_ref[1:2, :] = spread(values, piece, piece, width)
    bias_s[...] = spread(values, 2 * piece, chans // SLOTS, chans)

    def rows(i, _):
        at = aligned(i * 256, 256)
        v = x_ref[at, :].astype(F32)
        scale = lax.rsqrt(jnp.mean(v * v, axis=-1, keepdims=True) + EPSILON)
        xn = ((v * scale) * gmix).astype(BF)
        xn_ref[at, :] = xn
        xnt_ref[:, at] = xn.T
        return 0

    lax.fori_loop(0, x_ref.shape[0] // 256, rows, 0)


def mixer_forward(dev_ref, x_ref, g0, g1, g2, g3, hb_ref, f_ref, u1_ref, u2_ref, w_ref, xnt_ref, gain_ref,
                  small, bias_s, xn_s, k_s, c2_s):
    step = pl.program_id(0)
    per = SLOTS // 4
    parts = (g0, g1, g2, g3)

    @pl.when(step == 0)
    def _():
        mixer_prepare(dev_ref, parts, x_ref, xn_s, xnt_ref, gain_ref, bias_s, small)

    for s in range(SLOTS):
        d = dev_ref[s]
        for w in range(3):
            src = aligned((step * 3 + w) * 16, 16)
            w_ref[aligned(d * 16, 16), w * LANES : (w + 1) * LANES] = parts[s // per][s % per, src, :]

    bias = bias_s[:, aligned(step * LANES, LANES)]
    k_s[...] = dot(xn_s[...], w_ref[...])
    kf_c, ki_c, kc_c = (slice(w * LANES, (w + 1) * LANES) for w in range(3))
    zeros = jnp.zeros((CHUNKS, LANES), F32)
    tile = GROUP * CHUNKS
    count = xn_s.shape[0] // tile

    def first(i, carry):
        h, prod = carry
        at = aligned(i * tile, tile)
        kf = k_s[at, kf_c]
        ki = k_s[at, ki_c] + bias
        kc = k_s[at, kc_c]
        p = jnp.exp(-jnp.abs(kf))
        q = jnp.exp(-jnp.abs(ki))
        w = jnp.minimum(ki, 0.0) - jnp.minimum(kf, 0.0)
        e = jnp.exp(-jnp.abs(w))
        low = w <= 0.0
        a_part = jnp.where(low, 1.0, e)
        b_part = jnp.where(low, e, 1.0)
        a = a_part * (1.0 + q)
        b = b_part * (1.0 + p)
        inv = 1.0 / (a + b)
        forget = a * inv
        other = b * inv
        f_ref[at, :] = forget
        drive = other * kc
        k_s[at, kf_c] = forget * (inv * (b_part * jnp.where(kf >= 0.0, p, 1.0)))
        k_s[at, ki_c] = -other * (inv * (a_part * jnp.where(ki >= 0.0, q, 1.0)))
        c2_s[at, :] = drive
        for k in range(GROUP):
            part = slice(k * CHUNKS, (k + 1) * CHUNKS)
            h = forget[part] * h + drive[part]
            prod = prod * forget[part]
        return h, prod

    last, prod = lax.fori_loop(0, count, first, (zeros, zeros + 1.0))
    sub = lax.broadcasted_iota(jnp.int32, (CHUNKS, LANES), 0)
    start = zeros
    for s in range(CHUNKS - 1):
        moved = pltpu.roll(last + prod * start, 1, 0)
        start = jnp.where(sub == s + 1, moved, start)

    def second(i, h):
        at = aligned(i * tile, tile)
        forget = f_ref[at, :]
        drive = c2_s[at, :]
        before, after = [], []
        for k in range(GROUP):
            part = slice(k * CHUNKS, (k + 1) * CHUNKS)
            before.append(h)
            h = forget[part] * h + drive[part]
            after.append(h)
        diff = jnp.concatenate(before, axis=0) - k_s[at, kc_c]
        hb_ref[at, :] = jnp.concatenate(after, axis=0).astype(BF)
        u1_ref[at, :] = (k_s[at, kf_c] * diff).astype(BF)
        u2_ref[at, :] = (k_s[at, ki_c] * diff).astype(BF)
        return h

    lax.fori_loop(0, count, second, start)


def feed_forward(dev_ref, slot_ref, cols_ref, gain_ref, g0, g1, g2, g3, hb_hbm, x_hbm, dy_hbm,
                 out_hbm, dy1_hbm, dmix_hbm, wo_hbm, keep_hbm, send_hbm, small_ref,
                 outs_in, feed_in, hb_s, x_s, dy_s, wo_s, y1_s, xn_s, xnt_s, dyt_s, acc_s, dxn_s, up_s, dn_s,
                 pieces, out_s, dy1_s, dmix_s, sems):
    parts = (g0, g1, g2, g3)
    per = SLOTS // 4
    half = SLOTS // 2
    tokens, width = x_s.shape
    chans = hb_s.shape[1]
    rows = up_s.shape[0] // 8
    feed = 2 * rows
    used = []

    def copy(src, dst):
        used.append(pltpu.make_async_copy(src, dst, sems.at[len(used)]))
        used[-1].start()
        return used[-1]

    wait_out = [copy(parts[k].at[:, feed:, :], outs_in.at[pl.ds(k * per, per)]) for k in range(4)]
    wait_mix = [copy(hb_hbm, hb_s), copy(x_hbm, x_s)]
    wait_feed = [copy(parts[k].at[:, :feed, :], feed_in.at[pl.ds(k * per, per)]) for k in range(2)]
    wait_dy = copy(dy_hbm, dy_s)
    wait_more = [copy(parts[k].at[:, :feed, :], feed_in.at[pl.ds(k * per, per)]) for k in range(2, 4)]

    for c in wait_out:
        c.wait()
    for s in range(SLOTS):
        wo_s[aligned(dev_ref[s] * 32, 32), :] = outs_in[s]
    finish = [copy(wo_s, wo_hbm)]
    for c in wait_mix:
        c.wait()
    gain = gain_ref[1:2, :]

    def rows_in(i, _):
        at = aligned(i * 256, 256)
        y1 = x_s[at, :].astype(F32) + dot(hb_s[at, :], wo_s[...])
        y1_s[at, :] = y1
        scale = lax.rsqrt(jnp.mean(y1 * y1, axis=-1, keepdims=True) + EPSILON)
        xn = ((y1 * scale) * gain).astype(BF)
        xn_s[at, :] = xn
        xnt_s[:, at] = xn.T
        return 0

    lax.fori_loop(0, tokens // 256, rows_in, 0)
    wait_dy.wait()
    dyt_s[...] = dy_s[...].T

    for group in range(4):
        for c in {0: wait_feed, 2: wait_more}.get(group, ()):
            c.wait()
        block = cols_ref[group]
        for r in range(8):
            s = slot_ref[r * 4 + block]
            up_s[r * rows : (r + 1) * rows, :] = feed_in[s, 0:rows, :]
            dn_s[r * rows : (r + 1) * rows, :] = feed_in[s, rows:feed, :]
        pre = dot(xn_s[...], up_s[...])
        dact = dot(dy_s[...], dn_s[...])
        sq = pre * pre
        gate = 0.5 + 0.5 * jnp.tanh(pre * (C0 + C1 * sq))
        value = pre * gate
        act = value.astype(BF)
        slope = gate + value * (1.0 - gate) * (2.0 * C0 + 6.0 * C1 * sq)
        dpre = (slope * dact).astype(BF)
        upg = dot(xnt_s[...], dpre).astype(BF)
        dng = dot(dyt_s[...], act).astype(BF)
        for r in range(8):
            s = slot_ref[r * 4 + block]
            pieces[s, 0:rows, :] = upg[r * rows : (r + 1) * rows]
            pieces[s, rows:feed, :] = dng[r * rows : (r + 1) * rows]
        if group == 1:
            finish.append(copy(pieces.at[:half, :feed, :], keep_hbm.at[:, :feed, :]))
        if group == 3:
            finish.append(copy(pieces.at[half:, :feed, :], send_hbm.at[:, :feed, :]))
        out = dot(act, dn_s[...], ((1,), (1,)))
        dxn = dot(dpre, up_s[...], ((1,), (1,)))
        if group == 0:
            acc_s[...] = out
            dxn_s[...] = dxn
        else:
            acc_s[...] += out
            dxn_s[...] += dxn

    total = jnp.zeros((1, width), F32)
    for i in range(tokens // 256):
        at = slice(i * 256, (i + 1) * 256)
        y1 = y1_s[at, :]
        scale = lax.rsqrt(jnp.mean(y1 * y1, axis=-1, keepdims=True) + EPSILON)
        n2 = y1 * scale
        out_s[at, :] = (y1 + acc_s[at, :]).astype(BF)
        dxn = dxn_s[at, :]
        dn = dxn * gain
        dy1 = dy_s[at, :].astype(F32) + scale * (dn - n2 * jnp.mean(dn * n2, axis=-1, keepdims=True))
        dy1_s[at, :] = dy1
        dmix_s[at, :] = dy1.astype(BF)
        total = total + jnp.sum(dxn * n2, axis=0, keepdims=True)
    finish += [copy(out_s, out_hbm), copy(dy1_s, dy1_hbm), copy(dmix_s, dmix_hbm)]
    small_ref[...] = collect(total, 0, width // SLOTS)

    span = 256
    for b in range(chans // span):
        grad = dot(hb_s[:, b * span : (b + 1) * span], dmix_s[...], ((0,), (0,))).astype(BF)
        for r in range(span // 32):
            pieces[slot_ref[b * (span // 32) + r], feed:, :] = grad[r * 32 : (r + 1) * 32]
    finish.append(copy(pieces.at[:half, feed:, :], keep_hbm.at[:, feed:, :]))
    finish.append(copy(pieces.at[half:, feed:, :], send_hbm.at[:, feed:, :]))
    for c in finish:
        c.wait()


def mixer_backward(dev_ref, dmix_ref, xnt_ref, wo_ref, small_ref, f_ref, u1_ref, u2_ref,
                   dk_ref, keep_ref, send_ref, bias_s, dh_s, grad_s):
    step = pl.program_id(0)
    blocks = pl.num_programs(0)
    width, tokens = xnt_ref.shape
    half = SLOTS // 2

    @pl.when(step == 0)
    def _():
        for b in range(dh_s.shape[0]):
            dh_s[b] = dot(dmix_ref[...], wo_ref[b * LANES : (b + 1) * LANES, :], ((1,), (1,)))

    zeros = jnp.zeros((CHUNKS, LANES), F32)
    tile = GROUP * CHUNKS
    count = tokens // tile

    def first(i, carry):
        g, prod, decay = carry
        at = aligned((count - 1 - i) * tile, tile)
        dh = dh_s[step, at, :]
        forget = f_ref[at, :]
        for k in reversed(range(GROUP)):
            part = slice(k * CHUNKS, (k + 1) * CHUNKS)
            g = dh[part] + decay * g
            prod = prod * decay
            decay = forget[part]
        return g, prod, decay

    ones = zeros + 1.0
    head, prod, decay = lax.fori_loop(0, count, first, (zeros, ones, ones))
    sub = lax.broadcasted_iota(jnp.int32, (CHUNKS, LANES), 0)
    start = zeros
    for s in reversed(range(1, CHUNKS)):
        moved = pltpu.roll(decay * (head + prod * start), CHUNKS - 1, 0)
        start = jnp.where(sub == s - 1, moved, start)

    def second(i, carry):
        g, decay, total = carry
        at = aligned((count - 1 - i) * tile, tile)
        dh = dh_s[step, at, :]
        forget = f_ref[at, :]
        parts = [None] * GROUP
        for k in reversed(range(GROUP)):
            part = slice(k * CHUNKS, (k + 1) * CHUNKS)
            g = dh[part] + decay * g
            decay = forget[part]
            parts[k] = g
        grad = jnp.concatenate(parts, axis=0)
        dk_ref[at, 0:LANES] = (u1_ref[at, :].astype(F32) * grad).astype(BF)
        di = (u2_ref[at, :].astype(F32) * grad).astype(BF)
        dk_ref[at, LANES : 2 * LANES] = di
        dk_ref[at, 2 * LANES : 3 * LANES] = ((1.0 - forget) * grad).astype(BF)
        di = di.astype(F32)
        for k in range(GROUP):
            total = total + di[k * CHUNKS : (k + 1) * CHUNKS]
        return g, decay, total

    _, _, total = lax.fori_loop(0, count, second, (start, ones, zeros))
    bias_s[:, aligned(step * LANES, LANES)] = jnp.sum(total, axis=0, keepdims=True)

    grad_s[...] = dot(xnt_ref[...], dk_ref[...]).astype(BF)
    for s in range(SLOTS):
        target = keep_ref if s < half else send_ref
        src = aligned(dev_ref[s] * 16, 16)
        for w in range(3):
            dst = aligned((step * 3 + w) * 16, 16)
            target[s % half, dst, :] = grad_s[src, w * LANES : (w + 1) * LANES]

    @pl.when(step == blocks - 1)
    def _():
        bias = bias_s[...]
        piece = width // SLOTS
        values = small_ref[...] + collect(bias, 2 * piece, bias.shape[1] // SLOTS)
        dh_s[0, 0:SLOTS, :] = values
        row = lax.broadcasted_iota(jnp.int32, (16, LANES), 0)
        tail = keep_ref.shape[1] - 16
        for s in range(SLOTS):
            target = keep_ref if s < half else send_ref
            values = dh_s[0, pl.ds(dev_ref[s], 1), :]
            target[s % half, tail : tail + 16, :] = jnp.where(row == 0, values, 0.0).astype(BF)


def input_gradient(x_ref, dy1_ref, gain_ref, dk_ref, w_ref, out_ref):
    dxn = dot(dk_ref[...], w_ref[...], ((1,), (1,)))
    v = x_ref[...].astype(F32)
    scale = lax.rsqrt(jnp.mean(v * v, axis=-1, keepdims=True) + EPSILON)
    n1 = v * scale
    dn = dxn * gain_ref[0:1, :]
    out_ref[...] = dy1_ref[...] + scale * (dn - n1 * jnp.mean(dn * n1, axis=-1, keepdims=True))


def order_table():
    table = np.zeros((SLOTS, SLOTS), np.int32)
    for me in range(SLOTS):
        core, y, x, z = me & 1, me >> 1 & 1, me >> 2 & 1, me >> 3
        for slot in range(SLOTS):
            oc, second, first, oz = slot >> 4, slot >> 3 & 1, slot >> 2 & 1, (slot & 1) << 1 | slot >> 1 & 1
            c2 = core ^ oc
            x2 = x ^ (first if c2 == 0 else second)
            y2 = y ^ (second if c2 == 0 else first)
            table[me, slot] = ((z ^ oz) * 2 + x2) * 4 + y2 * 2 + c2
    return table


def flip(x0, y0, z0, c0, x1, y1, z1, c1):
    pairs = []
    for me in range(SLOTS):
        x, y, z, c = (x1, y1, z1, c1) if me & 1 else (x0, y0, z0, c0)
        pairs.append((me, me ^ (z << 3 | x << 2 | y << 1 | c)))
    return pairs


FAR, NEAR, BOTH = [flip(0, 0, k, 0, 0, 0, k, 0) for k in (2, 1, 3)]
FIRST = flip(1, 0, 0, 0, 0, 1, 0, 0)
SECOND = flip(0, 1, 0, 0, 1, 0, 0, 0)
CORE = flip(0, 0, 0, 1, 0, 0, 0, 1)


def send(value, pairs, name):
    with jax.named_scope(name):
        return lax.ppermute(value, AXES, pairs)


def after(value, *others):
    return lax.optimization_barrier((value,) + others)[0]


def after_all(*values):
    return lax.optimization_barrier(values)


def add(a, b):
    return (a.astype(F32) + b.astype(F32)).astype(BF)


def fold(low, high, pairs, name):
    got = send(high, pairs, name)
    half = low.shape[0] // 2
    return add(low[:half], got[:half]), add(low[half:], got[half:])


def pack(forget_weight, input_weight, candidate_weight, small):
    rows = 3 * forget_weight.shape[1] // LANES * 16 + 16
    return pl.pallas_call(
        pack_mixer,
        out_shape=jax.ShapeDtypeStruct((rows, LANES), BF),
        compiler_params=params(),
        name="pack",
    )(forget_weight, input_weight, candidate_weight, small)


def widen(small):
    return jnp.concatenate([small, jnp.zeros((LANES - small.shape[0],), small.dtype)])[None]


def local(fast, tokens, gain_mix, gain_mlp, forget_weight, input_weight, candidate_weight, input_gate_bias,
          output_weight, up_weight, down_weight, cotangent):
    rows, width = tokens.shape
    chans = forget_weight.shape[1]
    blocks = chans // LANES
    shard = width // SLOTS

    def permute(v):
        return v.reshape(CHUNKS, rows // CHUNKS, width).transpose(1, 0, 2).reshape(rows, width)

    def restore(v):
        return v.reshape(rows // CHUNKS, CHUNKS, width).transpose(1, 0, 2).reshape(rows, width)

    xp = permute(tokens)
    dyp = permute(cotangent)
    if fast:
        me = lax.axis_index(AXES)
        table = order_table()
        tables = jnp.asarray(np.stack([table, np.argsort(table, axis=1)], axis=1).astype(np.int32))
        dev, slot = lax.dynamic_index_in_dim(tables, me, keepdims=False)
        mine = me % 2
        cols = jnp.stack([mine, 2 + mine, 1 - mine, 3 - mine]).astype(jnp.int32)
        small = widen(jnp.concatenate([gain_mix, gain_mlp, input_gate_bias]))
        piece = pack(forget_weight, input_weight, candidate_weight, small)
        four = jnp.stack([piece] + [send(piece, p, "mixer_z") for p in (FAR, NEAR, BOTH)])
        four, piece_f = after_all(four, jnp.concatenate([up_weight, down_weight.T, output_weight]), dev, xp, dyp)[:2]
        got, far_f = after_all(send(four, FIRST, "mixer_first"), send(piece_f, FAR, "feed_far"))
        eight = jnp.concatenate([four, got])
        two_f = jnp.stack([piece_f, far_f])
        eight, two_f = after_all(eight, two_f)
        more, got = after_all(send(eight, SECOND, "mixer_second"), send(two_f, NEAR, "feed_near"))
        four_f = jnp.concatenate([two_f, got])
        more, four_f = after_all(more, four_f)
        got, core, core_more = after_all(
            send(four_f, FIRST, "feed_first"), send(eight, CORE, "mixer_core"), send(more, CORE, "mixer_core_more")
        )
        eight_f = jnp.concatenate([four_f, got])
        mixer = (eight, more, core, core_more)
        mixer, eight_f = lax.optimization_barrier((mixer, eight_f))
        more_f = send(eight_f, SECOND, "feed_second")
    else:
        dev = slot = jnp.arange(SLOTS, dtype=jnp.int32)
        cols = jnp.arange(4, dtype=jnp.int32)

        def full(v, axis=0, names=AXES):
            return lax.all_gather(v, names, axis=axis, tiled=True)

        gm, gl, gb = full(gain_mix), full(gain_mlp), full(input_gate_bias)
        weights = [full(w) for w in (forget_weight, input_weight, candidate_weight)]
        smalls = jnp.concatenate([v.reshape(SLOTS, -1) for v in (gm, gl, gb)], axis=1)
        up = full(full(up_weight, 0, "dp"), 1, "mp")
        down = full(full(down_weight, 1, "dp"), 0, "mp")

        def regroup(w):
            return w.reshape(8, width // 8, 4, width).transpose(0, 2, 1, 3).reshape(SLOTS, width // 8, width)

        both = jnp.concatenate([regroup(up), regroup(down.T), full(output_weight).reshape(SLOTS, -1, width)], axis=1)

        def quarters(v):
            return tuple(v[k * 8 : (k + 1) * 8] for k in range(4))

        mixer = quarters(
            jnp.stack([pack(*[w[s * 16 : (s + 1) * 16] for w in weights], widen(smalls[s])) for s in range(SLOTS)])
        )
        feed = quarters(both)

    smem = pl.BlockSpec(memory_space=pltpu.SMEM)
    part = 256

    def band(cols):
        return pl.BlockSpec((part, cols), lambda i: (i, 0))

    def shapes(*items):
        return [jax.ShapeDtypeStruct(shape, kind) for shape, kind in items]

    column = pl.BlockSpec((rows, LANES), lambda i: (0, i))

    wide = pl.BlockSpec((width, 3 * LANES), lambda i: (0, i))
    hb, forget, u1, u2, w3, xn1t, gains = pl.pallas_call(
        mixer_forward,
        grid=(blocks,),
        in_specs=[smem, whole((rows, width))] + [whole(mixer[0].shape)] * 4,
        out_specs=[column] * 4 + [wide, whole((width, rows)), whole((2, width))],
        out_shape=shapes(((rows, chans), BF), ((rows, chans), F32), ((rows, chans), BF), ((rows, chans), BF),
                         ((width, 3 * chans), BF), ((width, rows), BF), ((2, width), F32)),
        scratch_shapes=[pltpu.VMEM((SLOTS, LANES), F32), pltpu.VMEM((1, chans), F32), pltpu.VMEM((rows, width), BF),
                        pltpu.VMEM((rows, 3 * LANES), F32), pltpu.VMEM((rows, LANES), F32)],
        compiler_params=params(),
        cost_estimate=pl.CostEstimate(flops=6 * rows * width * chans, bytes_accessed=32 << 20, transcendentals=0),
        name="mixer_forward",
    )(dev, xp, *mixer)
    if fast:
        last = after(more_f, hb)
        feed = (eight_f, more_f, send(eight_f, CORE, "feed_core"), send(last, CORE, "feed_core_more"))

    size = width // 8
    piece = (SLOTS // 2,) + feed[0].shape[1:]
    block_out, dy1, dmix, wo, keep1, send1, gmlp_small = pl.pallas_call(
        feed_forward,
        in_specs=[smem] * 3 + [pl.BlockSpec(memory_space=pltpu.VMEM)] + [pl.BlockSpec(memory_space=pl.ANY)] * 7,
        out_specs=[pl.BlockSpec(memory_space=pl.ANY)] * 6 + [pl.BlockSpec(memory_space=pltpu.VMEM)],
        out_shape=shapes(((rows, width), BF), ((rows, width), F32), ((rows, width), BF), ((chans, width), BF),
                         (piece, BF), (piece, BF), ((SLOTS, LANES), F32)),
        scratch_shapes=[
            pltpu.VMEM((SLOTS, piece[1] - 2 * size, width), BF),
            pltpu.VMEM((SLOTS, 2 * size, width), BF),
            pltpu.VMEM((rows, chans), BF),
            pltpu.VMEM((rows, width), BF),
            pltpu.VMEM((rows, width), BF),
            pltpu.VMEM((chans, width), BF),
            pltpu.VMEM((rows, width), F32),
            pltpu.VMEM((rows, width), BF),
            pltpu.VMEM((width, rows), BF),
            pltpu.VMEM((width, rows), BF),
            pltpu.VMEM((rows, width), F32),
            pltpu.VMEM((rows, width), F32),
            pltpu.VMEM((width, width), BF),
            pltpu.VMEM((width, width), BF),
            pltpu.VMEM((SLOTS,) + piece[1:], BF),
            pltpu.VMEM((rows, width), BF),
            pltpu.VMEM((rows, width), F32),
            pltpu.VMEM((rows, width), BF),
            pltpu.SemaphoreType.DMA((20,)),
        ],
        compiler_params=params(),
        cost_estimate=pl.CostEstimate(flops=2 * rows * width * (24 * width + 2 * chans), bytes_accessed=60 << 20, transcendentals=0),
        name="feed_forward",
    )(dev, slot, cols, gains, *feed, hb, xp, dyp)

    piece = (SLOTS // 2, 3 * blocks * 16 + 16, LANES)
    dk, keep2, send2 = pl.pallas_call(
        mixer_backward,
        grid=(blocks,),
        in_specs=[smem, whole((rows, width)), whole((width, rows)), whole((chans, width)), whole((SLOTS, LANES)),
                  column, column, column],
        out_specs=[pl.BlockSpec((rows, 3 * LANES), lambda i: (0, i))] + [whole(piece)] * 2,
        out_shape=shapes(((rows, 3 * chans), BF), (piece, BF), (piece, BF)),
        scratch_shapes=[pltpu.VMEM((1, chans), F32), pltpu.VMEM((blocks, rows, LANES), F32),
                        pltpu.VMEM((width, 3 * LANES), BF)],
        compiler_params=params(),
        cost_estimate=pl.CostEstimate(flops=8 * rows * width * chans, bytes_accessed=40 << 20, transcendentals=0),
        name="mixer_backward",
    )(dev, dmix, xn1t, wo, gmlp_small, forget, u1, u2)

    tile = 256
    tokens_grad = pl.pallas_call(
        input_gradient,
        grid=(rows // tile,),
        in_specs=[band(width), band(width), whole((2, width))] + [band(3 * chans), whole((width, 3 * chans))],
        out_specs=band(width),
        out_shape=jax.ShapeDtypeStruct((rows, width), F32),
        compiler_params=params(),
        cost_estimate=pl.CostEstimate(flops=6 * rows * width * chans, bytes_accessed=24 << 20, transcendentals=0),
        name="input_gradient",
    )(xp, dy1, gains, dk, w3)

    def uncut(v):
        v = v[:, : 48 * blocks].reshape(-1, blocks, 3, 16, LANES)
        return [v[:, :, k].transpose(0, 2, 1, 3).reshape(-1, 16, chans) for k in range(3)]

    if fast:
        half = SLOTS // 4
        got = send(send1, CORE, "feed_back_core")
        low, high = add(keep1[:half], got[:half]), add(keep1[half:], got[half:])
        low, high = fold(low, high, SECOND, "feed_back_second")
        low, high = fold(low, after(high, dk), FIRST, "feed_back_first")
        got = send(send2, CORE, "mixer_back_core")
        mlow, mhigh = add(keep2[:half], got[:half]), add(keep2[half:], got[half:])
        mlow, mhigh, low, high, _ = after_all(mlow, mhigh, low, high, tokens_grad)
        got, near = after_all(send(mhigh, SECOND, "mixer_back_second"), send(high, NEAR, "feed_back_near"))
        low, high = add(low[0], near[0]), add(low[1], near[1])
        half = SLOTS // 8
        mlow, mhigh = add(mlow[:half], got[:half]), add(mlow[half:], got[half:])
        mlow, mhigh, low, high = after_all(mlow, mhigh, low, high)
        got, far = after_all(send(mhigh, FIRST, "mixer_back_first"), send(high, FAR, "feed_back_far"))
        four = add(mlow, got)
        first = low.astype(F32) + far.astype(F32)
        total = four[0].astype(F32)
        for k, p in enumerate((FAR, NEAR, BOTH)):
            total = total + send(four[k + 1], p, "mixer_back_z").astype(F32)
        up_grad, down_grad, out_grad = first[:size], first[size : 2 * size].T, first[2 * size :]
        grads = [v[0] for v in uncut(total[None])]
        edge = total[48 * blocks]
        gmlp_grad = edge[:shard]
        bias_grad = edge[2 * shard : 2 * shard + chans // SLOTS]
    else:
        first, total = (jnp.concatenate(v).astype(F32) for v in ((keep1, send1), (keep2, send2)))

        def summed(v, axis=0, names=AXES):
            return lax.psum_scatter(v, names, scatter_dimension=axis, tiled=True)

        def joined(base):
            w = first[:, base : base + size]
            return w.reshape(8, 4, size, width).transpose(0, 2, 1, 3).reshape(width, 4 * width)

        up_grad = summed(summed(joined(0), 0, "dp"), 1, "mp")
        down_grad = summed(summed(joined(size).T, 1, "dp"), 0, "mp")
        out_grad = summed(first[:, 2 * size :].reshape(chans, width))
        grads = [summed(v.reshape(width, chans)) for v in uncut(total)]
        edge = total[:, 48 * blocks]
        gmlp_grad = summed(edge[:, :shard].reshape(-1))
        bias_grad = summed(edge[:, 2 * shard : 2 * shard + chans // SLOTS].reshape(-1))

    dots = sum(
        jnp.sum(w.astype(F32) * g, axis=1) for w, g in zip((forget_weight, input_weight, candidate_weight), grads)
    )
    gmix_grad = dots / gain_mix.astype(F32)
    return (restore(block_out), restore(tokens_grad), gmix_grad, gmlp_grad, grads[0], grads[1], grads[2], bias_grad,
            out_grad, up_grad, down_grad)


def solution(mesh):
    fast = mesh.shape["dp"] == 8 and mesh.shape["mp"] == 4
    every = P(AXES, None)
    in_specs = (every, P(AXES), P(AXES), every, every, every, P(AXES), every, P("dp", "mp"), P("mp", "dp"), every)
    out_specs = (every, every, P(AXES), P(AXES), every, every, every, P(AXES), every, P("dp", "mp"), P("mp", "dp"))
    return jax.shard_map(
        functools.partial(local, fast), mesh=mesh, in_specs=in_specs, out_specs=out_specs, check_vma=False
    )
```

```python
import functools

import jax
import jax.numpy as jnp
import numpy as np
from jax import lax
from jax.experimental import pallas as pl
from jax.experimental.pallas import tpu as pltpu
from jax.sharding import PartitionSpec as P

LEN = 1024
EPSILON = 1e-06
AXES = ("dp", "mp")
SLOTS = 32
CHUNKS = 8
LANES = 256
GROUP = 8
BF = jnp.bfloat16
F32 = jnp.float32
MIB = 1024 * 1024
C0 = 0.7978845608028654
C1 = C0 * 0.044715


def params(mib):
    return pltpu.CompilerParams(vmem_limit_bytes=mib * MIB)


def dot(a, b, dims=((1,), (0,))):
    return lax.dot_general(a, b, (dims, ((), ())), preferred_element_type=F32)


def whole(shape):
    return pl.BlockSpec(shape, lambda *_: (0,) * len(shape), pipeline_mode=pl.Buffered(1))


def aligned(start, size):
    return pl.ds(pl.multiple_of(start, size), size)


def spread(small, piece, width):
    lane = lax.broadcasted_iota(jnp.int32, (LANES, width), 0)
    column = lax.broadcasted_iota(jnp.int32, (LANES, width), 1)
    pick = (lane == column % piece).astype(BF)
    placed = dot(small.astype(BF), pick)
    row = lax.broadcasted_iota(jnp.int32, (SLOTS, width), 0)
    col = lax.broadcasted_iota(jnp.int32, (SLOTS, width), 1)
    return jnp.sum(jnp.where(col // piece == row, placed, 0.0), axis=0, keepdims=True)


def collect(vector, offset, piece):
    width = vector.shape[1]
    row = lax.broadcasted_iota(jnp.int32, (SLOTS, width), 0)
    col = lax.broadcasted_iota(jnp.int32, (SLOTS, width), 1)
    kept = jnp.where(col // piece == row, vector, 0.0).astype(BF)
    column = lax.broadcasted_iota(jnp.int32, (width, LANES), 0)
    lane = lax.broadcasted_iota(jnp.int32, (width, LANES), 1)
    pick = (lane == offset + column % piece).astype(BF)
    return dot(kept, pick)


def pack_mixer(forget_ref, input_ref, cand_ref, gmix_ref, gmlp_ref, bias_ref, out_ref, small):
    blocks = forget_ref.shape[1] // LANES
    for b in range(blocks):
        for w, ref in enumerate((forget_ref, input_ref, cand_ref)):
            at = (b * 3 + w) * 16
            out_ref[at : at + 16, :] = ref[:, b * LANES : (b + 1) * LANES]
    small[...] = jnp.zeros_like(small)
    for k, ref in enumerate((gmix_ref, gmlp_ref, bias_ref)):
        small[k : k + 1, 0 : ref.shape[1]] = ref[...].astype(F32)
    out_ref[48 * blocks :, :] = small[...].astype(BF)


def mixer_prepare(dev_ref, parts, x_ref, xn_ref, xnt_ref, gain_ref, bias_s, small):
    per = SLOTS // 4
    tail = parts[0].shape[1] - 16
    for s in range(SLOTS):
        rows = parts[s // per][s % per, tail : tail + 16, :].astype(F32)
        for k in range(3):
            small[k, pl.ds(dev_ref[s], 1), :] = rows[k : k + 1, :]
    width, chans = x_ref.shape[1], bias_s.shape[1]
    piece = width // SLOTS
    gmix = spread(small[0], piece, width)
    gain_ref[0:1, :] = gmix
    gain_ref[1:2, :] = spread(small[1], piece, width)
    bias_s[...] = spread(small[2], chans // SLOTS, chans)

    def rows(i, _):
        at = aligned(i * 256, 256)
        v = x_ref[at, :].astype(F32)
        scale = lax.rsqrt(jnp.mean(v * v, axis=-1, keepdims=True) + EPSILON)
        xn = ((v * scale) * gmix).astype(BF)
        xn_ref[at, :] = xn
        xnt_ref[:, at] = xn.T
        return 0

    lax.fori_loop(0, x_ref.shape[0] // 256, rows, 0)


def mixer_forward(dev_ref, x_ref, g0, g1, g2, g3, hb_ref, o_ref, u1_ref, u2_ref, w_ref, xnt_ref, gain_ref,
                  small, bias_s, xn_s, k_s, c2_s, f_s):
    step = pl.program_id(0)
    per = SLOTS // 4
    parts = (g0, g1, g2, g3)

    @pl.when(step == 0)
    def _():
        mixer_prepare(dev_ref, parts, x_ref, xn_s, xnt_ref, gain_ref, bias_s, small)

    for s in range(SLOTS):
        d = dev_ref[s]
        for w in range(3):
            src = aligned((step * 3 + w) * 16, 16)
            w_ref[aligned(d * 16, 16), w * LANES : (w + 1) * LANES] = parts[s // per][s % per, src, :]

    bias = bias_s[:, aligned(step * LANES, LANES)]
    k_s[...] = dot(xn_s[...], w_ref[...])
    kf_c, ki_c, kc_c = (slice(w * LANES, (w + 1) * LANES) for w in range(3))
    zeros = jnp.zeros((CHUNKS, LANES), F32)
    tile = GROUP * CHUNKS
    count = xn_s.shape[0] // tile

    def first(i, carry):
        h, prod = carry
        at = aligned(i * tile, tile)
        kf = k_s[at, kf_c]
        ki = k_s[at, ki_c] + bias
        kc = k_s[at, kc_c]
        low = jnp.minimum(jnp.minimum(kf, ki), 0.0)
        one = jnp.exp(low)
        ef = jnp.exp(low - kf)
        ei = jnp.exp(low - ki)
        a = one + ei
        b = one + ef
        inv = 1.0 / (a + b)
        forget = a * inv
        other = b * inv
        f_s[at, :] = forget
        o_ref[at, :] = other.astype(BF)
        drive = other * kc
        k_s[at, kf_c] = forget * (inv * ef)
        k_s[at, ki_c] = other * (inv * ei)
        c2_s[at, :] = drive
        for k in range(GROUP):
            part = slice(k * CHUNKS, (k + 1) * CHUNKS)
            h = forget[part] * h + drive[part]
            prod = prod * forget[part]
        return h, prod

    last, prod = lax.fori_loop(0, count, first, (zeros, zeros + 1.0))
    sub = lax.broadcasted_iota(jnp.int32, (CHUNKS, LANES), 0)
    start = zeros
    for s in range(CHUNKS - 1):
        moved = pltpu.roll(last + prod * start, 1, 0)
        start = jnp.where(sub == s + 1, moved, start)

    def second(i, h):
        at = aligned(i * tile, tile)
        forget = f_s[at, :]
        drive = c2_s[at, :]
        before, after = [], []
        for k in range(GROUP):
            part = slice(k * CHUNKS, (k + 1) * CHUNKS)
            before.append(h)
            h = forget[part] * h + drive[part]
            after.append(h)
        diff = jnp.concatenate(before, axis=0) - k_s[at, kc_c]
        hb_ref[at, :] = jnp.concatenate(after, axis=0).astype(BF)
        u1_ref[at, :] = (k_s[at, kf_c] * diff).astype(BF)
        u2_ref[at, :] = (k_s[at, ki_c] * -diff).astype(BF)
        return h

    lax.fori_loop(0, count, second, start)


def feed_forward(dev_ref, gain_ref, g0, g1, g2, g3, hb_ref, x_ref, dy_ref,
                 out_ref, dmix_ref, wo_ref, low_ref, high_ref, send_ref, small_ref,
                 y1_s, xn_s, xnt_s, dyt_s, acc_s, dxn_s, up_s, dn_s, upg_s, dng_s, wog_s):
    parts = (g0, g1, g2, g3)
    per = SLOTS // 4
    tokens, width = x_ref.shape
    chans = hb_ref.shape[1]
    rows = width // 8
    feed = 2 * rows
    gain = gain_ref[1:2, :]

    def target(s):
        return (low_ref, high_ref, send_ref, send_ref)[s // per], s % per + (per if s >= 3 * per else 0)

    for s in range(SLOTS):
        wo_ref[aligned(dev_ref[s] * 32, 32), :] = parts[s // per][s % per, feed:, :]

    def rows_in(i, _):
        at = aligned(i * 256, 256)
        y1 = x_ref[at, :].astype(F32) + dot(hb_ref[at, :], wo_ref[...])
        y1_s[at, :] = y1
        scale = lax.rsqrt(jnp.mean(y1 * y1, axis=-1, keepdims=True) + EPSILON)
        xn = ((y1 * scale) * gain).astype(BF)
        xn_s[at, :] = xn
        xnt_s[:, at] = xn.T
        return 0

    lax.fori_loop(0, tokens // 256, rows_in, 0)
    dyt_s[...] = dy_ref[...].T

    for base in (0, SLOTS // 2):
        slots = range(base, base + SLOTS // 2)
        for s in slots:
            d = dev_ref[s]
            block, at = d // 2 % 2, aligned(d // 4 * rows, rows)
            up_s[block, at, :] = parts[s // per][s % per, 0:rows, :]
            dn_s[block, at, :] = parts[s // per][s % per, rows:feed, :]
        for block in range(2):
            pre = dot(xn_s[...], up_s[block])
            dact = dot(dy_ref[...], dn_s[block])
            sq = pre * pre
            gate = 0.5 + 0.5 * jnp.tanh(pre * (C0 + C1 * sq))
            value = pre * gate
            act = value.astype(BF)
            slope = gate + value * (1.0 - gate) * (2.0 * C0 + 6.0 * C1 * sq)
            dpre = (slope * dact).astype(BF)
            upg_s[block] = dot(xnt_s[...], dpre).astype(BF)
            dng_s[block] = dot(dyt_s[...], act).astype(BF)
            out = dot(act, dn_s[block], ((1,), (1,)))
            dxn = dot(dpre, up_s[block], ((1,), (1,)))
            if base + block == 0:
                acc_s[...] = out
                dxn_s[...] = dxn
            else:
                acc_s[...] += out
                dxn_s[...] += dxn
        for s in slots:
            d = dev_ref[s]
            block, at = d // 2 % 2, aligned(d // 4 * rows, rows)
            ref, k = target(s)
            ref[k, 0:rows, :] = upg_s[block, at, :]
            ref[k, rows:feed, :] = dng_s[block, at, :]

    total = jnp.zeros((1, width), F32)
    for i in range(tokens // 256):
        at = slice(i * 256, (i + 1) * 256)
        y1 = y1_s[at, :]
        scale = lax.rsqrt(jnp.mean(y1 * y1, axis=-1, keepdims=True) + EPSILON)
        n2 = y1 * scale
        out_ref[at, :] = (y1 + acc_s[at, :]).astype(BF)
        dxn = dxn_s[at, :]
        dn = dxn * gain
        dy1 = dy_ref[at, :].astype(F32) + scale * (dn - n2 * jnp.mean(dn * n2, axis=-1, keepdims=True))
        dmix_ref[at, :] = dy1.astype(BF)
        total = total + jnp.sum(dxn * n2, axis=0, keepdims=True)
    small_ref[...] = collect(total, 0, width // SLOTS)

    span = 256
    for b in range(chans // span):
        wog_s[b * span : (b + 1) * span, :] = dot(
            hb_ref[:, b * span : (b + 1) * span], dmix_ref[...], ((0,), (0,))
        ).astype(BF)
    for s in range(SLOTS):
        ref, k = target(s)
        ref[k, feed:, :] = wog_s[aligned(dev_ref[s] * 32, 32), :]


def mixer_backward(dev_ref, dmix_ref, xnt_ref, wo_ref, small_ref, o_ref, u1_ref, u2_ref,
                   dk_ref, keep_ref, send_ref, bias_s, dh_s, grad_s):
    step = pl.program_id(0)
    blocks = pl.num_programs(0)
    width, tokens = xnt_ref.shape
    half = SLOTS // 2

    @pl.when(step == 0)
    def _():
        for b in range(dh_s.shape[0]):
            dh_s[b] = dot(dmix_ref[...], wo_ref[b * LANES : (b + 1) * LANES, :], ((1,), (1,)))

    zeros = jnp.zeros((CHUNKS, LANES), F32)
    tile = GROUP * CHUNKS
    count = tokens // tile

    def first(i, carry):
        g, prod, decay = carry
        at = aligned((count - 1 - i) * tile, tile)
        dh = dh_s[step, at, :]
        forget = 1.0 - o_ref[at, :].astype(F32)
        for k in reversed(range(GROUP)):
            part = slice(k * CHUNKS, (k + 1) * CHUNKS)
            g = dh[part] + decay * g
            prod = prod * decay
            decay = forget[part]
        return g, prod, decay

    ones = zeros + 1.0
    head, prod, decay = lax.fori_loop(0, count, first, (zeros, ones, ones))
    sub = lax.broadcasted_iota(jnp.int32, (CHUNKS, LANES), 0)
    start = zeros
    for s in reversed(range(1, CHUNKS)):
        moved = pltpu.roll(decay * (head + prod * start), CHUNKS - 1, 0)
        start = jnp.where(sub == s - 1, moved, start)

    def second(i, carry):
        g, decay, total = carry
        at = aligned((count - 1 - i) * tile, tile)
        dh = dh_s[step, at, :]
        other = o_ref[at, :].astype(F32)
        forget = 1.0 - other
        parts = [None] * GROUP
        for k in reversed(range(GROUP)):
            part = slice(k * CHUNKS, (k + 1) * CHUNKS)
            g = dh[part] + decay * g
            decay = forget[part]
            parts[k] = g
        grad = jnp.concatenate(parts, axis=0)
        dk_ref[at, 0:LANES] = (u1_ref[at, :].astype(F32) * grad).astype(BF)
        di = (u2_ref[at, :].astype(F32) * grad).astype(BF)
        dk_ref[at, LANES : 2 * LANES] = di
        dk_ref[at, 2 * LANES : 3 * LANES] = (other * grad).astype(BF)
        di = di.astype(F32)
        for k in range(GROUP):
            total = total + di[k * CHUNKS : (k + 1) * CHUNKS]
        return g, decay, total

    _, _, total = lax.fori_loop(0, count, second, (start, ones, zeros))
    bias_s[:, aligned(step * LANES, LANES)] = jnp.sum(total, axis=0, keepdims=True)

    grad_s[...] = dot(xnt_ref[...], dk_ref[...]).astype(BF)
    for s in range(SLOTS):
        target = keep_ref if s < half else send_ref
        src = aligned(dev_ref[s] * 16, 16)
        for w in range(3):
            dst = aligned((step * 3 + w) * 16, 16)
            target[s % half, dst, :] = grad_s[src, w * LANES : (w + 1) * LANES]

    @pl.when(step == blocks - 1)
    def _():
        bias = bias_s[...]
        piece = width // SLOTS
        values = small_ref[...] + collect(bias, 2 * piece, bias.shape[1] // SLOTS)
        dh_s[0, 0:SLOTS, :] = values
        row = lax.broadcasted_iota(jnp.int32, (16, LANES), 0)
        tail = keep_ref.shape[1] - 16
        for s in range(SLOTS):
            target = keep_ref if s < half else send_ref
            values = dh_s[0, pl.ds(dev_ref[s], 1), :]
            target[s % half, tail : tail + 16, :] = jnp.where(row == 0, values, 0.0).astype(BF)


def input_gradient(x_ref, dmix_ref, gain_ref, dk_ref, w_ref, out_ref):
    size = dk_ref.shape[2]
    dxn = dot(dk_ref[0], w_ref[:, :size], ((1,), (1,)))
    for b in range(1, dk_ref.shape[0]):
        dxn = dxn + dot(dk_ref[b], w_ref[:, b * size : (b + 1) * size], ((1,), (1,)))
    v = x_ref[...].astype(F32)
    scale = lax.rsqrt(jnp.mean(v * v, axis=-1, keepdims=True) + EPSILON)
    n1 = v * scale
    dn = dxn * gain_ref[0:1, :]
    out_ref[...] = dmix_ref[...].astype(F32) + scale * (dn - n1 * jnp.mean(dn * n1, axis=-1, keepdims=True))


def finish_mixer(own_ref, p0, p1, p2, forget_ref, input_ref, cand_ref, gain_ref,
                 fg_ref, ig_ref, cg_ref, gmix_ref, gmlp_ref, bias_ref):
    total = own_ref[...].astype(F32)
    for ref in (p0, p1, p2):
        total = total + ref[...].astype(F32)
    chans = fg_ref.shape[1]
    dots = jnp.zeros((16, 1), F32)
    for b in range(chans // LANES):
        cols = slice(b * LANES, (b + 1) * LANES)
        for w, (ref, weight) in enumerate(((fg_ref, forget_ref), (ig_ref, input_ref), (cg_ref, cand_ref))):
            grad = total[(b * 3 + w) * 16 : (b * 3 + w + 1) * 16]
            ref[:, cols] = grad
            dots = dots + jnp.sum(grad * weight[:, cols].astype(F32), axis=1, keepdims=True)
    row = jnp.broadcast_to(dots, (16, 128)).T[0:1, :]
    gmix_ref[...] = row / gain_ref[...].astype(F32)
    edge = total[chans // LANES * 48 : chans // LANES * 48 + 1]
    piece = gmlp_ref.shape[1]
    gmlp_ref[...] = edge[:, :piece]
    bias_ref[...] = edge[:, 2 * piece : 2 * piece + bias_ref.shape[1]]


def order_table():
    table = np.zeros((SLOTS, SLOTS), np.int32)
    for me in range(SLOTS):
        core, y, x, z = me & 1, me >> 1 & 1, me >> 2 & 1, me >> 3
        for slot in range(SLOTS):
            oc, second, first, oz = slot >> 4, slot >> 3 & 1, slot >> 2 & 1, (slot & 1) << 1 | slot >> 1 & 1
            c2 = core ^ oc
            x2 = x ^ (first if c2 == 0 else second)
            y2 = y ^ (second if c2 == 0 else first)
            table[me, slot] = ((z ^ oz) * 2 + x2) * 4 + y2 * 2 + c2
    return table


def flip(x0, y0, z0, c0, x1, y1, z1, c1):
    pairs = []
    for me in range(SLOTS):
        x, y, z, c = (x1, y1, z1, c1) if me & 1 else (x0, y0, z0, c0)
        pairs.append((me, me ^ (z << 3 | x << 2 | y << 1 | c)))
    return pairs


FAR, NEAR, BOTH = [flip(0, 0, k, 0, 0, 0, k, 0) for k in (2, 1, 3)]
FIRST = flip(1, 0, 0, 0, 0, 1, 0, 0)
SECOND = flip(0, 1, 0, 0, 1, 0, 0, 0)
CORE = flip(0, 0, 0, 1, 0, 0, 0, 1)


def send(value, pairs, name):
    with jax.named_scope(name):
        return lax.ppermute(value, AXES, pairs)


def after(value, *others):
    return lax.optimization_barrier((value,) + others)[0]


def after_all(*values):
    return lax.optimization_barrier(values)


def add(a, b):
    return (a.astype(F32) + b.astype(F32)).astype(BF)


def fold(low, high, pairs, name):
    got = send(high, pairs, name)
    half = low.shape[0] // 2
    return add(low[:half], got[:half]), add(low[half:], got[half:])


def pack(forget_weight, input_weight, candidate_weight, gain_mix, gain_mlp, input_gate_bias):
    rows = 3 * forget_weight.shape[1] // LANES * 16 + 16
    return pl.pallas_call(
        pack_mixer,
        out_shape=jax.ShapeDtypeStruct((rows, LANES), BF),
        scratch_shapes=[pltpu.VMEM((16, LANES), F32)],
        compiler_params=params(60),
        name="pack",
    )(forget_weight, input_weight, candidate_weight, gain_mix[None], gain_mlp[None], input_gate_bias[None])


def local(fast, tokens, gain_mix, gain_mlp, forget_weight, input_weight, candidate_weight, input_gate_bias,
          output_weight, up_weight, down_weight, cotangent):
    rows, width = tokens.shape
    chans = forget_weight.shape[1]
    blocks = chans // LANES
    shard = width // SLOTS

    def permute(v):
        return v.reshape(CHUNKS, rows // CHUNKS, width).transpose(1, 0, 2).reshape(rows, width)

    def restore(v):
        return v.reshape(rows // CHUNKS, CHUNKS, width).transpose(1, 0, 2).reshape(rows, width)

    xp = permute(tokens)
    dyp = permute(cotangent)
    if fast:
        me = lax.axis_index(AXES)
        table = order_table()
        dev = lax.dynamic_index_in_dim(jnp.asarray(table), me, keepdims=False)
        piece = pack(forget_weight, input_weight, candidate_weight, gain_mix, gain_mlp, input_gate_bias)
        four = jnp.stack([piece] + [send(piece, p, "mixer_z") for p in (FAR, NEAR, BOTH)])
        four, piece_f = after_all(four, jnp.concatenate([up_weight, down_weight.T, output_weight]), dev, xp, dyp)[:2]
        got, far_f = after_all(send(four, FIRST, "mixer_first"), send(piece_f, FAR, "feed_far"))
        eight = jnp.concatenate([four, got])
        two_f = jnp.stack([piece_f, far_f])
        eight, two_f = after_all(eight, two_f)
        more, got = after_all(send(eight, SECOND, "mixer_second"), send(two_f, NEAR, "feed_near"))
        four_f = jnp.concatenate([two_f, got])
        more, four_f = after_all(more, four_f)
        got, core, core_more = after_all(
            send(four_f, FIRST, "feed_first"), send(eight, CORE, "mixer_core"), send(more, CORE, "mixer_core_more")
        )
        eight_f = jnp.concatenate([four_f, got])
        mixer = (eight, more, core, core_more)
        mixer, eight_f = lax.optimization_barrier((mixer, eight_f))
        more_f = send(eight_f, SECOND, "feed_second")
    else:
        order = np.argsort(np.arange(SLOTS) % 2, kind="stable").astype(np.int32)
        dev = jnp.asarray(order)

        def full(v, axis=0, names=AXES):
            return lax.all_gather(v, names, axis=axis, tiled=True)

        gm, gl, gb = full(gain_mix), full(gain_mlp), full(input_gate_bias)
        weights = [full(w) for w in (forget_weight, input_weight, candidate_weight)]
        smalls = [v.reshape(SLOTS, -1) for v in (gm, gl, gb)]
        up = full(full(up_weight, 0, "dp"), 1, "mp")
        down = full(full(down_weight, 1, "dp"), 0, "mp")

        def regroup(w):
            return w.reshape(8, width // 8, 4, width).transpose(0, 2, 1, 3).reshape(SLOTS, width // 8, width)

        both = jnp.concatenate([regroup(up), regroup(down.T), full(output_weight).reshape(SLOTS, -1, width)], axis=1)

        def quarters(v):
            return tuple(jnp.stack([v[d] for d in order[k * 8 : (k + 1) * 8]]) for k in range(4))

        mixer = quarters(
            jnp.stack([pack(*[w[s * 16 : (s + 1) * 16] for w in weights], *[v[s] for v in smalls]) for s in range(SLOTS)])
        )
        feed = quarters(both)

    smem = pl.BlockSpec(memory_space=pltpu.SMEM)
    vmem = pl.BlockSpec(memory_space=pltpu.VMEM)
    part = 256

    def band(cols):
        return pl.BlockSpec((part, cols), lambda i: (i, 0))

    def shapes(*items):
        return [jax.ShapeDtypeStruct(shape, kind) for shape, kind in items]

    column = pl.BlockSpec((rows, LANES), lambda i: (0, i))
    block = pl.BlockSpec((None, rows, LANES), lambda i: (i, 0, 0))

    wide = pl.BlockSpec((width, 3 * LANES), lambda i: (0, i))
    hb, other, u1, u2, w3, xn1t, gains = pl.pallas_call(
        mixer_forward,
        grid=(blocks,),
        in_specs=[smem, whole((rows, width))] + [whole(mixer[0].shape)] * 4,
        out_specs=[column] + [block] * 3 + [wide, whole((width, rows)), whole((2, width))],
        out_shape=shapes(((rows, chans), BF), *[((blocks, rows, LANES), BF)] * 3,
                         ((width, 3 * chans), BF), ((width, rows), BF), ((2, width), F32)),
        scratch_shapes=[pltpu.VMEM((3, SLOTS, LANES), F32), pltpu.VMEM((1, chans), F32), pltpu.VMEM((rows, width), BF),
                        pltpu.VMEM((rows, 3 * LANES), F32), pltpu.VMEM((rows, LANES), F32),
                        pltpu.VMEM((rows, LANES), F32)],
        compiler_params=params(16),
        cost_estimate=pl.CostEstimate(flops=6 * rows * width * chans, bytes_accessed=32 << 20, transcendentals=0),
        name="mixer_forward",
    )(dev, xp, *mixer)
    if fast:
        last = after(more_f, hb)
        feed = (eight_f, more_f, send(eight_f, CORE, "feed_core"), send(last, CORE, "feed_core_more"))

    size = width // 8
    piece = feed[0].shape[1:]
    block_out, dmix, wo, low1, high1, send1, gmlp_small = pl.pallas_call(
        feed_forward,
        in_specs=[smem] + [vmem] * 8,
        out_specs=[vmem] * 7,
        out_shape=shapes(((rows, width), BF), ((rows, width), BF), ((chans, width), BF),
                         *[((count,) + piece, BF) for count in (SLOTS // 4, SLOTS // 4, SLOTS // 2)], ((SLOTS, LANES), F32)),
        scratch_shapes=[
            pltpu.VMEM((rows, width), F32),
            pltpu.VMEM((rows, width), BF),
            pltpu.VMEM((width, rows), BF),
            pltpu.VMEM((width, rows), BF),
            pltpu.VMEM((rows, width), F32),
            pltpu.VMEM((rows, width), F32),
            *[pltpu.VMEM((2, width, width), BF)] * 4,
            pltpu.VMEM((chans, width), BF),
        ],
        compiler_params=params(30),
        cost_estimate=pl.CostEstimate(flops=2 * rows * width * (24 * width + 2 * chans), bytes_accessed=60 << 20, transcendentals=0),
        name="feed_forward",
    )(dev, gains, *feed, hb, xp, dyp)

    if fast:
        half = SLOTS // 4
        got = send(send1, CORE, "feed_back_core")
        high = add(high1, got[half:])
        high, dmix = after_all(high, dmix)
    piece = (SLOTS // 2, 3 * blocks * 16 + 16, LANES)
    dk, keep2, send2 = pl.pallas_call(
        mixer_backward,
        grid=(blocks,),
        in_specs=[smem, whole((rows, width)), whole((width, rows)), whole((chans, width)), whole((SLOTS, LANES)),
                  block, block, block],
        out_specs=[pl.BlockSpec((None, rows, 3 * LANES), lambda i: (i, 0, 0))] + [whole(piece)] * 2,
        out_shape=shapes(((blocks, rows, 3 * LANES), BF), (piece, BF), (piece, BF)),
        scratch_shapes=[pltpu.VMEM((1, chans), F32), pltpu.VMEM((blocks, rows, LANES), F32),
                        pltpu.VMEM((width, 3 * LANES), BF)],
        compiler_params=params(16),
        cost_estimate=pl.CostEstimate(flops=8 * rows * width * chans, bytes_accessed=40 << 20, transcendentals=0),
        name="mixer_backward",
    )(dev, dmix, xn1t, wo, gmlp_small, other, u1, u2)

    def input_grad(dk_later):
        return pl.pallas_call(
            input_gradient,
            grid=(rows // part,),
            in_specs=[band(width), band(width), whole((2, width))] + [pl.BlockSpec((blocks, part, 3 * LANES), lambda i: (0, i, 0)), whole((width, 3 * chans))],
            out_specs=band(width),
            out_shape=jax.ShapeDtypeStruct((rows, width), F32),
            compiler_params=params(14),
            cost_estimate=pl.CostEstimate(flops=6 * rows * width * chans, bytes_accessed=24 << 20, transcendentals=0),
            name="input_gradient",
        )(xp, dmix, gains, dk_later, w3)

    def uncut(v):
        v = v[:, : 48 * blocks].reshape(-1, blocks, 3, 16, LANES)
        return [v[:, :, k].transpose(0, 2, 1, 3).reshape(-1, 16, chans) for k in range(3)]

    if fast:
        low = add(after(low1, dk), got[:half])
        low, high = fold(low, high, SECOND, "feed_back_second")
        low, high = fold(low, after(high, dk), FIRST, "feed_back_first")
        got = send(send2, CORE, "mixer_back_core")
        mlow, mhigh = add(keep2[:half], got[:half]), add(keep2[half:], got[half:])
        mlow, mhigh, low, high, dk = after_all(mlow, mhigh, low, high, dk)
        got, near, tokens_grad = after_all(
            send(mhigh, SECOND, "mixer_back_second"), send(high, NEAR, "feed_back_near"), input_grad(dk)
        )
        low, high = add(low[0], near[0]), add(low[1], near[1])
        half = SLOTS // 8
        mlow, mhigh = add(mlow[:half], got[:half]), add(mlow[half:], got[half:])
        mlow, mhigh, low, high = after_all(mlow, mhigh, low, high)
        got, far = after_all(send(mhigh, FIRST, "mixer_back_first"), send(high, FAR, "feed_back_far"))
        four = add(mlow, got)
        first = low.astype(F32) + far.astype(F32)
        parts = [send(four[k + 1], p, "mixer_back_z") for k, p in enumerate((FAR, NEAR, BOTH))]
        up_grad, down_grad, out_grad = first[:size], first[size : 2 * size].T, first[2 * size :]
        *grads, gmix_grad, gmlp_grad, bias_grad = pl.pallas_call(
            finish_mixer,
            out_shape=shapes(*[((16, chans), F32)] * 3, ((1, shard), F32), ((1, shard), F32), ((1, chans // SLOTS), F32)),
            compiler_params=params(16),
            name="finish",
        )(four[0], *parts, forget_weight, input_weight, candidate_weight, gain_mix[None])
        gmix_grad, gmlp_grad, bias_grad = gmix_grad[0], gmlp_grad[0], bias_grad[0]
    else:
        tokens_grad = input_grad(dk)
        first, total = (
            jnp.stack([jnp.concatenate(v)[k] for k in np.argsort(order)]).astype(F32)
            for v in ((low1, high1, send1), (keep2, send2))
        )

        def summed(v, axis=0, names=AXES):
            return lax.psum_scatter(v, names, scatter_dimension=axis, tiled=True)

        def joined(base):
            w = first[:, base : base + size]
            return w.reshape(8, 4, size, width).transpose(0, 2, 1, 3).reshape(width, 4 * width)

        up_grad = summed(summed(joined(0), 0, "dp"), 1, "mp")
        down_grad = summed(summed(joined(size).T, 1, "dp"), 0, "mp")
        out_grad = summed(first[:, 2 * size :].reshape(chans, width))
        grads = [summed(v.reshape(width, chans)) for v in uncut(total)]
        edge = total[:, 48 * blocks]
        gmlp_grad = summed(edge[:, :shard].reshape(-1))
        bias_grad = summed(edge[:, 2 * shard : 2 * shard + chans // SLOTS].reshape(-1))
        dots = sum(
            jnp.sum(w.astype(F32) * g, axis=1) for w, g in zip((forget_weight, input_weight, candidate_weight), grads)
        )
        gmix_grad = dots / gain_mix.astype(F32)

    return (restore(block_out), restore(tokens_grad), gmix_grad, gmlp_grad, grads[0], grads[1], grads[2], bias_grad,
            out_grad, up_grad, down_grad)


def solution(mesh):
    fast = mesh.shape["dp"] == 8 and mesh.shape["mp"] == 4
    every = P(AXES, None)
    in_specs = (every, P(AXES), P(AXES), every, every, every, P(AXES), every, P("dp", "mp"), P("mp", "dp"), every)
    out_specs = (every, every, P(AXES), P(AXES), every, every, every, P(AXES), every, P("dp", "mp"), P("mp", "dp"))
    return jax.shard_map(
        functools.partial(local, fast), mesh=mesh, in_specs=in_specs, out_specs=out_specs, check_vma=False
    )
```

```python
import functools

import jax
import jax.numpy as jnp
import numpy as np
from jax import lax
from jax.experimental import pallas as pl
from jax.experimental.pallas import tpu as pltpu
from jax.sharding import PartitionSpec as P

LEN = 1024
EPSILON = 1e-06
AXES = ("dp", "mp")
SLOTS = 32
CHUNKS = 8
LANES = 256
GROUP = 8
BF = jnp.bfloat16
F32 = jnp.float32
MIB = 1024 * 1024
C0 = 0.7978845608028654
C1 = C0 * 0.044715


def params(mib):
    return pltpu.CompilerParams(vmem_limit_bytes=mib * MIB)


def dot(a, b, dims=((1,), (0,))):
    return lax.dot_general(a, b, (dims, ((), ())), preferred_element_type=F32)


def whole(shape):
    return pl.BlockSpec(shape, lambda *_: (0,) * len(shape), pipeline_mode=pl.Buffered(1))


def aligned(start, size):
    return pl.ds(pl.multiple_of(start, size), size)


def spread(small, piece, width):
    lane = lax.broadcasted_iota(jnp.int32, (LANES, width), 0)
    column = lax.broadcasted_iota(jnp.int32, (LANES, width), 1)
    pick = (lane == column % piece).astype(BF)
    placed = dot(small.astype(BF), pick)
    row = lax.broadcasted_iota(jnp.int32, (SLOTS, width), 0)
    col = lax.broadcasted_iota(jnp.int32, (SLOTS, width), 1)
    return jnp.sum(jnp.where(col // piece == row, placed, 0.0), axis=0, keepdims=True)


def collect(vector, offset, piece):
    width = vector.shape[1]
    row = lax.broadcasted_iota(jnp.int32, (SLOTS, width), 0)
    col = lax.broadcasted_iota(jnp.int32, (SLOTS, width), 1)
    kept = jnp.where(col // piece == row, vector, 0.0).astype(BF)
    column = lax.broadcasted_iota(jnp.int32, (width, LANES), 0)
    lane = lax.broadcasted_iota(jnp.int32, (width, LANES), 1)
    pick = (lane == offset + column % piece).astype(BF)
    return dot(kept, pick)


def pack_mixer(forget_ref, input_ref, cand_ref, gmix_ref, gmlp_ref, bias_ref, out_ref, small):
    blocks = forget_ref.shape[1] // LANES
    for b in range(blocks):
        for w, ref in enumerate((forget_ref, input_ref, cand_ref)):
            at = (b * 3 + w) * 16
            out_ref[at : at + 16, :] = ref[:, b * LANES : (b + 1) * LANES]
    small[...] = jnp.zeros_like(small)
    for k, ref in enumerate((gmix_ref, gmlp_ref, bias_ref)):
        small[k : k + 1, 0 : ref.shape[1]] = ref[...].astype(F32)
    out_ref[48 * blocks :, :] = small[...].astype(BF)


def mixer_prepare(dev_ref, parts, x_ref, xn_ref, xnt_ref, gain_ref, bias_s, small):
    per = SLOTS // 4
    tail = parts[0].shape[1] - 16
    for s in range(SLOTS):
        rows = parts[s // per][s % per, tail : tail + 16, :].astype(F32)
        for k in range(3):
            small[k, pl.ds(dev_ref[s], 1), :] = rows[k : k + 1, :]
    width, chans = x_ref.shape[1], bias_s.shape[1]
    piece = width // SLOTS
    gmix = spread(small[0], piece, width)
    gain_ref[0:1, :] = gmix
    gain_ref[1:2, :] = spread(small[1], piece, width)
    bias_s[...] = spread(small[2], chans // SLOTS, chans)

    def rows(i, _):
        at = aligned(i * 256, 256)
        v = x_ref[at, :].astype(F32)
        scale = lax.rsqrt(jnp.mean(v * v, axis=-1, keepdims=True) + EPSILON)
        xn = ((v * scale) * gmix).astype(BF)
        xn_ref[at, :] = xn
        xnt_ref[:, at] = xn.T
        return 0

    lax.fori_loop(0, x_ref.shape[0] // 256, rows, 0)


def mixer_forward(dev_ref, x_ref, g0, g1, g2, g3, hb_ref, o_ref, u1_ref, u2_ref, w_ref, xnt_ref, gain_ref,
                  small, bias_s, xn_s, k_s, c2_s, f_s):
    step = pl.program_id(0)
    per = SLOTS // 4
    parts = (g0, g1, g2, g3)

    @pl.when(step == 0)
    def _():
        mixer_prepare(dev_ref, parts, x_ref, xn_s, xnt_ref, gain_ref, bias_s, small)

    for s in range(SLOTS):
        d = dev_ref[s]
        for w in range(3):
            src = aligned((step * 3 + w) * 16, 16)
            w_ref[aligned(d * 16, 16), w * LANES : (w + 1) * LANES] = parts[s // per][s % per, src, :]

    bias = bias_s[:, aligned(step * LANES, LANES)]
    k_s[...] = dot(xn_s[...], w_ref[...])
    kf_c, ki_c, kc_c = (slice(w * LANES, (w + 1) * LANES) for w in range(3))
    zeros = jnp.zeros((CHUNKS, LANES), F32)
    tile = GROUP * CHUNKS
    count = xn_s.shape[0] // tile

    def first(i, carry):
        h, prod = carry
        at = aligned(i * tile, tile)
        kf = k_s[at, kf_c]
        ki = k_s[at, ki_c] + bias
        kc = k_s[at, kc_c]
        low = jnp.minimum(jnp.minimum(kf, ki), 0.0)
        one = jnp.exp(low)
        ef = jnp.exp(low - kf)
        ei = jnp.exp(low - ki)
        a = one + ei
        b = one + ef
        inv = 1.0 / (a + b)
        forget = a * inv
        other = b * inv
        f_s[at, :] = forget
        o_ref[at, :] = other.astype(BF)
        drive = other * kc
        k_s[at, kf_c] = forget * (inv * ef)
        k_s[at, ki_c] = other * (inv * ei)
        c2_s[at, :] = drive
        for k in range(GROUP):
            part = slice(k * CHUNKS, (k + 1) * CHUNKS)
            h = forget[part] * h + drive[part]
            prod = prod * forget[part]
        return h, prod

    last, prod = lax.fori_loop(0, count, first, (zeros, zeros + 1.0))
    sub = lax.broadcasted_iota(jnp.int32, (CHUNKS, LANES), 0)
    start = zeros
    for s in range(CHUNKS - 1):
        moved = pltpu.roll(last + prod * start, 1, 0)
        start = jnp.where(sub == s + 1, moved, start)

    def second(i, h):
        at = aligned(i * tile, tile)
        forget = f_s[at, :]
        drive = c2_s[at, :]
        before, after = [], []
        for k in range(GROUP):
            part = slice(k * CHUNKS, (k + 1) * CHUNKS)
            before.append(h)
            h = forget[part] * h + drive[part]
            after.append(h)
        diff = jnp.concatenate(before, axis=0) - k_s[at, kc_c]
        hb_ref[at, :] = jnp.concatenate(after, axis=0).astype(BF)
        u1_ref[at, :] = (k_s[at, kf_c] * diff).astype(BF)
        u2_ref[at, :] = (k_s[at, ki_c] * -diff).astype(BF)
        return h

    lax.fori_loop(0, count, second, start)


def hidden_units(dev_ref, parts, xn_ref, xnt_ref, dy_ref, dyt_ref, targets, add_out, up_s, dn_s, upg_s, dng_s):
    per = SLOTS // 4
    rows = up_s.shape[0] // 8
    for base in (0, SLOTS // 2):
        slots = range(base, base + SLOTS // 2)
        for s in slots:
            d = dev_ref[s]
            at, cols = aligned(d // 4 * rows, rows), aligned(d // 2 % 2 * LANES, LANES)
            up_s[at, cols] = parts[s // per][s % per, 0:rows, :]
            dn_s[at, cols] = parts[s // per][s % per, rows : 2 * rows, :]
        pre = dot(xn_ref[...], up_s[...])
        dact = dot(dy_ref[...], dn_s[...])
        sq = pre * pre
        gate = 0.5 + 0.5 * jnp.tanh(pre * (C0 + C1 * sq))
        value = pre * gate
        act = value.astype(BF)
        slope = gate + value * (1.0 - gate) * (2.0 * C0 + 6.0 * C1 * sq)
        dpre = (slope * dact).astype(BF)
        upg_s[...] = dot(xnt_ref[...], dpre).astype(BF)
        dng_s[...] = dot(dyt_ref[...], act).astype(BF)
        add_out(base == 0, dot(act, dn_s[...], ((1,), (1,))), dot(dpre, up_s[...], ((1,), (1,))))
        for s in slots:
            d = dev_ref[s]
            at, cols = aligned(d // 4 * rows, rows), aligned(d // 2 % 2 * LANES, LANES)
            ref, k = target(targets, s)
            ref[k, 0:rows, :] = upg_s[at, cols]
            ref[k, rows : 2 * rows, :] = dng_s[at, cols]


def target(targets, s):
    per = SLOTS // 4
    return (targets[0], s) if s < per else (targets[1], s - per) if s < 2 * per else (targets[2], s - 2 * per)


def feed_first(dev_ref, gain_ref, g0, g1, g2, g3, hb_ref, x_ref, dy_ref,
               y1_ref, xn_ref, xnt_ref, dyt_ref, acc_ref, dxn_ref, wo_ref, low_ref, high_ref, send_ref,
               up_s, dn_s, upg_s, dng_s):
    parts = (g0, g1, g2, g3)
    per = SLOTS // 4
    tokens, width = x_ref.shape
    feed = width // 4
    gain = gain_ref[1:2, :]
    for s in range(SLOTS):
        for c in range(width // LANES):
            piece = parts[s // per][s % per, feed + c * 32 : feed + (c + 1) * 32, :]
            wo_ref[aligned(dev_ref[s] * 32, 32), c * LANES : (c + 1) * LANES] = piece

    def rows_in(i, _):
        at = aligned(i * 256, 256)
        y1 = x_ref[at, :].astype(F32) + dot(hb_ref[at, :], wo_ref[...])
        y1_ref[at, :] = y1
        scale = lax.rsqrt(jnp.mean(y1 * y1, axis=-1, keepdims=True) + EPSILON)
        xn = ((y1 * scale) * gain).astype(BF)
        xn_ref[at, :] = xn
        xnt_ref[:, at] = xn.T
        return 0

    lax.fori_loop(0, tokens // 256, rows_in, 0)
    dyt_ref[...] = dy_ref[...].T

    def add_out(first, out, dxn):
        acc_ref[...] = out if first else acc_ref[...] + out
        dxn_ref[...] = dxn if first else dxn_ref[...] + dxn

    hidden_units(dev_ref, parts, xn_ref, xnt_ref, dy_ref, dyt_ref, (low_ref, high_ref, send_ref), add_out,
                 up_s, dn_s, upg_s, dng_s)


def feed_last(dev_ref, gain_ref, g0, g1, g2, g3, hb_ref, dy_ref, y1_ref, xn_ref, xnt_ref, dyt_ref, acc_ref, dxn_ref,
              out_ref, dmix_ref, low_ref, high_ref, send_ref, small_ref,
              up_s, dn_s, upg_s, dng_s, acc_s, dxn_s, wog_s):
    tokens, width = dy_ref.shape
    chans = hb_ref.shape[1]
    feed = width // 4
    gain = gain_ref[1:2, :]
    targets = (low_ref, high_ref, send_ref)

    def add_out(first, out, dxn):
        acc_s[...] = (acc_ref if first else acc_s)[...] + out
        dxn_s[...] = (dxn_ref if first else dxn_s)[...] + dxn

    hidden_units(dev_ref, (g0, g1, g2, g3), xn_ref, xnt_ref, dy_ref, dyt_ref, targets, add_out, up_s, dn_s, upg_s, dng_s)

    total = jnp.zeros((1, width), F32)
    for i in range(tokens // 256):
        at = slice(i * 256, (i + 1) * 256)
        y1 = y1_ref[at, :]
        scale = lax.rsqrt(jnp.mean(y1 * y1, axis=-1, keepdims=True) + EPSILON)
        n2 = y1 * scale
        out_ref[at, :] = (y1 + acc_s[at, :]).astype(BF)
        dxn = dxn_s[at, :]
        dn = dxn * gain
        dy1 = dy_ref[at, :].astype(F32) + scale * (dn - n2 * jnp.mean(dn * n2, axis=-1, keepdims=True))
        dmix_ref[at, :] = dy1.astype(BF)
        total = total + jnp.sum(dxn * n2, axis=0, keepdims=True)
    small_ref[...] = collect(total, 0, width // SLOTS)

    span = 256
    for b in range(chans // span):
        wog_s[b * span : (b + 1) * span, :] = dot(
            hb_ref[:, b * span : (b + 1) * span], dmix_ref[...], ((0,), (0,))
        ).astype(BF)
    for s in range(SLOTS):
        ref, k = target(targets, s)
        for c in range(width // LANES):
            piece = wog_s[aligned(dev_ref[s] * 32, 32), c * LANES : (c + 1) * LANES]
            ref[k, feed + c * 32 : feed + (c + 1) * 32, :] = piece


def mixer_backward(dev_ref, dmix_ref, xnt_ref, wo_ref, small_ref, o_ref, u1_ref, u2_ref,
                   dk_ref, keep_ref, send_ref, bias_s, dh_s, grad_s):
    step = pl.program_id(0)
    blocks = pl.num_programs(0)
    width, tokens = xnt_ref.shape
    half = SLOTS // 2

    @pl.when(step == 0)
    def _():
        for b in range(dh_s.shape[0]):
            dh_s[b] = dot(dmix_ref[...], wo_ref[b * LANES : (b + 1) * LANES, :], ((1,), (1,)))

    zeros = jnp.zeros((CHUNKS, LANES), F32)
    tile = GROUP * CHUNKS
    count = tokens // tile

    def first(i, carry):
        g, prod, decay = carry
        at = aligned((count - 1 - i) * tile, tile)
        dh = dh_s[step, at, :]
        forget = 1.0 - o_ref[at, :].astype(F32)
        for k in reversed(range(GROUP)):
            part = slice(k * CHUNKS, (k + 1) * CHUNKS)
            g = dh[part] + decay * g
            prod = prod * decay
            decay = forget[part]
        return g, prod, decay

    ones = zeros + 1.0
    head, prod, decay = lax.fori_loop(0, count, first, (zeros, ones, ones))
    sub = lax.broadcasted_iota(jnp.int32, (CHUNKS, LANES), 0)
    start = zeros
    for s in reversed(range(1, CHUNKS)):
        moved = pltpu.roll(decay * (head + prod * start), CHUNKS - 1, 0)
        start = jnp.where(sub == s - 1, moved, start)

    def second(i, carry):
        g, decay, total = carry
        at = aligned((count - 1 - i) * tile, tile)
        dh = dh_s[step, at, :]
        other = o_ref[at, :].astype(F32)
        forget = 1.0 - other
        parts = [None] * GROUP
        for k in reversed(range(GROUP)):
            part = slice(k * CHUNKS, (k + 1) * CHUNKS)
            g = dh[part] + decay * g
            decay = forget[part]
            parts[k] = g
        grad = jnp.concatenate(parts, axis=0)
        dk_ref[at, 0:LANES] = (u1_ref[at, :].astype(F32) * grad).astype(BF)
        di = (u2_ref[at, :].astype(F32) * grad).astype(BF)
        dk_ref[at, LANES : 2 * LANES] = di
        dk_ref[at, 2 * LANES : 3 * LANES] = (other * grad).astype(BF)
        di = di.astype(F32)
        for k in range(GROUP):
            total = total + di[k * CHUNKS : (k + 1) * CHUNKS]
        return g, decay, total

    _, _, total = lax.fori_loop(0, count, second, (start, ones, zeros))
    bias_s[:, aligned(step * LANES, LANES)] = jnp.sum(total, axis=0, keepdims=True)

    grad_s[...] = dot(xnt_ref[...], dk_ref[...]).astype(BF)
    for s in range(SLOTS):
        target = keep_ref if s < half else send_ref
        src = aligned(dev_ref[s] * 16, 16)
        for w in range(3):
            dst = aligned((step * 3 + w) * 16, 16)
            target[s % half, dst, :] = grad_s[src, w * LANES : (w + 1) * LANES]

    @pl.when(step == blocks - 1)
    def _():
        bias = bias_s[...]
        piece = width // SLOTS
        values = small_ref[...] + collect(bias, 2 * piece, bias.shape[1] // SLOTS)
        dh_s[0, 0:SLOTS, :] = values
        row = lax.broadcasted_iota(jnp.int32, (16, LANES), 0)
        tail = keep_ref.shape[1] - 16
        for s in range(SLOTS):
            target = keep_ref if s < half else send_ref
            values = dh_s[0, pl.ds(dev_ref[s], 1), :]
            target[s % half, tail : tail + 16, :] = jnp.where(row == 0, values, 0.0).astype(BF)


def input_gradient(x_ref, dmix_ref, gain_ref, dk_ref, w_ref, out_ref):
    size = dk_ref.shape[2]
    dxn = dot(dk_ref[0], w_ref[:, :size], ((1,), (1,)))
    for b in range(1, dk_ref.shape[0]):
        dxn = dxn + dot(dk_ref[b], w_ref[:, b * size : (b + 1) * size], ((1,), (1,)))
    v = x_ref[...].astype(F32)
    scale = lax.rsqrt(jnp.mean(v * v, axis=-1, keepdims=True) + EPSILON)
    n1 = v * scale
    dn = dxn * gain_ref[0:1, :]
    out_ref[...] = dmix_ref[...].astype(F32) + scale * (dn - n1 * jnp.mean(dn * n1, axis=-1, keepdims=True))


def finish_mixer(own_ref, p0, p1, p2, forget_ref, input_ref, cand_ref, gain_ref,
                 fg_ref, ig_ref, cg_ref, gmix_ref, gmlp_ref, bias_ref):
    total = own_ref[...].astype(F32)
    for ref in (p0, p1, p2):
        total = total + ref[...].astype(F32)
    chans = fg_ref.shape[1]
    dots = jnp.zeros((16, 1), F32)
    for b in range(chans // LANES):
        cols = slice(b * LANES, (b + 1) * LANES)
        for w, (ref, weight) in enumerate(((fg_ref, forget_ref), (ig_ref, input_ref), (cg_ref, cand_ref))):
            grad = total[(b * 3 + w) * 16 : (b * 3 + w + 1) * 16]
            ref[:, cols] = grad
            dots = dots + jnp.sum(grad * weight[:, cols].astype(F32), axis=1, keepdims=True)
    row = jnp.broadcast_to(dots, (16, 128)).T[0:1, :]
    gmix_ref[...] = row / gain_ref[...].astype(F32)
    edge = total[chans // LANES * 48 : chans // LANES * 48 + 1]
    piece = gmlp_ref.shape[1]
    gmlp_ref[...] = edge[:, :piece]
    bias_ref[...] = edge[:, 2 * piece : 2 * piece + bias_ref.shape[1]]


def order_table():
    table = np.zeros((SLOTS, SLOTS), np.int32)
    for me in range(SLOTS):
        core, y, x, z = me & 1, me >> 1 & 1, me >> 2 & 1, me >> 3
        for slot in range(SLOTS):
            oc, second, first, oz = slot >> 4, slot >> 3 & 1, slot >> 2 & 1, (slot & 1) << 1 | slot >> 1 & 1
            c2 = core ^ oc
            x2 = x ^ (first if c2 == 0 else second)
            y2 = y ^ (second if c2 == 0 else first)
            table[me, slot] = ((z ^ oz) * 2 + x2) * 4 + y2 * 2 + c2
    return table


def flip(x0, y0, z0, c0, x1, y1, z1, c1):
    pairs = []
    for me in range(SLOTS):
        x, y, z, c = (x1, y1, z1, c1) if me & 1 else (x0, y0, z0, c0)
        pairs.append((me, me ^ (z << 3 | x << 2 | y << 1 | c)))
    return pairs


FAR, NEAR, BOTH = [flip(0, 0, k, 0, 0, 0, k, 0) for k in (2, 1, 3)]
FIRST = flip(1, 0, 0, 0, 0, 1, 0, 0)
SECOND = flip(0, 1, 0, 0, 1, 0, 0, 0)
CORE = flip(0, 0, 0, 1, 0, 0, 0, 1)


def send(value, pairs, name):
    with jax.named_scope(name):
        return lax.ppermute(value, AXES, pairs)


def after(value, *others):
    return lax.optimization_barrier((value,) + others)[0]


def after_all(*values):
    return lax.optimization_barrier(values)


def add(a, b):
    return (a.astype(F32) + b.astype(F32)).astype(BF)


def fold(low, high, pairs, name):
    got = send(high, pairs, name)
    half = low.shape[0] // 2
    return add(low[:half], got[:half]), add(low[half:], got[half:])


def pack(forget_weight, input_weight, candidate_weight, gain_mix, gain_mlp, input_gate_bias):
    rows = 3 * forget_weight.shape[1] // LANES * 16 + 16
    return pl.pallas_call(
        pack_mixer,
        out_shape=jax.ShapeDtypeStruct((rows, LANES), BF),
        scratch_shapes=[pltpu.VMEM((16, LANES), F32)],
        compiler_params=params(60),
        name="pack",
    )(forget_weight, input_weight, candidate_weight, gain_mix[None], gain_mlp[None], input_gate_bias[None])


def local(fast, tokens, gain_mix, gain_mlp, forget_weight, input_weight, candidate_weight, input_gate_bias,
          output_weight, up_weight, down_weight, cotangent):
    rows, width = tokens.shape
    chans = forget_weight.shape[1]
    blocks = chans // LANES
    shard = width // SLOTS

    def permute(v):
        return v.reshape(CHUNKS, rows // CHUNKS, width).transpose(1, 0, 2).reshape(rows, width)

    def restore(v):
        return v.reshape(rows // CHUNKS, CHUNKS, width).transpose(1, 0, 2).reshape(rows, width)

    xp = permute(tokens)
    dyp = permute(cotangent)
    def pack_feed(up, down, out):
        pieces = [v[:, c : c + LANES] for v in (up, down, out) for c in (0, LANES)]
        return jnp.concatenate([pieces[0], pieces[2], pieces[4], pieces[5]]), jnp.concatenate([pieces[1], pieces[3]])

    if fast:
        me = lax.axis_index(AXES)
        table = order_table()
        dev = lax.dynamic_index_in_dim(jnp.asarray(table), me, keepdims=False)
        piece = pack(forget_weight, input_weight, candidate_weight, gain_mix, gain_mlp, input_gate_bias)
        four = jnp.stack([piece] + [send(piece, p, "mixer_z") for p in (FAR, NEAR, BOTH)])
        piece1, piece2 = pack_feed(up_weight, down_weight.T, output_weight)
        four, piece1, piece2, *_ = after_all(four, piece1, piece2, dev, xp, dyp)
        got, far1 = after_all(send(four, FIRST, "mixer_first"), send(piece1, FAR, "feed1_far"))
        eight, two1, piece2 = after_all(jnp.concatenate([four, got]), jnp.stack([piece1, far1]), piece2)
        more, near1, far2 = after_all(
            send(eight, SECOND, "mixer_second"), send(two1, NEAR, "feed1_near"), send(piece2, FAR, "feed2_far")
        )
        more, four1, two2 = after_all(more, jnp.concatenate([two1, near1]), jnp.stack([piece2, far2]))
        got1, near2, core, core_more = after_all(
            send(four1, FIRST, "feed1_first"), send(two2, NEAR, "feed2_near"),
            send(eight, CORE, "mixer_core"), send(more, CORE, "mixer_core_more"),
        )
        eight1, four2 = jnp.concatenate([four1, got1]), jnp.concatenate([two2, near2])
        mixer, eight1, four2 = after_all((eight, more, core, core_more), eight1, four2)
        more1 = send(eight1, SECOND, "feed1_second")
        got2 = send(four2, FIRST, "feed2_first")
    else:
        order = np.argsort(np.arange(SLOTS) % 2, kind="stable").astype(np.int32)
        dev = jnp.asarray(order)

        def full(v, axis=0, names=AXES):
            return lax.all_gather(v, names, axis=axis, tiled=True)

        gm, gl, gb = full(gain_mix), full(gain_mlp), full(input_gate_bias)
        weights = [full(w) for w in (forget_weight, input_weight, candidate_weight)]
        smalls = [v.reshape(SLOTS, -1) for v in (gm, gl, gb)]
        up = full(full(up_weight, 0, "dp"), 1, "mp")
        down = full(full(down_weight, 1, "dp"), 0, "mp")

        def regroup(w):
            return w.reshape(8, width // 8, 4, width).transpose(0, 2, 1, 3).reshape(SLOTS, width // 8, width)

        both = [
            pack_feed(*v) for v in zip(regroup(up), regroup(down.T), full(output_weight).reshape(SLOTS, -1, width))
        ]

        def quarters(v):
            return tuple(jnp.stack([v[d] for d in order[k * 8 : (k + 1) * 8]]) for k in range(4))

        mixer = quarters(
            jnp.stack([pack(*[w[s * 16 : (s + 1) * 16] for w in weights], *[v[s] for v in smalls]) for s in range(SLOTS)])
        )
        feed1, feed2 = (quarters([v[k] for v in both]) for k in range(2))

    smem = pl.BlockSpec(memory_space=pltpu.SMEM)
    vmem = pl.BlockSpec(memory_space=pltpu.VMEM)
    part = 256

    def band(cols):
        return pl.BlockSpec((part, cols), lambda i: (i, 0))

    def shapes(*items):
        return [jax.ShapeDtypeStruct(shape, kind) for shape, kind in items]

    column = pl.BlockSpec((rows, LANES), lambda i: (0, i))
    block = pl.BlockSpec((None, rows, LANES), lambda i: (i, 0, 0))

    wide = pl.BlockSpec((width, 3 * LANES), lambda i: (0, i))
    hb, other, u1, u2, w3, xn1t, gains = pl.pallas_call(
        mixer_forward,
        grid=(blocks,),
        in_specs=[smem, whole((rows, width))] + [whole(mixer[0].shape)] * 4,
        out_specs=[column] + [block] * 3 + [wide, whole((width, rows)), whole((2, width))],
        out_shape=shapes(((rows, chans), BF), *[((blocks, rows, LANES), BF)] * 3,
                         ((width, 3 * chans), BF), ((width, rows), BF), ((2, width), F32)),
        scratch_shapes=[pltpu.VMEM((3, SLOTS, LANES), F32), pltpu.VMEM((1, chans), F32), pltpu.VMEM((rows, width), BF),
                        pltpu.VMEM((rows, 3 * LANES), F32), pltpu.VMEM((rows, LANES), F32),
                        pltpu.VMEM((rows, LANES), F32)],
        compiler_params=params(16),
        cost_estimate=pl.CostEstimate(flops=6 * rows * width * chans, bytes_accessed=32 << 20, transcendentals=0),
        name="mixer_forward",
    )(dev, xp, *mixer)
    if fast:
        core1 = send(eight1, CORE, "feed1_core")
        more1, got2, gains = after_all(more1, got2, gains)
        eight2 = jnp.concatenate([four2, got2])
        feed1 = (eight1, more1, core1, send(more1, CORE, "feed1_core_more"))
        more2 = send(eight2, SECOND, "feed2_second")

    size = width // 8
    weights = [pltpu.VMEM((width, 2 * LANES), BF)] * 4

    def pieces(count):
        return [((slots, count, LANES), BF) for slots in (SLOTS // 4, SLOTS // 4, SLOTS // 2)]

    y1, xn2, xn2t, dyt, acc, dxn2, wo, low1, high1, send1 = pl.pallas_call(
        feed_first,
        in_specs=[smem] + [vmem] * 8,
        out_specs=[vmem] * 10,
        out_shape=shapes(((rows, width), F32), ((rows, width), BF), ((width, rows), BF), ((width, rows), BF),
                         ((rows, width), F32), ((rows, width), F32), ((chans, width), BF), *pieces(2 * size)),
        scratch_shapes=weights,
        compiler_params=params(20),
        cost_estimate=pl.CostEstimate(flops=2 * rows * width * (12 * width + chans), bytes_accessed=30 << 20, transcendentals=0),
        name="feed_first",
    )(dev, gains, *feed1, hb, xp, dyp)
    if fast:
        core2 = send(eight2, CORE, "feed2_core")
        more2, y1, send1 = after_all(more2, y1, send1)
        feed2 = (eight2, more2, core2, send(more2, CORE, "feed2_core_more"))
        half = SLOTS // 4
        got1 = send(send1, CORE, "feed1_back_core")
        high1, y1 = after_all(add(high1, got1[half:]), y1)
        second1 = send(high1, SECOND, "feed1_back_second")
    block_out, dmix, low2, high2, send2, gmlp_small = pl.pallas_call(
        feed_last,
        in_specs=[smem] + [vmem] * 13,
        out_specs=[vmem] * 6,
        out_shape=shapes(((rows, width), BF), ((rows, width), BF), *pieces(3 * size), ((SLOTS, LANES), F32)),
        scratch_shapes=weights + [pltpu.VMEM((rows, width), F32)] * 2 + [pltpu.VMEM((chans, width), BF)],
        compiler_params=params(20),
        cost_estimate=pl.CostEstimate(flops=2 * rows * width * (12 * width + chans), bytes_accessed=30 << 20, transcendentals=0),
        name="feed_last",
    )(dev, gains, *feed2, hb, dyp, y1, xn2, xn2t, dyt, acc, dxn2)

    if fast:
        second1, dmix, send2 = after_all(second1, dmix, send2)
        got2 = send(send2, CORE, "feed2_back_core")
        high2, dmix = after_all(add(high2, got2[half:]), dmix)
        second2 = send(high2, SECOND, "feed2_back_second")
    piece = (SLOTS // 2, 3 * blocks * 16 + 16, LANES)
    dk, keep3, send3 = pl.pallas_call(
        mixer_backward,
        grid=(blocks,),
        in_specs=[smem, whole((rows, width)), whole((width, rows)), whole((chans, width)), whole((SLOTS, LANES)),
                  block, block, block],
        out_specs=[pl.BlockSpec((None, rows, 3 * LANES), lambda i: (i, 0, 0))] + [whole(piece)] * 2,
        out_shape=shapes(((blocks, rows, 3 * LANES), BF), (piece, BF), (piece, BF)),
        scratch_shapes=[pltpu.VMEM((1, chans), F32), pltpu.VMEM((blocks, rows, LANES), F32),
                        pltpu.VMEM((width, 3 * LANES), BF)],
        compiler_params=params(16),
        cost_estimate=pl.CostEstimate(flops=8 * rows * width * chans, bytes_accessed=40 << 20, transcendentals=0),
        name="mixer_backward",
    )(dev, dmix, xn1t, wo, gmlp_small, other, u1, u2)

    def input_grad(dk_later):
        return pl.pallas_call(
            input_gradient,
            grid=(rows // part,),
            in_specs=[band(width), band(width), whole((2, width))] + [pl.BlockSpec((blocks, part, 3 * LANES), lambda i: (0, i, 0)), whole((width, 3 * chans))],
            out_specs=band(width),
            out_shape=jax.ShapeDtypeStruct((rows, width), F32),
            compiler_params=params(14),
            cost_estimate=pl.CostEstimate(flops=6 * rows * width * chans, bytes_accessed=24 << 20, transcendentals=0),
            name="input_gradient",
        )(xp, dmix, gains, dk_later, w3)

    def uncut(v):
        v = v[:, : 48 * blocks].reshape(-1, blocks, 3, 16, LANES)
        return [v[:, :, k].transpose(0, 2, 1, 3).reshape(-1, 16, chans) for k in range(3)]

    if fast:
        second1, second2, low1, low2, dk = after_all(second1, second2, low1, low2, dk)
        low1, low2 = add(low1, got1[:half]), add(low2, got2[:half])
        low, high = (
            jnp.concatenate([add(low1[k], second1[k]), add(low2[k], second2[k])], axis=1)
            for k in (slice(0, half // 2), slice(half // 2, half))
        )
        low, high = fold(low, high, FIRST, "feed_back_first")
        got = send(send3, CORE, "mixer_back_core")
        mlow, mhigh = add(keep3[:half], got[:half]), add(keep3[half:], got[half:])
        mlow, mhigh, low, high, dk = after_all(mlow, mhigh, low, high, dk)
        got, near, tokens_grad = after_all(
            send(mhigh, SECOND, "mixer_back_second"), send(high, NEAR, "feed_back_near"), input_grad(dk)
        )
        low, high = add(low[0], near[0]), add(low[1], near[1])
        half = SLOTS // 8
        mlow, mhigh = add(mlow[:half], got[:half]), add(mlow[half:], got[half:])
        mlow, mhigh, low, high = after_all(mlow, mhigh, low, high)
        got, far = after_all(send(mhigh, FIRST, "mixer_back_first"), send(high, FAR, "feed_back_far"))
        four = add(mlow, got)
        first = low.astype(F32) + far.astype(F32)
        parts = [send(four[k + 1], p, "mixer_back_z") for k, p in enumerate((FAR, NEAR, BOTH))]
        up_grad, down_grad, out_grad = (
            jnp.concatenate([first[a : a + count], first[b : b + count]], axis=1)
            for a, b, count in ((0, 2 * size, size), (size, 3 * size, size), (4 * size, 4 * size + 32, 32))
        )
        down_grad = down_grad.T
        *grads, gmix_grad, gmlp_grad, bias_grad = pl.pallas_call(
            finish_mixer,
            out_shape=shapes(*[((16, chans), F32)] * 3, ((1, shard), F32), ((1, shard), F32), ((1, chans // SLOTS), F32)),
            compiler_params=params(16),
            name="finish",
        )(four[0], *parts, forget_weight, input_weight, candidate_weight, gain_mix[None])
        gmix_grad, gmlp_grad, bias_grad = gmix_grad[0], gmlp_grad[0], bias_grad[0]
    else:
        tokens_grad = input_grad(dk)
        first, last, total = (
            jnp.stack([jnp.concatenate(v)[k] for k in np.argsort(order)]).astype(F32)
            for v in ((low1, high1, send1), (low2, high2, send2), (keep3, send3))
        )

        def summed(v, axis=0, names=AXES):
            return lax.psum_scatter(v, names, scatter_dimension=axis, tiled=True)

        def joined(base):
            w = jnp.concatenate([first[:, base : base + size], last[:, base : base + size]], axis=2)
            return w.reshape(8, 4, size, width).transpose(0, 2, 1, 3).reshape(width, 4 * width)

        up_grad = summed(summed(joined(0), 0, "dp"), 1, "mp")
        down_grad = summed(summed(joined(size).T, 1, "dp"), 0, "mp")
        out_grad = jnp.concatenate([last[:, 2 * size : 2 * size + 32], last[:, 2 * size + 32 :]], axis=2)
        out_grad = summed(out_grad.reshape(chans, width))
        grads = [summed(v.reshape(width, chans)) for v in uncut(total)]
        edge = total[:, 48 * blocks]
        gmlp_grad = summed(edge[:, :shard].reshape(-1))
        bias_grad = summed(edge[:, 2 * shard : 2 * shard + chans // SLOTS].reshape(-1))
        dots = sum(
            jnp.sum(w.astype(F32) * g, axis=1) for w, g in zip((forget_weight, input_weight, candidate_weight), grads)
        )
        gmix_grad = dots / gain_mix.astype(F32)

    return (restore(block_out), restore(tokens_grad), gmix_grad, gmlp_grad, grads[0], grads[1], grads[2], bias_grad,
            out_grad, up_grad, down_grad)


def solution(mesh):
    fast = mesh.shape["dp"] == 8 and mesh.shape["mp"] == 4
    every = P(AXES, None)
    in_specs = (every, P(AXES), P(AXES), every, every, every, P(AXES), every, P("dp", "mp"), P("mp", "dp"), every)
    out_specs = (every, every, P(AXES), P(AXES), every, every, every, P(AXES), every, P("dp", "mp"), P("mp", "dp"))
    return jax.shard_map(
        functools.partial(local, fast), mesh=mesh, in_specs=in_specs, out_specs=out_specs, check_vma=False
    )
```

```python
import functools

import jax
import jax.numpy as jnp
import numpy as np
from jax import lax
from jax.experimental import pallas as pl
from jax.experimental.pallas import tpu as pltpu
from jax.sharding import PartitionSpec as P

LEN = 1024
EPSILON = 1e-06
AXES = ("dp", "mp")
SLOTS = 32
CHUNKS = 8
LANES = 256
GROUP = 8
BF = jnp.bfloat16
F32 = jnp.float32
MIB = 1024 * 1024
C0 = 0.7978845608028654
C1 = C0 * 0.044715


def params(mib):
    return pltpu.CompilerParams(vmem_limit_bytes=mib * MIB)


def dot(a, b, dims=((1,), (0,))):
    return lax.dot_general(a, b, (dims, ((), ())), preferred_element_type=F32)


def whole(shape):
    return pl.BlockSpec(shape, lambda *_: (0,) * len(shape), pipeline_mode=pl.Buffered(1))


def aligned(start, size):
    return pl.ds(pl.multiple_of(start, size), size)


def spread(small, piece, width):
    lane = lax.broadcasted_iota(jnp.int32, (LANES, width), 0)
    column = lax.broadcasted_iota(jnp.int32, (LANES, width), 1)
    pick = (lane == column % piece).astype(BF)
    placed = dot(small.astype(BF), pick)
    row = lax.broadcasted_iota(jnp.int32, (SLOTS, width), 0)
    col = lax.broadcasted_iota(jnp.int32, (SLOTS, width), 1)
    return jnp.sum(jnp.where(col // piece == row, placed, 0.0), axis=0, keepdims=True)


def collect(vector, offset, piece):
    width = vector.shape[1]
    row = lax.broadcasted_iota(jnp.int32, (SLOTS, width), 0)
    col = lax.broadcasted_iota(jnp.int32, (SLOTS, width), 1)
    kept = jnp.where(col // piece == row, vector, 0.0).astype(BF)
    column = lax.broadcasted_iota(jnp.int32, (width, LANES), 0)
    lane = lax.broadcasted_iota(jnp.int32, (width, LANES), 1)
    pick = (lane == offset + column % piece).astype(BF)
    return dot(kept, pick)


def pack_mixer(forget_ref, input_ref, cand_ref, gmix_ref, gmlp_ref, bias_ref, out_ref, small):
    blocks = forget_ref.shape[1] // LANES
    for b in range(blocks):
        for w, ref in enumerate((forget_ref, input_ref, cand_ref)):
            at = (b * 3 + w) * 16
            out_ref[at : at + 16, :] = ref[:, b * LANES : (b + 1) * LANES]
    small[...] = jnp.zeros_like(small)
    for k, ref in enumerate((gmix_ref, gmlp_ref, bias_ref)):
        small[k : k + 1, 0 : ref.shape[1]] = ref[...].astype(F32)
    out_ref[48 * blocks :, :] = small[...].astype(BF)


def mixer_prepare(dev_ref, parts, x_ref, xn_ref, xnt_ref, gain_ref, bias_s, small):
    per = SLOTS // 4
    tail = parts[0].shape[1] - 16
    for s in range(SLOTS):
        rows = parts[s // per][s % per, tail : tail + 16, :].astype(F32)
        for k in range(3):
            small[k, pl.ds(dev_ref[s], 1), :] = rows[k : k + 1, :]
    width, chans = x_ref.shape[1], bias_s.shape[1]
    piece = width // SLOTS
    gmix = spread(small[0], piece, width)
    gain_ref[0:1, :] = gmix
    gain_ref[1:2, :] = spread(small[1], piece, width)
    bias_s[...] = spread(small[2], chans // SLOTS, chans)

    def rows(i, _):
        at = aligned(i * 256, 256)
        v = x_ref[at, :].astype(F32)
        scale = lax.rsqrt(jnp.mean(v * v, axis=-1, keepdims=True) + EPSILON)
        xn = ((v * scale) * gmix).astype(BF)
        xn_ref[at, :] = xn
        xnt_ref[:, at] = xn.T
        return 0

    lax.fori_loop(0, x_ref.shape[0] // 256, rows, 0)


def mixer_forward(dev_ref, x_ref, g0, g1, g2, g3, hb_ref, o_ref, u1_ref, u2_ref, w_ref, xnt_ref, gain_ref,
                  small, bias_s, xn_s, k_s, c2_s, f_s):
    step = pl.program_id(0)
    per = SLOTS // 4
    parts = (g0, g1, g2, g3)

    @pl.when(step == 0)
    def _():
        mixer_prepare(dev_ref, parts, x_ref, xn_s, xnt_ref, gain_ref, bias_s, small)

    for s in range(SLOTS):
        d = dev_ref[s]
        for w in range(3):
            src = aligned((step * 3 + w) * 16, 16)
            w_ref[aligned(d * 16, 16), w * LANES : (w + 1) * LANES] = parts[s // per][s % per, src, :]

    bias = bias_s[:, aligned(step * LANES, LANES)]
    kf_c, ki_c, kc_c = (slice(w * LANES, (w + 1) * LANES) for w in range(3))
    zeros = jnp.zeros((CHUNKS, LANES), F32)
    tile = GROUP * CHUNKS
    count = xn_s.shape[0] // tile
    span = 16 * CHUNKS

    def first(i, carry):
        h, prod = carry
        at = slice(i * span, (i + 1) * span)
        k = dot(xn_s[at, :], w_ref[...])
        kf, ki, kc = k[:, kf_c], k[:, ki_c] + bias, k[:, kc_c]
        k_s[at, kc_c] = kc
        low = jnp.minimum(jnp.minimum(kf, ki), 0.0)
        one = jnp.exp(low)
        ef = jnp.exp(low - kf)
        ei = jnp.exp(low - ki)
        a = one + ei
        b = one + ef
        inv = 1.0 / (a + b)
        forget = a * inv
        other = b * inv
        f_s[at, :] = forget
        o_ref[at, :] = other.astype(BF)
        drive = other * kc
        k_s[at, kf_c] = forget * (inv * ef)
        k_s[at, ki_c] = other * (inv * ei)
        c2_s[at, :] = drive
        for k in range(span // CHUNKS):
            part = slice(k * CHUNKS, (k + 1) * CHUNKS)
            h = forget[part] * h + drive[part]
            prod = prod * forget[part]
        return h, prod

    carry = zeros, zeros + 1.0
    for i in range(xn_s.shape[0] // span):
        carry = first(i, carry)
    last, prod = carry
    sub = lax.broadcasted_iota(jnp.int32, (CHUNKS, LANES), 0)
    start = zeros
    for s in range(CHUNKS - 1):
        moved = pltpu.roll(last + prod * start, 1, 0)
        start = jnp.where(sub == s + 1, moved, start)

    def second(i, h):
        at = aligned(i * tile, tile)
        forget = f_s[at, :]
        drive = c2_s[at, :]
        before, after = [], []
        for k in range(GROUP):
            part = slice(k * CHUNKS, (k + 1) * CHUNKS)
            before.append(h)
            h = forget[part] * h + drive[part]
            after.append(h)
        diff = jnp.concatenate(before, axis=0) - k_s[at, kc_c]
        hb_ref[at, :] = jnp.concatenate(after, axis=0).astype(BF)
        u1_ref[at, :] = (k_s[at, kf_c] * diff).astype(BF)
        u2_ref[at, :] = (k_s[at, ki_c] * -diff).astype(BF)
        return h

    lax.fori_loop(0, count, second, start)


def hidden_units(dev_ref, parts, xn_ref, xnt_ref, dy_ref, dyt_ref, targets, add_out, up_s, dn_s, upg_s, dng_s):
    per = SLOTS // 4
    rows = up_s.shape[0] // 8
    for base in (0, SLOTS // 2):
        slots = range(base, base + SLOTS // 2)
        for s in slots:
            d = dev_ref[s]
            at, cols = aligned(d // 4 * rows, rows), aligned(d // 2 % 2 * LANES, LANES)
            up_s[at, cols] = parts[s // per][s % per, 0:rows, :]
            dn_s[at, cols] = parts[s // per][s % per, rows : 2 * rows, :]
        pre = dot(xn_ref[...], up_s[...])
        dact = dot(dy_ref[...], dn_s[...])
        sq = pre * pre
        gate = 0.5 + 0.5 * jnp.tanh(pre * (C0 + C1 * sq))
        value = pre * gate
        act = value.astype(BF)
        slope = gate + value * (1.0 - gate) * (2.0 * C0 + 6.0 * C1 * sq)
        dpre = (slope * dact).astype(BF)
        upg_s[...] = dot(xnt_ref[...], dpre).astype(BF)
        dng_s[...] = dot(dyt_ref[...], act).astype(BF)
        add_out(base == 0, dot(act, dn_s[...], ((1,), (1,))), dot(dpre, up_s[...], ((1,), (1,))))
        for s in slots:
            d = dev_ref[s]
            at, cols = aligned(d // 4 * rows, rows), aligned(d // 2 % 2 * LANES, LANES)
            ref, k = target(targets, s)
            ref[k, 0:rows, :] = upg_s[at, cols]
            ref[k, rows : 2 * rows, :] = dng_s[at, cols]


def target(targets, s):
    per = SLOTS // 4
    return (targets[0], s) if s < per else (targets[1], s - per) if s < 2 * per else (targets[2], s - 2 * per)


def feed_prepare(dev_ref, gain_ref, g0, g1, g2, g3, hb_ref, x_ref, dy_ref, y1_ref, xn_ref, xnt_ref, dyt_ref, wo_ref):
    parts = (g0, g1, g2, g3)
    per = SLOTS // 4
    tokens, width = x_ref.shape
    feed = width // 4
    gain = gain_ref[1:2, :]
    for s in range(SLOTS):
        for c in range(width // LANES):
            piece = parts[s // per][s % per, feed + c * 32 : feed + (c + 1) * 32, :]
            wo_ref[aligned(dev_ref[s] * 32, 32), c * LANES : (c + 1) * LANES] = piece

    def rows_in(i, _):
        at = aligned(i * 256, 256)
        y1 = x_ref[at, :].astype(F32) + dot(hb_ref[at, :], wo_ref[...])
        y1_ref[at, :] = y1
        scale = lax.rsqrt(jnp.mean(y1 * y1, axis=-1, keepdims=True) + EPSILON)
        xn = ((y1 * scale) * gain).astype(BF)
        xn_ref[at, :] = xn
        xnt_ref[:, at] = xn.T
        return 0

    lax.fori_loop(0, tokens // 256, rows_in, 0)
    dyt_ref[...] = dy_ref[...].T


def feed_half(dev_ref, g0, g1, g2, g3, xn_ref, xnt_ref, dy_ref, dyt_ref, *refs):
    *before, acc_ref, dxn_ref, low_ref, high_ref, send_ref, up_s, dn_s, upg_s, dng_s = refs

    def add_out(first, out, dxn):
        for ref, old, value in zip((acc_ref, dxn_ref), before or (None, None), (out, dxn)):
            if not first:
                old = ref
            ref[...] = value if old is None else old[...] + value

    hidden_units(dev_ref, (g0, g1, g2, g3), xn_ref, xnt_ref, dy_ref, dyt_ref, (low_ref, high_ref, send_ref), add_out,
                 up_s, dn_s, upg_s, dng_s)


def feed_finish(dev_ref, gain_ref, hb_ref, dy_ref, y1_ref, acc_ref, dxn_ref,
                out_ref, dmix_ref, low_ref, high_ref, send_ref, small_ref, wog_s):
    tokens, width = dy_ref.shape
    chans = hb_ref.shape[1]
    gain = gain_ref[1:2, :]
    total = jnp.zeros((1, width), F32)
    for i in range(tokens // 256):
        at = slice(i * 256, (i + 1) * 256)
        y1 = y1_ref[at, :]
        scale = lax.rsqrt(jnp.mean(y1 * y1, axis=-1, keepdims=True) + EPSILON)
        n2 = y1 * scale
        out_ref[at, :] = (y1 + acc_ref[at, :]).astype(BF)
        dxn = dxn_ref[at, :]
        dn = dxn * gain
        dy1 = dy_ref[at, :].astype(F32) + scale * (dn - n2 * jnp.mean(dn * n2, axis=-1, keepdims=True))
        dmix_ref[at, :] = dy1.astype(BF)
        total = total + jnp.sum(dxn * n2, axis=0, keepdims=True)
    small_ref[...] = collect(total, 0, width // SLOTS)

    span = 256
    for b in range(chans // span):
        wog_s[b * span : (b + 1) * span, :] = dot(
            hb_ref[:, b * span : (b + 1) * span], dmix_ref[...], ((0,), (0,))
        ).astype(BF)
    for s in range(SLOTS):
        ref, k = target((low_ref, high_ref, send_ref), s)
        for c in range(width // LANES):
            piece = wog_s[aligned(dev_ref[s] * 32, 32), c * LANES : (c + 1) * LANES]
            ref[k, c * 32 : (c + 1) * 32, :] = piece


def mixer_backward(dev_ref, dmix_ref, xnt_ref, wo_ref, small_ref, o_ref, u1_ref, u2_ref,
                   dk_ref, keep_ref, send_ref, bias_s, dh_s, grad_s):
    step = pl.program_id(0)
    blocks = pl.num_programs(0)
    width, tokens = xnt_ref.shape
    half = SLOTS // 2

    @pl.when(step == 0)
    def _():
        for b in range(dh_s.shape[0]):
            dh_s[b] = dot(dmix_ref[...], wo_ref[b * LANES : (b + 1) * LANES, :], ((1,), (1,)))

    zeros = jnp.zeros((CHUNKS, LANES), F32)
    tile = GROUP * CHUNKS
    count = tokens // tile

    def first(i, carry):
        g, prod, decay = carry
        at = aligned((count - 1 - i) * tile, tile)
        dh = dh_s[step, at, :]
        forget = 1.0 - o_ref[at, :].astype(F32)
        for k in reversed(range(GROUP)):
            part = slice(k * CHUNKS, (k + 1) * CHUNKS)
            g = dh[part] + decay * g
            prod = prod * decay
            decay = forget[part]
        return g, prod, decay

    ones = zeros + 1.0
    head, prod, decay = lax.fori_loop(0, count, first, (zeros, ones, ones))
    sub = lax.broadcasted_iota(jnp.int32, (CHUNKS, LANES), 0)
    start = zeros
    for s in reversed(range(1, CHUNKS)):
        moved = pltpu.roll(decay * (head + prod * start), CHUNKS - 1, 0)
        start = jnp.where(sub == s - 1, moved, start)

    def second(i, carry):
        g, decay, total = carry
        at = aligned((count - 1 - i) * tile, tile)
        dh = dh_s[step, at, :]
        other = o_ref[at, :].astype(F32)
        forget = 1.0 - other
        parts = [None] * GROUP
        for k in reversed(range(GROUP)):
            part = slice(k * CHUNKS, (k + 1) * CHUNKS)
            g = dh[part] + decay * g
            decay = forget[part]
            parts[k] = g
        grad = jnp.concatenate(parts, axis=0)
        dk_ref[at, 0:LANES] = (u1_ref[at, :].astype(F32) * grad).astype(BF)
        di = (u2_ref[at, :].astype(F32) * grad).astype(BF)
        dk_ref[at, LANES : 2 * LANES] = di
        dk_ref[at, 2 * LANES : 3 * LANES] = (other * grad).astype(BF)
        di = di.astype(F32)
        for k in range(GROUP):
            total = total + di[k * CHUNKS : (k + 1) * CHUNKS]
        return g, decay, total

    _, _, total = lax.fori_loop(0, count, second, (start, ones, zeros))
    bias_s[:, aligned(step * LANES, LANES)] = jnp.sum(total, axis=0, keepdims=True)

    grad_s[...] = dot(xnt_ref[...], dk_ref[...]).astype(BF)
    for s in range(SLOTS):
        target = keep_ref if s < half else send_ref
        src = aligned(dev_ref[s] * 16, 16)
        for w in range(3):
            dst = aligned((step * 3 + w) * 16, 16)
            target[s % half, dst, :] = grad_s[src, w * LANES : (w + 1) * LANES]

    @pl.when(step == blocks - 1)
    def _():
        bias = bias_s[...]
        piece = width // SLOTS
        values = small_ref[...] + collect(bias, 2 * piece, bias.shape[1] // SLOTS)
        dh_s[0, 0:SLOTS, :] = values
        row = lax.broadcasted_iota(jnp.int32, (16, LANES), 0)
        tail = keep_ref.shape[1] - 16
        for s in range(SLOTS):
            target = keep_ref if s < half else send_ref
            values = dh_s[0, pl.ds(dev_ref[s], 1), :]
            target[s % half, tail : tail + 16, :] = jnp.where(row == 0, values, 0.0).astype(BF)


def input_gradient(x_ref, dmix_ref, gain_ref, dk_ref, w_ref, out_ref):
    size = dk_ref.shape[2]
    dxn = dot(dk_ref[0], w_ref[:, :size], ((1,), (1,)))
    for b in range(1, dk_ref.shape[0]):
        dxn = dxn + dot(dk_ref[b], w_ref[:, b * size : (b + 1) * size], ((1,), (1,)))
    v = x_ref[...].astype(F32)
    scale = lax.rsqrt(jnp.mean(v * v, axis=-1, keepdims=True) + EPSILON)
    n1 = v * scale
    dn = dxn * gain_ref[0:1, :]
    out_ref[...] = dmix_ref[...].astype(F32) + scale * (dn - n1 * jnp.mean(dn * n1, axis=-1, keepdims=True))


def finish_mixer(own_ref, p0, p1, p2, forget_ref, input_ref, cand_ref, gain_ref,
                 fg_ref, ig_ref, cg_ref, gmix_ref, gmlp_ref, bias_ref):
    total = own_ref[...].astype(F32)
    for ref in (p0, p1, p2):
        total = total + ref[...].astype(F32)
    chans = fg_ref.shape[1]
    dots = jnp.zeros((16, 1), F32)
    for b in range(chans // LANES):
        cols = slice(b * LANES, (b + 1) * LANES)
        for w, (ref, weight) in enumerate(((fg_ref, forget_ref), (ig_ref, input_ref), (cg_ref, cand_ref))):
            grad = total[(b * 3 + w) * 16 : (b * 3 + w + 1) * 16]
            ref[:, cols] = grad
            dots = dots + jnp.sum(grad * weight[:, cols].astype(F32), axis=1, keepdims=True)
    row = jnp.broadcast_to(dots, (16, 128)).T[0:1, :]
    gmix_ref[...] = row / gain_ref[...].astype(F32)
    edge = total[chans // LANES * 48 : chans // LANES * 48 + 1]
    piece = gmlp_ref.shape[1]
    gmlp_ref[...] = edge[:, :piece]
    bias_ref[...] = edge[:, 2 * piece : 2 * piece + bias_ref.shape[1]]


def order_table():
    table = np.zeros((SLOTS, SLOTS), np.int32)
    for me in range(SLOTS):
        core, y, x, z = me & 1, me >> 1 & 1, me >> 2 & 1, me >> 3
        for slot in range(SLOTS):
            oc, second, first, oz = slot >> 4, slot >> 3 & 1, slot >> 2 & 1, (slot & 1) << 1 | slot >> 1 & 1
            c2 = core ^ oc
            x2 = x ^ (first if c2 == 0 else second)
            y2 = y ^ (second if c2 == 0 else first)
            table[me, slot] = ((z ^ oz) * 2 + x2) * 4 + y2 * 2 + c2
    return table


def flip(x0, y0, z0, c0, x1, y1, z1, c1):
    pairs = []
    for me in range(SLOTS):
        x, y, z, c = (x1, y1, z1, c1) if me & 1 else (x0, y0, z0, c0)
        pairs.append((me, me ^ (z << 3 | x << 2 | y << 1 | c)))
    return pairs


FAR, NEAR, BOTH = [flip(0, 0, k, 0, 0, 0, k, 0) for k in (2, 1, 3)]
FIRST = flip(1, 0, 0, 0, 0, 1, 0, 0)
SECOND = flip(0, 1, 0, 0, 1, 0, 0, 0)
CORE = flip(0, 0, 0, 1, 0, 0, 0, 1)


def send(value, pairs, name):
    with jax.named_scope(name):
        return lax.ppermute(value, AXES, pairs)


def after(value, *others):
    return lax.optimization_barrier((value,) + others)[0]


def after_all(*values):
    return lax.optimization_barrier(values)


def add(a, b):
    return (a.astype(F32) + b.astype(F32)).astype(BF)


def fold(low, high, pairs, name):
    got = send(high, pairs, name)
    half = low.shape[0] // 2
    return add(low[:half], got[:half]), add(low[half:], got[half:])


def pack(forget_weight, input_weight, candidate_weight, gain_mix, gain_mlp, input_gate_bias):
    rows = 3 * forget_weight.shape[1] // LANES * 16 + 16
    return pl.pallas_call(
        pack_mixer,
        out_shape=jax.ShapeDtypeStruct((rows, LANES), BF),
        scratch_shapes=[pltpu.VMEM((16, LANES), F32)],
        compiler_params=params(60),
        name="pack",
    )(forget_weight, input_weight, candidate_weight, gain_mix[None], gain_mlp[None], input_gate_bias[None])


def local(fast, tokens, gain_mix, gain_mlp, forget_weight, input_weight, candidate_weight, input_gate_bias,
          output_weight, up_weight, down_weight, cotangent):
    rows, width = tokens.shape
    chans = forget_weight.shape[1]
    blocks = chans // LANES
    shard = width // SLOTS

    def permute(v):
        return v.reshape(CHUNKS, rows // CHUNKS, width).transpose(1, 0, 2).reshape(rows, width)

    def restore(v):
        return v.reshape(rows // CHUNKS, CHUNKS, width).transpose(1, 0, 2).reshape(rows, width)

    xp = permute(tokens)
    dyp = permute(cotangent)
    def pack_feed(up, down, out):
        pieces = [v[:, c : c + LANES] for v in (up, down, out) for c in (0, LANES)]
        return jnp.concatenate([pieces[0], pieces[2], pieces[4], pieces[5]]), jnp.concatenate([pieces[1], pieces[3]])

    if fast:
        me = lax.axis_index(AXES)
        table = order_table()
        dev = lax.dynamic_index_in_dim(jnp.asarray(table), me, keepdims=False)
        piece = pack(forget_weight, input_weight, candidate_weight, gain_mix, gain_mlp, input_gate_bias)
        four = jnp.stack([piece] + [send(piece, p, "mixer_z") for p in (FAR, NEAR, BOTH)])
        piece1, piece2 = pack_feed(up_weight, down_weight.T, output_weight)
        four, piece1, piece2, *_ = after_all(four, piece1, piece2, dev, xp, dyp)
        got, far1 = after_all(send(four, FIRST, "mixer_first"), send(piece1, FAR, "feed1_far"))
        eight, two1, piece2 = after_all(jnp.concatenate([four, got]), jnp.stack([piece1, far1]), piece2)
        more, near1, far2 = after_all(
            send(eight, SECOND, "mixer_second"), send(two1, NEAR, "feed1_near"), send(piece2, FAR, "feed2_far")
        )
        more, four1, two2 = after_all(more, jnp.concatenate([two1, near1]), jnp.stack([piece2, far2]))
        got1, near2, core, core_more = after_all(
            send(four1, FIRST, "feed1_first"), send(two2, NEAR, "feed2_near"),
            send(eight, CORE, "mixer_core"), send(more, CORE, "mixer_core_more"),
        )
        eight1, four2 = jnp.concatenate([four1, got1]), jnp.concatenate([two2, near2])
        mixer, eight1, four2 = after_all((eight, more, core, core_more), eight1, four2)
        more1 = send(eight1, SECOND, "feed1_second")
    else:
        order = np.argsort(np.arange(SLOTS) % 2, kind="stable").astype(np.int32)
        dev = jnp.asarray(order)

        def full(v, axis=0, names=AXES):
            return lax.all_gather(v, names, axis=axis, tiled=True)

        gm, gl, gb = full(gain_mix), full(gain_mlp), full(input_gate_bias)
        weights = [full(w) for w in (forget_weight, input_weight, candidate_weight)]
        smalls = [v.reshape(SLOTS, -1) for v in (gm, gl, gb)]
        up = full(full(up_weight, 0, "dp"), 1, "mp")
        down = full(full(down_weight, 1, "dp"), 0, "mp")

        def regroup(w):
            return w.reshape(8, width // 8, 4, width).transpose(0, 2, 1, 3).reshape(SLOTS, width // 8, width)

        both = [
            pack_feed(*v) for v in zip(regroup(up), regroup(down.T), full(output_weight).reshape(SLOTS, -1, width))
        ]

        def quarters(v):
            return tuple(jnp.stack([v[d] for d in order[k * 8 : (k + 1) * 8]]) for k in range(4))

        mixer = quarters(
            jnp.stack([pack(*[w[s * 16 : (s + 1) * 16] for w in weights], *[v[s] for v in smalls]) for s in range(SLOTS)])
        )
        feed1, feed2 = (quarters([v[k] for v in both]) for k in range(2))

    smem = pl.BlockSpec(memory_space=pltpu.SMEM)
    vmem = pl.BlockSpec(memory_space=pltpu.VMEM)
    part = 256

    def band(cols):
        return pl.BlockSpec((part, cols), lambda i: (i, 0))

    def shapes(*items):
        return [jax.ShapeDtypeStruct(shape, kind) for shape, kind in items]

    column = pl.BlockSpec((rows, LANES), lambda i: (0, i))
    block = pl.BlockSpec((None, rows, LANES), lambda i: (i, 0, 0))

    wide = pl.BlockSpec((width, 3 * LANES), lambda i: (0, i))
    hb, other, u1, u2, w3, xn1t, gains = pl.pallas_call(
        mixer_forward,
        grid=(blocks,),
        in_specs=[smem, whole((rows, width))] + [whole(mixer[0].shape)] * 4,
        out_specs=[column] + [block] * 3 + [wide, whole((width, rows)), whole((2, width))],
        out_shape=shapes(((rows, chans), BF), *[((blocks, rows, LANES), BF)] * 3,
                         ((width, 3 * chans), BF), ((width, rows), BF), ((2, width), F32)),
        scratch_shapes=[pltpu.VMEM((3, SLOTS, LANES), F32), pltpu.VMEM((1, chans), F32), pltpu.VMEM((rows, width), BF),
                        pltpu.VMEM((rows, 3 * LANES), F32), pltpu.VMEM((rows, LANES), F32),
                        pltpu.VMEM((rows, LANES), F32)],
        compiler_params=params(16),
        cost_estimate=pl.CostEstimate(flops=6 * rows * width * chans, bytes_accessed=32 << 20, transcendentals=0),
        name="mixer_forward",
    )(dev, xp, *mixer)
    if fast:
        core1 = send(eight1, CORE, "feed1_core")
        more1, four2, gains = after_all(more1, four2, gains)
        feed1 = (eight1, more1, core1, send(more1, CORE, "feed1_core_more"))
        got2 = send(four2, FIRST, "feed2_first")

    size = width // 8

    def pieces(count):
        return [((slots, count, LANES), BF) for slots in (SLOTS // 4, SLOTS // 4, SLOTS // 2)]

    y1, xn2, xn2t, dyt, wo = pl.pallas_call(
        feed_prepare,
        in_specs=[smem] + [vmem] * 8,
        out_specs=[vmem] * 5,
        out_shape=shapes(((rows, width), F32), ((rows, width), BF), ((width, rows), BF), ((width, rows), BF), ((chans, width), BF)),
        compiler_params=params(16),
        cost_estimate=pl.CostEstimate(flops=2 * rows * width * chans, bytes_accessed=10 << 20, transcendentals=0),
        name="feed_prepare",
    )(dev, gains, *feed1, hb, xp, dyp)

    def feed(weights, *before):
        return pl.pallas_call(
            feed_half,
            in_specs=[smem] + [vmem] * (8 + len(before)),
            out_specs=[vmem] * 5,
            out_shape=shapes(((rows, width), F32), ((rows, width), F32), *pieces(2 * size)),
            scratch_shapes=[pltpu.VMEM((width, 2 * LANES), BF)] * 4,
            compiler_params=params(20),
            cost_estimate=pl.CostEstimate(flops=24 * rows * width * width, bytes_accessed=20 << 20, transcendentals=0),
            name="feed_last" if before else "feed_first",
        )(dev, *weights, xn2, xn2t, dyp, dyt, *before)

    if fast:
        got2, y1, xn2, xn2t, dyt, wo = after_all(got2, y1, xn2, xn2t, dyt, wo)
        eight2 = jnp.concatenate([four2, got2])
        more2 = send(eight2, SECOND, "feed2_second")
        core2 = send(eight2, CORE, "feed2_core")
    acc, dxn2, low1, high1, send1 = feed(feed1)
    if fast:
        half, quarter = SLOTS // 4, SLOTS // 8
        more2, acc, dxn2, low1, high1, send1 = after_all(more2, acc, dxn2, low1, high1, send1)
        feed2 = (eight2, more2, core2, send(more2, CORE, "feed2_core_more"))
        got1 = send(send1, CORE, "feed1_back_core")
        high1, acc, dxn2 = after_all(add(high1, got1[half:]), acc, dxn2)
        second1 = send(high1, SECOND, "feed1_back_second")
    acc, dxn2, low2, high2, send2 = feed(feed2, acc, dxn2)
    if fast:
        low1 = add(low1, got1[:half])
        second1, low1, acc, dxn2, low2, high2, send2 = after_all(second1, low1, acc, dxn2, low2, high2, send2)
        low1, high1 = add(low1[:quarter], second1[:quarter]), add(low1[quarter:], second1[quarter:])
        high1, acc, dxn2 = after_all(high1, acc, dxn2)
        first1 = send(high1, FIRST, "feed1_back_first")
        got2 = send(send2, CORE, "feed2_back_core")
    block_out, dmix, low_o, high_o, send_o, gmlp_small = pl.pallas_call(
        feed_finish,
        in_specs=[smem] + [vmem] * 6,
        out_specs=[vmem] * 6,
        out_shape=shapes(((rows, width), BF), ((rows, width), BF), *pieces(size), ((SLOTS, LANES), F32)),
        scratch_shapes=[pltpu.VMEM((chans, width), BF)],
        compiler_params=params(16),
        cost_estimate=pl.CostEstimate(flops=2 * rows * width * chans, bytes_accessed=10 << 20, transcendentals=0),
        name="feed_finish",
    )(dev, gains, hb, dyp, y1, acc, dxn2)
    if fast:
        first1, got2, dmix, low_o, high_o, send_o = after_all(first1, got2, dmix, low_o, high_o, send_o)
        got_o = send(send_o, CORE, "out_back_core")
        low1, high1 = add(low1[:2], first1[:2]), add(low1[2:], first1[2:])
        high2 = jnp.concatenate([add(high2, got2[half:]), add(high_o, got_o[half:])], axis=1)
        high1, high2, dmix = after_all(high1, high2, dmix)
        second2 = send(high2, SECOND, "feed2_back_second")
        near1 = send(high1, NEAR, "feed1_back_near")
    piece = (SLOTS // 2, 3 * blocks * 16 + 16, LANES)
    dk, keep3, send3 = pl.pallas_call(
        mixer_backward,
        grid=(blocks,),
        in_specs=[smem, whole((rows, width)), whole((width, rows)), whole((chans, width)), whole((SLOTS, LANES)),
                  block, block, block],
        out_specs=[pl.BlockSpec((None, rows, 3 * LANES), lambda i: (i, 0, 0))] + [whole(piece)] * 2,
        out_shape=shapes(((blocks, rows, 3 * LANES), BF), (piece, BF), (piece, BF)),
        scratch_shapes=[pltpu.VMEM((1, chans), F32), pltpu.VMEM((blocks, rows, LANES), F32),
                        pltpu.VMEM((width, 3 * LANES), BF)],
        compiler_params=params(16),
        cost_estimate=pl.CostEstimate(flops=8 * rows * width * chans, bytes_accessed=40 << 20, transcendentals=0),
        name="mixer_backward",
    )(dev, dmix, xn1t, wo, gmlp_small, other, u1, u2)

    def input_grad(dk_later):
        return pl.pallas_call(
            input_gradient,
            grid=(rows // part,),
            in_specs=[band(width), band(width), whole((2, width))] + [pl.BlockSpec((blocks, part, 3 * LANES), lambda i: (0, i, 0)), whole((width, 3 * chans))],
            out_specs=band(width),
            out_shape=jax.ShapeDtypeStruct((rows, width), F32),
            compiler_params=params(14),
            cost_estimate=pl.CostEstimate(flops=6 * rows * width * chans, bytes_accessed=24 << 20, transcendentals=0),
            name="input_gradient",
        )(xp, dmix, gains, dk_later, w3)

    def uncut(v):
        v = v[:, : 48 * blocks].reshape(-1, blocks, 3, 16, LANES)
        return [v[:, :, k].transpose(0, 2, 1, 3).reshape(-1, 16, chans) for k in range(3)]

    if fast:
        second2, near1, low1, low2, low_o, dk, send3, keep3 = after_all(second2, near1, low1, low2, low_o, dk, send3, keep3)
        low1, high1 = add(low1[0], near1[0]), add(low1[1], near1[1])
        low2 = jnp.concatenate([add(low2, got2[:half]), add(low_o, got_o[:half])], axis=1)
        low2, high2 = add(low2[:quarter], second2[:quarter]), add(low2[quarter:], second2[quarter:])
        high1, high2 = after_all(high1, high2)
        got = send(send3, CORE, "mixer_back_core")
        first2, far1 = send(high2, FIRST, "feed2_back_first"), send(high1, FAR, "feed1_back_far")
        mlow, mhigh = add(keep3[:half], got[:half]), add(keep3[half:], got[half:])
        first2, far1, mlow, mhigh, dk = after_all(first2, far1, mlow, mhigh, dk)
        first = low1.astype(F32) + far1.astype(F32)
        low2, high2 = add(low2[:2], first2[:2]), add(low2[2:], first2[2:])
        mhigh, high2 = after_all(mhigh, high2)
        got, near2, tokens_grad = after_all(
            send(mhigh, SECOND, "mixer_back_second"), send(high2, NEAR, "feed2_back_near"), input_grad(dk)
        )
        low2, high2 = add(low2[0], near2[0]), add(low2[1], near2[1])
        mlow, mhigh = add(mlow[:quarter], got[:quarter]), add(mlow[quarter:], got[quarter:])
        mlow, mhigh, low2, high2 = after_all(mlow, mhigh, low2, high2)
        got, far2 = after_all(send(mhigh, FIRST, "mixer_back_first"), send(high2, FAR, "feed2_back_far"))
        four = add(mlow, got)
        last = low2.astype(F32) + far2.astype(F32)
        parts = [send(four[k + 1], p, "mixer_back_z") for k, p in enumerate((FAR, NEAR, BOTH))]
        up_grad = jnp.concatenate([first[:size], last[:size]], axis=1)
        down_grad = jnp.concatenate([first[size:], last[size : 2 * size]], axis=1)
        out_grad = jnp.concatenate([last[2 * size : 2 * size + 32], last[2 * size + 32 :]], axis=1)
        down_grad = down_grad.T
        *grads, gmix_grad, gmlp_grad, bias_grad = pl.pallas_call(
            finish_mixer,
            out_shape=shapes(*[((16, chans), F32)] * 3, ((1, shard), F32), ((1, shard), F32), ((1, chans // SLOTS), F32)),
            compiler_params=params(16),
            name="finish",
        )(four[0], *parts, forget_weight, input_weight, candidate_weight, gain_mix[None])
        gmix_grad, gmlp_grad, bias_grad = gmix_grad[0], gmlp_grad[0], bias_grad[0]
    else:
        tokens_grad = input_grad(dk)
        first, last, out_grad, total = (
            jnp.stack([jnp.concatenate(v)[k] for k in np.argsort(order)]).astype(F32)
            for v in ((low1, high1, send1), (low2, high2, send2), (low_o, high_o, send_o), (keep3, send3))
        )

        def summed(v, axis=0, names=AXES):
            return lax.psum_scatter(v, names, scatter_dimension=axis, tiled=True)

        def joined(base):
            w = jnp.concatenate([first[:, base : base + size], last[:, base : base + size]], axis=2)
            return w.reshape(8, 4, size, width).transpose(0, 2, 1, 3).reshape(width, 4 * width)

        up_grad = summed(summed(joined(0), 0, "dp"), 1, "mp")
        down_grad = summed(summed(joined(size).T, 1, "dp"), 0, "mp")
        out_grad = jnp.concatenate([out_grad[:, :32], out_grad[:, 32:]], axis=2)
        out_grad = summed(out_grad.reshape(chans, width))
        grads = [summed(v.reshape(width, chans)) for v in uncut(total)]
        edge = total[:, 48 * blocks]
        gmlp_grad = summed(edge[:, :shard].reshape(-1))
        bias_grad = summed(edge[:, 2 * shard : 2 * shard + chans // SLOTS].reshape(-1))
        dots = sum(
            jnp.sum(w.astype(F32) * g, axis=1) for w, g in zip((forget_weight, input_weight, candidate_weight), grads)
        )
        gmix_grad = dots / gain_mix.astype(F32)

    return (restore(block_out), restore(tokens_grad), gmix_grad, gmlp_grad, grads[0], grads[1], grads[2], bias_grad,
            out_grad, up_grad, down_grad)


def solution(mesh):
    fast = mesh.shape["dp"] == 8 and mesh.shape["mp"] == 4
    every = P(AXES, None)
    in_specs = (every, P(AXES), P(AXES), every, every, every, P(AXES), every, P("dp", "mp"), P("mp", "dp"), every)
    out_specs = (every, every, P(AXES), P(AXES), every, every, every, P(AXES), every, P("dp", "mp"), P("mp", "dp"))
    return jax.shard_map(
        functools.partial(local, fast), mesh=mesh, in_specs=in_specs, out_specs=out_specs, check_vma=False
    )
```

```python
import functools

import jax
import jax.numpy as jnp
import numpy as np
from jax import lax
from jax.experimental import pallas as pl
from jax.experimental.pallas import tpu as pltpu
from jax.sharding import PartitionSpec as P

LEN = 1024
EPSILON = 1e-06
AXES = ("dp", "mp")
SLOTS = 32
CHUNKS = 8
LANES = 256
GROUP = 8
BF = jnp.bfloat16
F32 = jnp.float32
MIB = 1024 * 1024
C0 = 0.7978845608028654
C1 = C0 * 0.044715


def params(mib):
    return pltpu.CompilerParams(vmem_limit_bytes=mib * MIB)


def dot(a, b, dims=((1,), (0,))):
    return lax.dot_general(a, b, (dims, ((), ())), preferred_element_type=F32)


def whole(shape):
    return pl.BlockSpec(shape, lambda *_: (0,) * len(shape), pipeline_mode=pl.Buffered(1))


def aligned(start, size):
    return pl.ds(pl.multiple_of(start, size), size)


def spread(small, piece, width):
    lane = lax.broadcasted_iota(jnp.int32, (LANES, width), 0)
    column = lax.broadcasted_iota(jnp.int32, (LANES, width), 1)
    pick = (lane == column % piece).astype(BF)
    placed = dot(small.astype(BF), pick)
    row = lax.broadcasted_iota(jnp.int32, (SLOTS, width), 0)
    col = lax.broadcasted_iota(jnp.int32, (SLOTS, width), 1)
    return jnp.sum(jnp.where(col // piece == row, placed, 0.0), axis=0, keepdims=True)


def collect(vector, offset, piece):
    width = vector.shape[1]
    row = lax.broadcasted_iota(jnp.int32, (SLOTS, width), 0)
    col = lax.broadcasted_iota(jnp.int32, (SLOTS, width), 1)
    kept = jnp.where(col // piece == row, vector, 0.0).astype(BF)
    column = lax.broadcasted_iota(jnp.int32, (width, LANES), 0)
    lane = lax.broadcasted_iota(jnp.int32, (width, LANES), 1)
    pick = (lane == offset + column % piece).astype(BF)
    return dot(kept, pick)


def pack_mixer(forget_ref, input_ref, cand_ref, gmix_ref, gmlp_ref, bias_ref, out_ref, small):
    blocks = forget_ref.shape[1] // LANES
    for b in range(blocks):
        for w, ref in enumerate((forget_ref, input_ref, cand_ref)):
            at = (b * 3 + w) * 16
            out_ref[at : at + 16, :] = ref[:, b * LANES : (b + 1) * LANES]
    small[...] = jnp.zeros_like(small)
    for k, ref in enumerate((gmix_ref, gmlp_ref, bias_ref)):
        small[k : k + 1, 0 : ref.shape[1]] = ref[...].astype(F32)
    out_ref[48 * blocks :, :] = small[...].astype(BF)


def mixer_prepare(dev_ref, parts, x_ref, xn_ref, xnt_ref, gain_ref, bias_s, small):
    per = SLOTS // 4
    tail = parts[0].shape[1] - 16
    for s in range(SLOTS):
        rows = parts[s // per][s % per, tail : tail + 16, :].astype(F32)
        for k in range(3):
            small[k, pl.ds(dev_ref[s], 1), :] = rows[k : k + 1, :]
    width, chans = x_ref.shape[1], bias_s.shape[1]
    piece = width // SLOTS
    gmix = spread(small[0], piece, width)
    gain_ref[0:1, :] = gmix
    gain_ref[1:2, :] = spread(small[1], piece, width)
    bias_s[...] = spread(small[2], chans // SLOTS, chans)

    def rows(i, _):
        at = aligned(i * 256, 256)
        v = x_ref[at, :].astype(F32)
        scale = lax.rsqrt(jnp.mean(v * v, axis=-1, keepdims=True) + EPSILON)
        xn = ((v * scale) * gmix).astype(BF)
        xn_ref[at, :] = xn
        xnt_ref[:, at] = xn.T
        return 0

    lax.fori_loop(0, x_ref.shape[0] // 256, rows, 0)


def mixer_forward(dev_ref, x_ref, g0, g1, g2, g3, hb_ref, o_ref, u1_ref, u2_ref, w_ref, xnt_ref, gain_ref,
                  small, bias_s, xn_s, k_s, c2_s, f_s):
    step = pl.program_id(0)
    per = SLOTS // 4
    parts = (g0, g1, g2, g3)

    @pl.when(step == 0)
    def _():
        mixer_prepare(dev_ref, parts, x_ref, xn_s, xnt_ref, gain_ref, bias_s, small)

    for s in range(SLOTS):
        d = dev_ref[s]
        for w in range(3):
            src = aligned((step * 3 + w) * 16, 16)
            w_ref[aligned(d * 16, 16), w * LANES : (w + 1) * LANES] = parts[s // per][s % per, src, :]

    bias = bias_s[:, aligned(step * LANES, LANES)]
    kf_c, ki_c, kc_c = (slice(w * LANES, (w + 1) * LANES) for w in range(3))
    zeros = jnp.zeros((CHUNKS, LANES), F32)
    tile = GROUP * CHUNKS
    count = xn_s.shape[0] // tile
    span = 16 * CHUNKS

    def first(i, carry):
        h, prod = carry
        at = slice(i * span, (i + 1) * span)
        k = dot(xn_s[at, :], w_ref[...])
        kf, ki, kc = k[:, kf_c], k[:, ki_c] + bias, k[:, kc_c]
        k_s[at, kc_c] = kc
        low = jnp.minimum(jnp.minimum(kf, ki), 0.0)
        one = jnp.exp(low)
        ef = jnp.exp(low - kf)
        ei = jnp.exp(low - ki)
        a = one + ei
        b = one + ef
        inv = 1.0 / (a + b)
        forget = a * inv
        other = b * inv
        f_s[at, :] = forget
        o_ref[at, :] = other.astype(BF)
        drive = other * kc
        k_s[at, kf_c] = forget * (inv * ef)
        k_s[at, ki_c] = other * (inv * ei)
        c2_s[at, :] = drive
        for k in range(span // CHUNKS):
            part = slice(k * CHUNKS, (k + 1) * CHUNKS)
            h = forget[part] * h + drive[part]
            prod = prod * forget[part]
        return h, prod

    carry = zeros, zeros + 1.0
    for i in range(xn_s.shape[0] // span):
        carry = first(i, carry)
    last, prod = carry
    sub = lax.broadcasted_iota(jnp.int32, (CHUNKS, LANES), 0)
    start = zeros
    for s in range(CHUNKS - 1):
        moved = pltpu.roll(last + prod * start, 1, 0)
        start = jnp.where(sub == s + 1, moved, start)

    def second(i, h):
        at = aligned(i * tile, tile)
        forget = f_s[at, :]
        drive = c2_s[at, :]
        before, after = [], []
        for k in range(GROUP):
            part = slice(k * CHUNKS, (k + 1) * CHUNKS)
            before.append(h)
            h = forget[part] * h + drive[part]
            after.append(h)
        diff = jnp.concatenate(before, axis=0) - k_s[at, kc_c]
        hb_ref[at, :] = jnp.concatenate(after, axis=0).astype(BF)
        u1_ref[at, :] = (k_s[at, kf_c] * diff).astype(BF)
        u2_ref[at, :] = (k_s[at, ki_c] * -diff).astype(BF)
        return h

    lax.fori_loop(0, count, second, start)


def hidden_units(dev_ref, parts, xn_ref, xnt_ref, dy_ref, dyt_ref, targets, add_out, up_s, dn_s, upg_s, dng_s):
    per = SLOTS // 4
    rows = up_s.shape[0] // 8
    for base in (0, SLOTS // 2):
        slots = range(base, base + SLOTS // 2)
        for s in slots:
            d = dev_ref[s]
            at, cols = aligned(d // 4 * rows, rows), aligned(d // 2 % 2 * LANES, LANES)
            up_s[at, cols] = parts[s // per][s % per, 0:rows, :]
            dn_s[at, cols] = parts[s // per][s % per, rows : 2 * rows, :]
        acts, dpres = [], []
        for i in range(xn_ref.shape[0] // 128):
            at = slice(i * 128, (i + 1) * 128)
            pre = dot(xn_ref[at, :], up_s[...])
            dact = dot(dy_ref[at, :], dn_s[...])
            sq = pre * pre
            gate = 0.5 + 0.5 * jnp.tanh(pre * (C0 + C1 * sq))
            value = pre * gate
            acts.append(value.astype(BF))
            slope = gate + value * (1.0 - gate) * (2.0 * C0 + 6.0 * C1 * sq)
            dpres.append((slope * dact).astype(BF))
        act, dpre = jnp.concatenate(acts), jnp.concatenate(dpres)
        upg_s[...] = dot(xnt_ref[...], dpre).astype(BF)
        dng_s[...] = dot(dyt_ref[...], act).astype(BF)
        add_out(base == 0, dot(act, dn_s[...], ((1,), (1,))), dot(dpre, up_s[...], ((1,), (1,))))
        for s in slots:
            d = dev_ref[s]
            at, cols = aligned(d // 4 * rows, rows), aligned(d // 2 % 2 * LANES, LANES)
            ref, k = target(targets, s)
            ref[k, 0:rows, :] = upg_s[at, cols]
            ref[k, rows : 2 * rows, :] = dng_s[at, cols]


def target(targets, s):
    per = SLOTS // 4
    return (targets[0], s) if s < per else (targets[1], s - per) if s < 2 * per else (targets[2], s - 2 * per)


def feed_prepare(dev_ref, gain_ref, g0, g1, g2, g3, hb_ref, x_ref, dy_ref, y1_ref, xn_ref, xnt_ref, dyt_ref, wo_ref):
    parts = (g0, g1, g2, g3)
    per = SLOTS // 4
    tokens, width = x_ref.shape
    feed = width // 4
    gain = gain_ref[1:2, :]
    for s in range(SLOTS):
        for c in range(width // LANES):
            piece = parts[s // per][s % per, feed + c * 32 : feed + (c + 1) * 32, :]
            wo_ref[aligned(dev_ref[s] * 32, 32), c * LANES : (c + 1) * LANES] = piece

    def rows_in(i, _):
        at = aligned(i * 256, 256)
        y1 = x_ref[at, :].astype(F32) + dot(hb_ref[at, :], wo_ref[...])
        y1_ref[at, :] = y1
        scale = lax.rsqrt(jnp.mean(y1 * y1, axis=-1, keepdims=True) + EPSILON)
        xn = ((y1 * scale) * gain).astype(BF)
        xn_ref[at, :] = xn
        xnt_ref[:, at] = xn.T
        return 0

    lax.fori_loop(0, tokens // 256, rows_in, 0)
    dyt_ref[...] = dy_ref[...].T


def feed_half(dev_ref, g0, g1, g2, g3, xn_ref, xnt_ref, dy_ref, dyt_ref, *refs):
    *before, acc_ref, dxn_ref, low_ref, high_ref, send_ref, up_s, dn_s, upg_s, dng_s = refs

    def add_out(first, out, dxn):
        for ref, old, value in zip((acc_ref, dxn_ref), before or (None, None), (out, dxn)):
            if not first:
                old = ref
            ref[...] = value if old is None else old[...] + value

    hidden_units(dev_ref, (g0, g1, g2, g3), xn_ref, xnt_ref, dy_ref, dyt_ref, (low_ref, high_ref, send_ref), add_out,
                 up_s, dn_s, upg_s, dng_s)


def feed_finish(dev_ref, gain_ref, hb_ref, dy_ref, y1_ref, acc_ref, dxn_ref,
                out_ref, dmix_ref, low_ref, high_ref, send_ref, small_ref, wog_s):
    tokens, width = dy_ref.shape
    chans = hb_ref.shape[1]
    gain = gain_ref[1:2, :]
    total = jnp.zeros((1, width), F32)
    for i in range(tokens // 256):
        at = slice(i * 256, (i + 1) * 256)
        y1 = y1_ref[at, :]
        scale = lax.rsqrt(jnp.mean(y1 * y1, axis=-1, keepdims=True) + EPSILON)
        n2 = y1 * scale
        out_ref[at, :] = (y1 + acc_ref[at, :]).astype(BF)
        dxn = dxn_ref[at, :]
        dn = dxn * gain
        dy1 = dy_ref[at, :].astype(F32) + scale * (dn - n2 * jnp.mean(dn * n2, axis=-1, keepdims=True))
        dmix_ref[at, :] = dy1.astype(BF)
        total = total + jnp.sum(dxn * n2, axis=0, keepdims=True)
    small_ref[...] = collect(total, 0, width // SLOTS)

    span = 256
    for b in range(chans // span):
        wog_s[b * span : (b + 1) * span, :] = dot(
            hb_ref[:, b * span : (b + 1) * span], dmix_ref[...], ((0,), (0,))
        ).astype(BF)
    for s in range(SLOTS):
        ref, k = target((low_ref, high_ref, send_ref), s)
        for c in range(width // LANES):
            piece = wog_s[aligned(dev_ref[s] * 32, 32), c * LANES : (c + 1) * LANES]
            ref[k, c * 32 : (c + 1) * 32, :] = piece


def mixer_backward(dev_ref, dmix_ref, xnt_ref, wo_ref, small_ref, o_ref, u1_ref, u2_ref,
                   dk_ref, keep_ref, send_ref, bias_s, dh_s, grad_s):
    step = pl.program_id(0)
    blocks = pl.num_programs(0)
    width, tokens = xnt_ref.shape
    half = SLOTS // 2

    @pl.when(step == 0)
    def _():
        for b in range(dh_s.shape[0]):
            dh_s[b] = dot(dmix_ref[...], wo_ref[b * LANES : (b + 1) * LANES, :], ((1,), (1,)))

    zeros = jnp.zeros((CHUNKS, LANES), F32)
    tile = GROUP * CHUNKS
    count = tokens // tile

    def first(i, carry):
        g, prod, decay = carry
        at = aligned((count - 1 - i) * tile, tile)
        dh = dh_s[step, at, :]
        forget = 1.0 - o_ref[at, :].astype(F32)
        for k in reversed(range(GROUP)):
            part = slice(k * CHUNKS, (k + 1) * CHUNKS)
            g = dh[part] + decay * g
            prod = prod * decay
            decay = forget[part]
        return g, prod, decay

    ones = zeros + 1.0
    head, prod, decay = lax.fori_loop(0, count, first, (zeros, ones, ones))
    sub = lax.broadcasted_iota(jnp.int32, (CHUNKS, LANES), 0)
    start = zeros
    for s in reversed(range(1, CHUNKS)):
        moved = pltpu.roll(decay * (head + prod * start), CHUNKS - 1, 0)
        start = jnp.where(sub == s - 1, moved, start)

    def second(i, carry):
        g, decay, total = carry
        at = aligned((count - 1 - i) * tile, tile)
        dh = dh_s[step, at, :]
        other = o_ref[at, :].astype(F32)
        forget = 1.0 - other
        parts = [None] * GROUP
        for k in reversed(range(GROUP)):
            part = slice(k * CHUNKS, (k + 1) * CHUNKS)
            g = dh[part] + decay * g
            decay = forget[part]
            parts[k] = g
        grad = jnp.concatenate(parts, axis=0)
        dk_ref[at, 0:LANES] = (u1_ref[at, :].astype(F32) * grad).astype(BF)
        di = (u2_ref[at, :].astype(F32) * grad).astype(BF)
        dk_ref[at, LANES : 2 * LANES] = di
        dk_ref[at, 2 * LANES : 3 * LANES] = (other * grad).astype(BF)
        di = di.astype(F32)
        for k in range(GROUP):
            total = total + di[k * CHUNKS : (k + 1) * CHUNKS]
        return g, decay, total

    _, _, total = lax.fori_loop(0, count, second, (start, ones, zeros))
    bias_s[:, aligned(step * LANES, LANES)] = jnp.sum(total, axis=0, keepdims=True)

    grad_s[...] = dot(xnt_ref[...], dk_ref[...]).astype(BF)
    for s in range(SLOTS):
        target = keep_ref if s < half else send_ref
        src = aligned(dev_ref[s] * 16, 16)
        for w in range(3):
            dst = aligned((step * 3 + w) * 16, 16)
            target[s % half, dst, :] = grad_s[src, w * LANES : (w + 1) * LANES]

    @pl.when(step == blocks - 1)
    def _():
        bias = bias_s[...]
        piece = width // SLOTS
        values = small_ref[...] + collect(bias, 2 * piece, bias.shape[1] // SLOTS)
        dh_s[0, 0:SLOTS, :] = values
        row = lax.broadcasted_iota(jnp.int32, (16, LANES), 0)
        tail = keep_ref.shape[1] - 16
        for s in range(SLOTS):
            target = keep_ref if s < half else send_ref
            values = dh_s[0, pl.ds(dev_ref[s], 1), :]
            target[s % half, tail : tail + 16, :] = jnp.where(row == 0, values, 0.0).astype(BF)


def input_gradient(x_ref, dmix_ref, gain_ref, dk_ref, w_ref, out_ref):
    size = dk_ref.shape[2]
    dxn = dot(dk_ref[0], w_ref[:, :size], ((1,), (1,)))
    for b in range(1, dk_ref.shape[0]):
        dxn = dxn + dot(dk_ref[b], w_ref[:, b * size : (b + 1) * size], ((1,), (1,)))
    v = x_ref[...].astype(F32)
    scale = lax.rsqrt(jnp.mean(v * v, axis=-1, keepdims=True) + EPSILON)
    n1 = v * scale
    dn = dxn * gain_ref[0:1, :]
    out_ref[...] = dmix_ref[...].astype(F32) + scale * (dn - n1 * jnp.mean(dn * n1, axis=-1, keepdims=True))


def finish_mixer(own_ref, p0, p1, p2, forget_ref, input_ref, cand_ref, gain_ref,
                 fg_ref, ig_ref, cg_ref, gmix_ref, gmlp_ref, bias_ref):
    total = own_ref[...].astype(F32)
    for ref in (p0, p1, p2):
        total = total + ref[...].astype(F32)
    chans = fg_ref.shape[1]
    dots = jnp.zeros((16, 1), F32)
    for b in range(chans // LANES):
        cols = slice(b * LANES, (b + 1) * LANES)
        for w, (ref, weight) in enumerate(((fg_ref, forget_ref), (ig_ref, input_ref), (cg_ref, cand_ref))):
            grad = total[(b * 3 + w) * 16 : (b * 3 + w + 1) * 16]
            ref[:, cols] = grad
            dots = dots + jnp.sum(grad * weight[:, cols].astype(F32), axis=1, keepdims=True)
    row = jnp.broadcast_to(dots, (16, 128)).T[0:1, :]
    gmix_ref[...] = row / gain_ref[...].astype(F32)
    edge = total[chans // LANES * 48 : chans // LANES * 48 + 1]
    piece = gmlp_ref.shape[1]
    gmlp_ref[...] = edge[:, :piece]
    bias_ref[...] = edge[:, 2 * piece : 2 * piece + bias_ref.shape[1]]


def order_table():
    table = np.zeros((SLOTS, SLOTS), np.int32)
    for me in range(SLOTS):
        core, y, x, z = me & 1, me >> 1 & 1, me >> 2 & 1, me >> 3
        for slot in range(SLOTS):
            oc, second, first, oz = slot >> 4, slot >> 3 & 1, slot >> 2 & 1, (slot & 1) << 1 | slot >> 1 & 1
            c2 = core ^ oc
            x2 = x ^ (first if c2 == 0 else second)
            y2 = y ^ (second if c2 == 0 else first)
            table[me, slot] = ((z ^ oz) * 2 + x2) * 4 + y2 * 2 + c2
    return table


def flip(x0, y0, z0, c0, x1, y1, z1, c1):
    pairs = []
    for me in range(SLOTS):
        x, y, z, c = (x1, y1, z1, c1) if me & 1 else (x0, y0, z0, c0)
        pairs.append((me, me ^ (z << 3 | x << 2 | y << 1 | c)))
    return pairs


FAR, NEAR, BOTH = [flip(0, 0, k, 0, 0, 0, k, 0) for k in (2, 1, 3)]
FIRST = flip(1, 0, 0, 0, 0, 1, 0, 0)
SECOND = flip(0, 1, 0, 0, 1, 0, 0, 0)
CORE = flip(0, 0, 0, 1, 0, 0, 0, 1)


def send(value, pairs, name):
    with jax.named_scope(name):
        return lax.ppermute(value, AXES, pairs)


def after(value, *others):
    return lax.optimization_barrier((value,) + others)[0]


def after_all(*values):
    return lax.optimization_barrier(values)


def add(a, b):
    return (a.astype(F32) + b.astype(F32)).astype(BF)


def fold(low, high, pairs, name):
    got = send(high, pairs, name)
    half = low.shape[0] // 2
    return add(low[:half], got[:half]), add(low[half:], got[half:])


def pack(forget_weight, input_weight, candidate_weight, gain_mix, gain_mlp, input_gate_bias):
    rows = 3 * forget_weight.shape[1] // LANES * 16 + 16
    return pl.pallas_call(
        pack_mixer,
        out_shape=jax.ShapeDtypeStruct((rows, LANES), BF),
        scratch_shapes=[pltpu.VMEM((16, LANES), F32)],
        compiler_params=params(60),
        name="pack",
    )(forget_weight, input_weight, candidate_weight, gain_mix[None], gain_mlp[None], input_gate_bias[None])


def local(fast, tokens, gain_mix, gain_mlp, forget_weight, input_weight, candidate_weight, input_gate_bias,
          output_weight, up_weight, down_weight, cotangent):
    rows, width = tokens.shape
    chans = forget_weight.shape[1]
    blocks = chans // LANES
    shard = width // SLOTS

    def permute(v):
        return v.reshape(CHUNKS, rows // CHUNKS, width).transpose(1, 0, 2).reshape(rows, width)

    def restore(v):
        return v.reshape(rows // CHUNKS, CHUNKS, width).transpose(1, 0, 2).reshape(rows, width)

    xp = permute(tokens)
    dyp = permute(cotangent)
    def pack_feed(up, down, out):
        pieces = [v[:, c : c + LANES] for v in (up, down, out) for c in (0, LANES)]
        return jnp.concatenate([pieces[0], pieces[2], pieces[4], pieces[5]]), jnp.concatenate([pieces[1], pieces[3]])

    if fast:
        me = lax.axis_index(AXES)
        table = order_table()
        dev = lax.dynamic_index_in_dim(jnp.asarray(table), me, keepdims=False)
        piece = pack(forget_weight, input_weight, candidate_weight, gain_mix, gain_mlp, input_gate_bias)
        four = jnp.stack([piece] + [send(piece, p, "mixer_z") for p in (FAR, NEAR, BOTH)])
        piece1, piece2 = pack_feed(up_weight, down_weight.T, output_weight)
        four, piece1, piece2, *_ = after_all(four, piece1, piece2, dev, xp, dyp)
        got, far1 = after_all(send(four, FIRST, "mixer_first"), send(piece1, FAR, "feed1_far"))
        eight, two1, piece2 = after_all(jnp.concatenate([four, got]), jnp.stack([piece1, far1]), piece2)
        more, near1, far2 = after_all(
            send(eight, SECOND, "mixer_second"), send(two1, NEAR, "feed1_near"), send(piece2, FAR, "feed2_far")
        )
        more, four1, two2 = after_all(more, jnp.concatenate([two1, near1]), jnp.stack([piece2, far2]))
        got1, near2, core, core_more = after_all(
            send(four1, FIRST, "feed1_first"), send(two2, NEAR, "feed2_near"),
            send(eight, CORE, "mixer_core"), send(more, CORE, "mixer_core_more"),
        )
        eight1, four2 = jnp.concatenate([four1, got1]), jnp.concatenate([two2, near2])
        mixer, eight1, four2 = after_all((eight, more, core, core_more), eight1, four2)
        more1 = send(eight1, SECOND, "feed1_second")
    else:
        order = np.argsort(np.arange(SLOTS) % 2, kind="stable").astype(np.int32)
        dev = jnp.asarray(order)

        def full(v, axis=0, names=AXES):
            return lax.all_gather(v, names, axis=axis, tiled=True)

        gm, gl, gb = full(gain_mix), full(gain_mlp), full(input_gate_bias)
        weights = [full(w) for w in (forget_weight, input_weight, candidate_weight)]
        smalls = [v.reshape(SLOTS, -1) for v in (gm, gl, gb)]
        up = full(full(up_weight, 0, "dp"), 1, "mp")
        down = full(full(down_weight, 1, "dp"), 0, "mp")

        def regroup(w):
            return w.reshape(8, width // 8, 4, width).transpose(0, 2, 1, 3).reshape(SLOTS, width // 8, width)

        both = [
            pack_feed(*v) for v in zip(regroup(up), regroup(down.T), full(output_weight).reshape(SLOTS, -1, width))
        ]

        def quarters(v):
            return tuple(jnp.stack([v[d] for d in order[k * 8 : (k + 1) * 8]]) for k in range(4))

        mixer = quarters(
            jnp.stack([pack(*[w[s * 16 : (s + 1) * 16] for w in weights], *[v[s] for v in smalls]) for s in range(SLOTS)])
        )
        feed1, feed2 = (quarters([v[k] for v in both]) for k in range(2))

    smem = pl.BlockSpec(memory_space=pltpu.SMEM)
    vmem = pl.BlockSpec(memory_space=pltpu.VMEM)
    part = 256

    def band(cols):
        return pl.BlockSpec((part, cols), lambda i: (i, 0))

    def shapes(*items):
        return [jax.ShapeDtypeStruct(shape, kind) for shape, kind in items]

    column = pl.BlockSpec((rows, LANES), lambda i: (0, i))
    block = pl.BlockSpec((None, rows, LANES), lambda i: (i, 0, 0))

    wide = pl.BlockSpec((width, 3 * LANES), lambda i: (0, i))
    hb, other, u1, u2, w3, xn1t, gains = pl.pallas_call(
        mixer_forward,
        grid=(blocks,),
        in_specs=[smem, whole((rows, width))] + [whole(mixer[0].shape)] * 4,
        out_specs=[column] + [block] * 3 + [wide, whole((width, rows)), whole((2, width))],
        out_shape=shapes(((rows, chans), BF), *[((blocks, rows, LANES), BF)] * 3,
                         ((width, 3 * chans), BF), ((width, rows), BF), ((2, width), F32)),
        scratch_shapes=[pltpu.VMEM((3, SLOTS, LANES), F32), pltpu.VMEM((1, chans), F32), pltpu.VMEM((rows, width), BF),
                        pltpu.VMEM((rows, 3 * LANES), F32), pltpu.VMEM((rows, LANES), F32),
                        pltpu.VMEM((rows, LANES), F32)],
        compiler_params=params(16),
        cost_estimate=pl.CostEstimate(flops=6 * rows * width * chans, bytes_accessed=32 << 20, transcendentals=0),
        name="mixer_forward",
    )(dev, xp, *mixer)
    if fast:
        core1 = send(eight1, CORE, "feed1_core")
        more1, four2, gains = after_all(more1, four2, gains)
        feed1 = (eight1, more1, core1, send(more1, CORE, "feed1_core_more"))
        got2 = send(four2, FIRST, "feed2_first")

    size = width // 8

    def pieces(count):
        return [((slots, count, LANES), BF) for slots in (SLOTS // 4, SLOTS // 4, SLOTS // 2)]

    y1, xn2, xn2t, dyt, wo = pl.pallas_call(
        feed_prepare,
        in_specs=[smem] + [vmem] * 8,
        out_specs=[vmem] * 5,
        out_shape=shapes(((rows, width), F32), ((rows, width), BF), ((width, rows), BF), ((width, rows), BF), ((chans, width), BF)),
        compiler_params=params(16),
        cost_estimate=pl.CostEstimate(flops=2 * rows * width * chans, bytes_accessed=10 << 20, transcendentals=0),
        name="feed_prepare",
    )(dev, gains, *feed1, hb, xp, dyp)

    def feed(weights, *before):
        return pl.pallas_call(
            feed_half,
            in_specs=[smem] + [vmem] * (8 + len(before)),
            out_specs=[vmem] * 5,
            out_shape=shapes(((rows, width), F32), ((rows, width), F32), *pieces(2 * size)),
            scratch_shapes=[pltpu.VMEM((width, 2 * LANES), BF)] * 4,
            compiler_params=params(20),
            cost_estimate=pl.CostEstimate(flops=24 * rows * width * width, bytes_accessed=20 << 20, transcendentals=0),
            name="feed_last" if before else "feed_first",
        )(dev, *weights, xn2, xn2t, dyp, dyt, *before)

    if fast:
        got2, y1, xn2, xn2t, dyt, wo = after_all(got2, y1, xn2, xn2t, dyt, wo)
        eight2 = jnp.concatenate([four2, got2])
        more2 = send(eight2, SECOND, "feed2_second")
        core2 = send(eight2, CORE, "feed2_core")
    acc, dxn2, low1, high1, send1 = feed(feed1)
    if fast:
        half, quarter = SLOTS // 4, SLOTS // 8
        more2, acc, dxn2, low1, high1, send1 = after_all(more2, acc, dxn2, low1, high1, send1)
        feed2 = (eight2, more2, core2, send(more2, CORE, "feed2_core_more"))
        got1 = send(send1, CORE, "feed1_back_core")
        high1, acc, dxn2 = after_all(add(high1, got1[half:]), acc, dxn2)
        second1 = send(high1, SECOND, "feed1_back_second")
    acc, dxn2, low2, high2, send2 = feed(feed2, acc, dxn2)
    if fast:
        low1 = add(low1, got1[:half])
        second1, low1, acc, dxn2, low2, high2, send2 = after_all(second1, low1, acc, dxn2, low2, high2, send2)
        low1, high1 = add(low1[:quarter], second1[:quarter]), add(low1[quarter:], second1[quarter:])
        high1, acc, dxn2 = after_all(high1, acc, dxn2)
        first1 = send(high1, FIRST, "feed1_back_first")
        got2 = send(send2, CORE, "feed2_back_core")
    block_out, dmix, low_o, high_o, send_o, gmlp_small = pl.pallas_call(
        feed_finish,
        in_specs=[smem] + [vmem] * 6,
        out_specs=[vmem] * 6,
        out_shape=shapes(((rows, width), BF), ((rows, width), BF), *pieces(size), ((SLOTS, LANES), F32)),
        scratch_shapes=[pltpu.VMEM((chans, width), BF)],
        compiler_params=params(16),
        cost_estimate=pl.CostEstimate(flops=2 * rows * width * chans, bytes_accessed=10 << 20, transcendentals=0),
        name="feed_finish",
    )(dev, gains, hb, dyp, y1, acc, dxn2)
    if fast:
        first1, got2, dmix, low_o, high_o, send_o = after_all(first1, got2, dmix, low_o, high_o, send_o)
        got_o = send(send_o, CORE, "out_back_core")
        low1, high1 = add(low1[:2], first1[:2]), add(low1[2:], first1[2:])
        high2 = jnp.concatenate([add(high2, got2[half:]), add(high_o, got_o[half:])], axis=1)
        high1, high2, dmix = after_all(high1, high2, dmix)
        second2 = send(high2, SECOND, "feed2_back_second")
        near1 = send(high1, NEAR, "feed1_back_near")
    piece = (SLOTS // 2, 3 * blocks * 16 + 16, LANES)
    dk, keep3, send3 = pl.pallas_call(
        mixer_backward,
        grid=(blocks,),
        in_specs=[smem, whole((rows, width)), whole((width, rows)), whole((chans, width)), whole((SLOTS, LANES)),
                  block, block, block],
        out_specs=[pl.BlockSpec((None, rows, 3 * LANES), lambda i: (i, 0, 0))] + [whole(piece)] * 2,
        out_shape=shapes(((blocks, rows, 3 * LANES), BF), (piece, BF), (piece, BF)),
        scratch_shapes=[pltpu.VMEM((1, chans), F32), pltpu.VMEM((blocks, rows, LANES), F32),
                        pltpu.VMEM((width, 3 * LANES), BF)],
        compiler_params=params(16),
        cost_estimate=pl.CostEstimate(flops=8 * rows * width * chans, bytes_accessed=40 << 20, transcendentals=0),
        name="mixer_backward",
    )(dev, dmix, xn1t, wo, gmlp_small, other, u1, u2)

    def input_grad(dk_later):
        return pl.pallas_call(
            input_gradient,
            grid=(rows // part,),
            in_specs=[band(width), band(width), whole((2, width))] + [pl.BlockSpec((blocks, part, 3 * LANES), lambda i: (0, i, 0)), whole((width, 3 * chans))],
            out_specs=band(width),
            out_shape=jax.ShapeDtypeStruct((rows, width), F32),
            compiler_params=params(14),
            cost_estimate=pl.CostEstimate(flops=6 * rows * width * chans, bytes_accessed=24 << 20, transcendentals=0),
            name="input_gradient",
        )(xp, dmix, gains, dk_later, w3)

    def uncut(v):
        v = v[:, : 48 * blocks].reshape(-1, blocks, 3, 16, LANES)
        return [v[:, :, k].transpose(0, 2, 1, 3).reshape(-1, 16, chans) for k in range(3)]

    if fast:
        second2, near1, low1, low2, low_o, dk, send3, keep3 = after_all(second2, near1, low1, low2, low_o, dk, send3, keep3)
        low1, high1 = add(low1[0], near1[0]), add(low1[1], near1[1])
        low2 = jnp.concatenate([add(low2, got2[:half]), add(low_o, got_o[:half])], axis=1)
        low2, high2 = add(low2[:quarter], second2[:quarter]), add(low2[quarter:], second2[quarter:])
        high1, high2 = after_all(high1, high2)
        got = send(send3, CORE, "mixer_back_core")
        first2, far1 = send(high2, FIRST, "feed2_back_first"), send(high1, FAR, "feed1_back_far")
        mlow, mhigh = add(keep3[:half], got[:half]), add(keep3[half:], got[half:])
        first2, far1, mlow, mhigh, dk = after_all(first2, far1, mlow, mhigh, dk)
        first = low1.astype(F32) + far1.astype(F32)
        low2, high2 = add(low2[:2], first2[:2]), add(low2[2:], first2[2:])
        mhigh, high2 = after_all(mhigh, high2)
        got, near2, tokens_grad = after_all(
            send(mhigh, SECOND, "mixer_back_second"), send(high2, NEAR, "feed2_back_near"), input_grad(dk)
        )
        low2, high2 = add(low2[0], near2[0]), add(low2[1], near2[1])
        mlow, mhigh = add(mlow[:quarter], got[:quarter]), add(mlow[quarter:], got[quarter:])
        mlow, mhigh, low2, high2 = after_all(mlow, mhigh, low2, high2)
        got, far2 = after_all(send(mhigh, FIRST, "mixer_back_first"), send(high2, FAR, "feed2_back_far"))
        four = add(mlow, got)
        last = low2.astype(F32) + far2.astype(F32)
        parts = [send(four[k + 1], p, "mixer_back_z") for k, p in enumerate((FAR, NEAR, BOTH))]
        up_grad = jnp.concatenate([first[:size], last[:size]], axis=1)
        down_grad = jnp.concatenate([first[size:], last[size : 2 * size]], axis=1)
        out_grad = jnp.concatenate([last[2 * size : 2 * size + 32], last[2 * size + 32 :]], axis=1)
        down_grad = down_grad.T
        *grads, gmix_grad, gmlp_grad, bias_grad = pl.pallas_call(
            finish_mixer,
            out_shape=shapes(*[((16, chans), F32)] * 3, ((1, shard), F32), ((1, shard), F32), ((1, chans // SLOTS), F32)),
            compiler_params=params(16),
            name="finish",
        )(four[0], *parts, forget_weight, input_weight, candidate_weight, gain_mix[None])
        gmix_grad, gmlp_grad, bias_grad = gmix_grad[0], gmlp_grad[0], bias_grad[0]
    else:
        tokens_grad = input_grad(dk)
        first, last, out_grad, total = (
            jnp.stack([jnp.concatenate(v)[k] for k in np.argsort(order)]).astype(F32)
            for v in ((low1, high1, send1), (low2, high2, send2), (low_o, high_o, send_o), (keep3, send3))
        )

        def summed(v, axis=0, names=AXES):
            return lax.psum_scatter(v, names, scatter_dimension=axis, tiled=True)

        def joined(base):
            w = jnp.concatenate([first[:, base : base + size], last[:, base : base + size]], axis=2)
            return w.reshape(8, 4, size, width).transpose(0, 2, 1, 3).reshape(width, 4 * width)

        up_grad = summed(summed(joined(0), 0, "dp"), 1, "mp")
        down_grad = summed(summed(joined(size).T, 1, "dp"), 0, "mp")
        out_grad = jnp.concatenate([out_grad[:, :32], out_grad[:, 32:]], axis=2)
        out_grad = summed(out_grad.reshape(chans, width))
        grads = [summed(v.reshape(width, chans)) for v in uncut(total)]
        edge = total[:, 48 * blocks]
        gmlp_grad = summed(edge[:, :shard].reshape(-1))
        bias_grad = summed(edge[:, 2 * shard : 2 * shard + chans // SLOTS].reshape(-1))
        dots = sum(
            jnp.sum(w.astype(F32) * g, axis=1) for w, g in zip((forget_weight, input_weight, candidate_weight), grads)
        )
        gmix_grad = dots / gain_mix.astype(F32)

    return (restore(block_out), restore(tokens_grad), gmix_grad, gmlp_grad, grads[0], grads[1], grads[2], bias_grad,
            out_grad, up_grad, down_grad)


def solution(mesh):
    fast = mesh.shape["dp"] == 8 and mesh.shape["mp"] == 4
    every = P(AXES, None)
    in_specs = (every, P(AXES), P(AXES), every, every, every, P(AXES), every, P("dp", "mp"), P("mp", "dp"), every)
    out_specs = (every, every, P(AXES), P(AXES), every, every, every, P(AXES), every, P("dp", "mp"), P("mp", "dp"))
    return jax.shard_map(
        functools.partial(local, fast), mesh=mesh, in_specs=in_specs, out_specs=out_specs, check_vma=False
    )
```

```python
import functools

import jax
import jax.numpy as jnp
import numpy as np
from jax import lax
from jax.experimental import pallas as pl
from jax.experimental.pallas import tpu as pltpu
from jax.sharding import PartitionSpec as P

LEN = 1024
EPSILON = 1e-06
AXES = ("dp", "mp")
SLOTS = 32
CHUNKS = 8
LANES = 256
GROUP = 8
BF = jnp.bfloat16
F32 = jnp.float32
MIB = 1024 * 1024
C0 = 0.7978845608028654
C1 = C0 * 0.044715


def params(mib):
    return pltpu.CompilerParams(vmem_limit_bytes=mib * MIB)


def dot(a, b, dims=((1,), (0,))):
    return lax.dot_general(a, b, (dims, ((), ())), preferred_element_type=F32)


def whole(shape):
    return pl.BlockSpec(shape, lambda *_: (0,) * len(shape), pipeline_mode=pl.Buffered(1))


def aligned(start, size):
    return pl.ds(pl.multiple_of(start, size), size)


def spread(small, piece, width):
    lane = lax.broadcasted_iota(jnp.int32, (LANES, width), 0)
    column = lax.broadcasted_iota(jnp.int32, (LANES, width), 1)
    pick = (lane == column % piece).astype(BF)
    placed = dot(small.astype(BF), pick)
    row = lax.broadcasted_iota(jnp.int32, (SLOTS, width), 0)
    col = lax.broadcasted_iota(jnp.int32, (SLOTS, width), 1)
    return jnp.sum(jnp.where(col // piece == row, placed, 0.0), axis=0, keepdims=True)


def collect(vector, offset, piece):
    width = vector.shape[1]
    row = lax.broadcasted_iota(jnp.int32, (SLOTS, width), 0)
    col = lax.broadcasted_iota(jnp.int32, (SLOTS, width), 1)
    kept = jnp.where(col // piece == row, vector, 0.0).astype(BF)
    column = lax.broadcasted_iota(jnp.int32, (width, LANES), 0)
    lane = lax.broadcasted_iota(jnp.int32, (width, LANES), 1)
    pick = (lane == offset + column % piece).astype(BF)
    return dot(kept, pick)


def pack_mixer(forget_ref, input_ref, cand_ref, gmix_ref, gmlp_ref, bias_ref, out_ref, small):
    blocks = forget_ref.shape[1] // LANES
    for b in range(blocks):
        for w, ref in enumerate((forget_ref, input_ref, cand_ref)):
            at = (b * 3 + w) * 16
            out_ref[at : at + 16, :] = ref[:, b * LANES : (b + 1) * LANES]
    small[...] = jnp.zeros_like(small)
    for k, ref in enumerate((gmix_ref, gmlp_ref, bias_ref)):
        small[k : k + 1, 0 : ref.shape[1]] = ref[...].astype(F32)
    out_ref[48 * blocks :, :] = small[...].astype(BF)


def mixer_prepare(dev_ref, parts, x_ref, xn_ref, xnt_ref, gain_ref, bias_s, small):
    per = SLOTS // 4
    tail = parts[0].shape[1] - 16
    for s in range(SLOTS):
        rows = parts[s // per][s % per, tail : tail + 16, :].astype(F32)
        for k in range(3):
            small[k, pl.ds(dev_ref[s], 1), :] = rows[k : k + 1, :]
    width, chans = x_ref.shape[1], bias_s.shape[1]
    piece = width // SLOTS
    gmix = spread(small[0], piece, width)
    gain_ref[0:1, :] = gmix
    gain_ref[1:2, :] = spread(small[1], piece, width)
    bias_s[...] = spread(small[2], chans // SLOTS, chans)

    def rows(i, _):
        at = aligned(i * 256, 256)
        v = x_ref[at, :].astype(F32)
        scale = lax.rsqrt(jnp.mean(v * v, axis=-1, keepdims=True) + EPSILON)
        xn = ((v * scale) * gmix).astype(BF)
        xn_ref[at, :] = xn
        xnt_ref[:, at] = xn.T
        return 0

    lax.fori_loop(0, x_ref.shape[0] // 256, rows, 0)


def mixer_forward(dev_ref, x_ref, g0, g1, g2, g3, hb_ref, o_ref, u1_ref, u2_ref, w_ref, xnt_ref, gain_ref,
                  small, bias_s, xn_s, k_s, c2_s, f_s):
    step = pl.program_id(0)
    per = SLOTS // 4
    parts = (g0, g1, g2, g3)

    @pl.when(step == 0)
    def _():
        mixer_prepare(dev_ref, parts, x_ref, xn_s, xnt_ref, gain_ref, bias_s, small)

    for s in range(SLOTS):
        d = dev_ref[s]
        for w in range(3):
            src = aligned((step * 3 + w) * 16, 16)
            w_ref[aligned(d * 16, 16), w * LANES : (w + 1) * LANES] = parts[s // per][s % per, src, :]

    bias = bias_s[:, aligned(step * LANES, LANES)]
    kf_c, ki_c, kc_c = (slice(w * LANES, (w + 1) * LANES) for w in range(3))
    zeros = jnp.zeros((CHUNKS, LANES), F32)
    tile = GROUP * CHUNKS
    count = xn_s.shape[0] // tile
    span = 16 * CHUNKS

    def first(i, carry):
        h, prod = carry
        at = slice(i * span, (i + 1) * span)
        k = dot(xn_s[at, :], w_ref[...])
        kf, ki, kc = k[:, kf_c], k[:, ki_c] + bias, k[:, kc_c]
        k_s[at, kc_c] = kc
        low = jnp.minimum(jnp.minimum(kf, ki), 0.0)
        one = jnp.exp(low)
        ef = jnp.exp(low - kf)
        ei = jnp.exp(low - ki)
        a = one + ei
        b = one + ef
        inv = 1.0 / (a + b)
        forget = a * inv
        other = b * inv
        f_s[at, :] = forget
        o_ref[at, :] = other.astype(BF)
        drive = other * kc
        k_s[at, kf_c] = forget * (inv * ef)
        k_s[at, ki_c] = other * (inv * ei)
        c2_s[at, :] = drive
        for k in range(span // CHUNKS):
            part = slice(k * CHUNKS, (k + 1) * CHUNKS)
            h = forget[part] * h + drive[part]
            prod = prod * forget[part]
        return h, prod

    carry = zeros, zeros + 1.0
    for i in range(xn_s.shape[0] // span):
        carry = first(i, carry)
    last, prod = carry
    sub = lax.broadcasted_iota(jnp.int32, (CHUNKS, LANES), 0)
    start = zeros
    for s in range(CHUNKS - 1):
        moved = pltpu.roll(last + prod * start, 1, 0)
        start = jnp.where(sub == s + 1, moved, start)

    def second(i, h):
        at = aligned(i * tile, tile)
        forget = f_s[at, :]
        drive = c2_s[at, :]
        before, after = [], []
        for k in range(GROUP):
            part = slice(k * CHUNKS, (k + 1) * CHUNKS)
            before.append(h)
            h = forget[part] * h + drive[part]
            after.append(h)
        diff = jnp.concatenate(before, axis=0) - k_s[at, kc_c]
        hb_ref[at, :] = jnp.concatenate(after, axis=0).astype(BF)
        u1_ref[at, :] = (k_s[at, kf_c] * diff).astype(BF)
        u2_ref[at, :] = (k_s[at, ki_c] * -diff).astype(BF)
        return h

    lax.fori_loop(0, count, second, start)


def hidden_units(dev_ref, parts, xn_ref, xnt_ref, dy_ref, dyt_ref, targets, add_out, up_s, dn_s, upg_s, dng_s):
    per = SLOTS // 4
    rows = up_s.shape[0] // 8
    for base in (0, SLOTS // 2):
        slots = range(base, base + SLOTS // 2)
        for s in slots:
            d = dev_ref[s]
            at, cols = aligned(d // 4 * rows, rows), aligned(d // 2 % 2 * LANES, LANES)
            up_s[at, cols] = parts[s // per][s % per, 0:rows, :]
            dn_s[at, cols] = parts[s // per][s % per, rows : 2 * rows, :]
        acts, dpres = [], []
        for i in range(xn_ref.shape[0] // 128):
            at = slice(i * 128, (i + 1) * 128)
            pre = dot(xn_ref[at, :], up_s[...])
            dact = dot(dy_ref[at, :], dn_s[...])
            sq = pre * pre
            gate = 0.5 + 0.5 * jnp.tanh(pre * (C0 + C1 * sq))
            value = pre * gate
            acts.append(value.astype(BF))
            slope = gate + value * (1.0 - gate) * (2.0 * C0 + 6.0 * C1 * sq)
            dpres.append((slope * dact).astype(BF))
        act, dpre = jnp.concatenate(acts), jnp.concatenate(dpres)
        upg_s[...] = dot(xnt_ref[...], dpre).astype(BF)
        dng_s[...] = dot(dyt_ref[...], act).astype(BF)
        add_out(base == 0, dot(act, dn_s[...], ((1,), (1,))), dot(dpre, up_s[...], ((1,), (1,))))
        for s in slots:
            d = dev_ref[s]
            at, cols = aligned(d // 4 * rows, rows), aligned(d // 2 % 2 * LANES, LANES)
            ref, k = target(targets, s)
            ref[k, 0:rows, :] = upg_s[at, cols]
            ref[k, rows : 2 * rows, :] = dng_s[at, cols]


def target(targets, s):
    per = SLOTS // 4
    return (targets[0], s) if s < per else (targets[1], s - per) if s < 2 * per else (targets[2], s - 2 * per)


def feed_prepare(dev_ref, gain_ref, g0, g1, g2, g3, hb_ref, x_ref, dy_ref, y1_ref, xn_ref, xnt_ref, dyt_ref, wo_ref):
    parts = (g0, g1, g2, g3)
    per = SLOTS // 4
    tokens, width = x_ref.shape
    feed = width // 4
    gain = gain_ref[1:2, :]
    for s in range(SLOTS):
        for c in range(width // LANES):
            piece = parts[s // per][s % per, feed + c * 32 : feed + (c + 1) * 32, :]
            wo_ref[aligned(dev_ref[s] * 32, 32), c * LANES : (c + 1) * LANES] = piece

    for i in range(tokens // 256):
        at = slice(i * 256, (i + 1) * 256)
        y1 = x_ref[at, :].astype(F32) + dot(hb_ref[at, :], wo_ref[...])
        y1_ref[at, :] = y1
        scale = lax.rsqrt(jnp.mean(y1 * y1, axis=-1, keepdims=True) + EPSILON)
        xn = ((y1 * scale) * gain).astype(BF)
        xn_ref[at, :] = xn
        xnt_ref[:, at] = xn.T
    dyt_ref[...] = dy_ref[...].T


def feed_half(dev_ref, g0, g1, g2, g3, xn_ref, xnt_ref, dy_ref, dyt_ref, *refs):
    *before, acc_ref, dxn_ref, low_ref, high_ref, send_ref, up_s, dn_s, upg_s, dng_s = refs

    def add_out(first, out, dxn):
        for ref, old, value in zip((acc_ref, dxn_ref), before or (None, None), (out, dxn)):
            if not first:
                old = ref
            ref[...] = value if old is None else old[...] + value

    hidden_units(dev_ref, (g0, g1, g2, g3), xn_ref, xnt_ref, dy_ref, dyt_ref, (low_ref, high_ref, send_ref), add_out,
                 up_s, dn_s, upg_s, dng_s)


def feed_finish(dev_ref, gain_ref, hb_ref, dy_ref, y1_ref, acc_ref, dxn_ref,
                out_ref, dmix_ref, low_ref, high_ref, send_ref, small_ref, wog_s):
    tokens, width = dy_ref.shape
    chans = hb_ref.shape[1]
    gain = gain_ref[1:2, :]
    total = jnp.zeros((1, width), F32)
    for i in range(tokens // 256):
        at = slice(i * 256, (i + 1) * 256)
        y1 = y1_ref[at, :]
        scale = lax.rsqrt(jnp.mean(y1 * y1, axis=-1, keepdims=True) + EPSILON)
        n2 = y1 * scale
        out_ref[at, :] = (y1 + acc_ref[at, :]).astype(BF)
        dxn = dxn_ref[at, :]
        dn = dxn * gain
        dy1 = dy_ref[at, :].astype(F32) + scale * (dn - n2 * jnp.mean(dn * n2, axis=-1, keepdims=True))
        dmix_ref[at, :] = dy1.astype(BF)
        total = total + jnp.sum(dxn * n2, axis=0, keepdims=True)
    small_ref[...] = collect(total, 0, width // SLOTS)

    span = 256
    for b in range(chans // span):
        wog_s[b * span : (b + 1) * span, :] = dot(
            hb_ref[:, b * span : (b + 1) * span], dmix_ref[...], ((0,), (0,))
        ).astype(BF)
    for s in range(SLOTS):
        ref, k = target((low_ref, high_ref, send_ref), s)
        for c in range(width // LANES):
            piece = wog_s[aligned(dev_ref[s] * 32, 32), c * LANES : (c + 1) * LANES]
            ref[k, c * 32 : (c + 1) * 32, :] = piece


def mixer_backward(dev_ref, dmix_ref, xnt_ref, wo_ref, small_ref, o_ref, u1_ref, u2_ref,
                   dk_ref, keep_ref, send_ref, bias_s, dh_s, grad_s):
    step = pl.program_id(0)
    blocks = pl.num_programs(0)
    width, tokens = xnt_ref.shape
    half = SLOTS // 2

    @pl.when(step == 0)
    def _():
        for b in range(dh_s.shape[0]):
            dh_s[b] = dot(dmix_ref[...], wo_ref[b * LANES : (b + 1) * LANES, :], ((1,), (1,)))

    zeros = jnp.zeros((CHUNKS, LANES), F32)
    tile = GROUP * CHUNKS
    count = tokens // tile

    def first(i, carry):
        g, prod, decay = carry
        at = aligned((count - 1 - i) * tile, tile)
        dh = dh_s[step, at, :]
        forget = 1.0 - o_ref[at, :].astype(F32)
        for k in reversed(range(GROUP)):
            part = slice(k * CHUNKS, (k + 1) * CHUNKS)
            g = dh[part] + decay * g
            prod = prod * decay
            decay = forget[part]
        return g, prod, decay

    ones = zeros + 1.0
    head, prod, decay = lax.fori_loop(0, count, first, (zeros, ones, ones))
    sub = lax.broadcasted_iota(jnp.int32, (CHUNKS, LANES), 0)
    start = zeros
    for s in reversed(range(1, CHUNKS)):
        moved = pltpu.roll(decay * (head + prod * start), CHUNKS - 1, 0)
        start = jnp.where(sub == s - 1, moved, start)

    def second(i, carry):
        g, decay, total = carry
        at = aligned((count - 1 - i) * tile, tile)
        dh = dh_s[step, at, :]
        other = o_ref[at, :].astype(F32)
        forget = 1.0 - other
        parts = [None] * GROUP
        for k in reversed(range(GROUP)):
            part = slice(k * CHUNKS, (k + 1) * CHUNKS)
            g = dh[part] + decay * g
            decay = forget[part]
            parts[k] = g
        grad = jnp.concatenate(parts, axis=0)
        dk_ref[at, 0:LANES] = (u1_ref[at, :].astype(F32) * grad).astype(BF)
        di = (u2_ref[at, :].astype(F32) * grad).astype(BF)
        dk_ref[at, LANES : 2 * LANES] = di
        dk_ref[at, 2 * LANES : 3 * LANES] = (other * grad).astype(BF)
        di = di.astype(F32)
        for k in range(GROUP):
            total = total + di[k * CHUNKS : (k + 1) * CHUNKS]
        return g, decay, total

    _, _, total = lax.fori_loop(0, count, second, (start, ones, zeros))
    bias_s[:, aligned(step * LANES, LANES)] = jnp.sum(total, axis=0, keepdims=True)

    grad_s[...] = dot(xnt_ref[...], dk_ref[...]).astype(BF)
    for s in range(SLOTS):
        target = keep_ref if s < half else send_ref
        src = aligned(dev_ref[s] * 16, 16)
        for w in range(3):
            dst = aligned((step * 3 + w) * 16, 16)
            target[s % half, dst, :] = grad_s[src, w * LANES : (w + 1) * LANES]

    @pl.when(step == blocks - 1)
    def _():
        bias = bias_s[...]
        piece = width // SLOTS
        values = small_ref[...] + collect(bias, 2 * piece, bias.shape[1] // SLOTS)
        dh_s[0, 0:SLOTS, :] = values
        row = lax.broadcasted_iota(jnp.int32, (16, LANES), 0)
        tail = keep_ref.shape[1] - 16
        for s in range(SLOTS):
            target = keep_ref if s < half else send_ref
            values = dh_s[0, pl.ds(dev_ref[s], 1), :]
            target[s % half, tail : tail + 16, :] = jnp.where(row == 0, values, 0.0).astype(BF)


def input_gradient(x_ref, dmix_ref, gain_ref, dk_ref, w_ref, out_ref):
    size = dk_ref.shape[2]
    dxn = dot(dk_ref[0], w_ref[:, :size], ((1,), (1,)))
    for b in range(1, dk_ref.shape[0]):
        dxn = dxn + dot(dk_ref[b], w_ref[:, b * size : (b + 1) * size], ((1,), (1,)))
    v = x_ref[...].astype(F32)
    scale = lax.rsqrt(jnp.mean(v * v, axis=-1, keepdims=True) + EPSILON)
    n1 = v * scale
    dn = dxn * gain_ref[0:1, :]
    out_ref[...] = dmix_ref[...].astype(F32) + scale * (dn - n1 * jnp.mean(dn * n1, axis=-1, keepdims=True))


def finish_mixer(own_ref, p0, p1, p2, forget_ref, input_ref, cand_ref, gain_ref,
                 fg_ref, ig_ref, cg_ref, gmix_ref, gmlp_ref, bias_ref):
    total = own_ref[...].astype(F32)
    for ref in (p0, p1, p2):
        total = total + ref[...].astype(F32)
    chans = fg_ref.shape[1]
    dots = jnp.zeros((16, 1), F32)
    for b in range(chans // LANES):
        cols = slice(b * LANES, (b + 1) * LANES)
        for w, (ref, weight) in enumerate(((fg_ref, forget_ref), (ig_ref, input_ref), (cg_ref, cand_ref))):
            grad = total[(b * 3 + w) * 16 : (b * 3 + w + 1) * 16]
            ref[:, cols] = grad
            dots = dots + jnp.sum(grad * weight[:, cols].astype(F32), axis=1, keepdims=True)
    row = jnp.broadcast_to(dots, (16, 128)).T[0:1, :]
    gmix_ref[...] = row / gain_ref[...].astype(F32)
    edge = total[chans // LANES * 48 : chans // LANES * 48 + 1]
    piece = gmlp_ref.shape[1]
    gmlp_ref[...] = edge[:, :piece]
    bias_ref[...] = edge[:, 2 * piece : 2 * piece + bias_ref.shape[1]]


def order_table():
    table = np.zeros((SLOTS, SLOTS), np.int32)
    for me in range(SLOTS):
        core, y, x, z = me & 1, me >> 1 & 1, me >> 2 & 1, me >> 3
        for slot in range(SLOTS):
            oc, second, first, oz = slot >> 4, slot >> 3 & 1, slot >> 2 & 1, (slot & 1) << 1 | slot >> 1 & 1
            c2 = core ^ oc
            x2 = x ^ (first if c2 == 0 else second)
            y2 = y ^ (second if c2 == 0 else first)
            table[me, slot] = ((z ^ oz) * 2 + x2) * 4 + y2 * 2 + c2
    return table


def flip(x0, y0, z0, c0, x1, y1, z1, c1):
    pairs = []
    for me in range(SLOTS):
        x, y, z, c = (x1, y1, z1, c1) if me & 1 else (x0, y0, z0, c0)
        pairs.append((me, me ^ (z << 3 | x << 2 | y << 1 | c)))
    return pairs


FAR, NEAR, BOTH = [flip(0, 0, k, 0, 0, 0, k, 0) for k in (2, 1, 3)]
FIRST = flip(1, 0, 0, 0, 0, 1, 0, 0)
SECOND = flip(0, 1, 0, 0, 1, 0, 0, 0)
CORE = flip(0, 0, 0, 1, 0, 0, 0, 1)


def send(value, pairs, name):
    with jax.named_scope(name):
        return lax.ppermute(value, AXES, pairs)


def after(value, *others):
    return lax.optimization_barrier((value,) + others)[0]


def after_all(*values):
    return lax.optimization_barrier(values)


def add(a, b):
    return (a.astype(F32) + b.astype(F32)).astype(BF)


def fold(low, high, pairs, name):
    got = send(high, pairs, name)
    half = low.shape[0] // 2
    return add(low[:half], got[:half]), add(low[half:], got[half:])


def pack(forget_weight, input_weight, candidate_weight, gain_mix, gain_mlp, input_gate_bias):
    rows = 3 * forget_weight.shape[1] // LANES * 16 + 16
    return pl.pallas_call(
        pack_mixer,
        out_shape=jax.ShapeDtypeStruct((rows, LANES), BF),
        scratch_shapes=[pltpu.VMEM((16, LANES), F32)],
        compiler_params=params(60),
        name="pack",
    )(forget_weight, input_weight, candidate_weight, gain_mix[None], gain_mlp[None], input_gate_bias[None])


def local(fast, tokens, gain_mix, gain_mlp, forget_weight, input_weight, candidate_weight, input_gate_bias,
          output_weight, up_weight, down_weight, cotangent):
    rows, width = tokens.shape
    chans = forget_weight.shape[1]
    blocks = chans // LANES
    shard = width // SLOTS

    def permute(v):
        return v.reshape(CHUNKS, rows // CHUNKS, width).transpose(1, 0, 2).reshape(rows, width)

    def restore(v):
        return v.reshape(rows // CHUNKS, CHUNKS, width).transpose(1, 0, 2).reshape(rows, width)

    xp = permute(tokens)
    dyp = permute(cotangent)
    def pack_feed(up, down, out):
        pieces = [v[:, c : c + LANES] for v in (up, down, out) for c in (0, LANES)]
        return jnp.concatenate([pieces[0], pieces[2], pieces[4], pieces[5]]), jnp.concatenate([pieces[1], pieces[3]])

    if fast:
        me = lax.axis_index(AXES)
        table = order_table()
        dev = lax.dynamic_index_in_dim(jnp.asarray(table), me, keepdims=False)
        piece = pack(forget_weight, input_weight, candidate_weight, gain_mix, gain_mlp, input_gate_bias)
        four = jnp.stack([piece] + [send(piece, p, "mixer_z") for p in (FAR, NEAR, BOTH)])
        piece1, piece2 = pack_feed(up_weight, down_weight.T, output_weight)
        four, piece1, piece2, *_ = after_all(four, piece1, piece2, dev, xp, dyp)
        got, far1 = after_all(send(four, FIRST, "mixer_first"), send(piece1, FAR, "feed1_far"))
        eight, two1, piece2 = after_all(jnp.concatenate([four, got]), jnp.stack([piece1, far1]), piece2)
        more, near1, far2 = after_all(
            send(eight, SECOND, "mixer_second"), send(two1, NEAR, "feed1_near"), send(piece2, FAR, "feed2_far")
        )
        more, four1, two2 = after_all(more, jnp.concatenate([two1, near1]), jnp.stack([piece2, far2]))
        got1, near2, core, core_more = after_all(
            send(four1, FIRST, "feed1_first"), send(two2, NEAR, "feed2_near"),
            send(eight, CORE, "mixer_core"), send(more, CORE, "mixer_core_more"),
        )
        eight1, four2 = jnp.concatenate([four1, got1]), jnp.concatenate([two2, near2])
        mixer, eight1, four2 = after_all((eight, more, core, core_more), eight1, four2)
        more1 = send(eight1, SECOND, "feed1_second")
        got2 = send(four2, FIRST, "feed2_first")
    else:
        order = np.argsort(np.arange(SLOTS) % 2, kind="stable").astype(np.int32)
        dev = jnp.asarray(order)

        def full(v, axis=0, names=AXES):
            return lax.all_gather(v, names, axis=axis, tiled=True)

        gm, gl, gb = full(gain_mix), full(gain_mlp), full(input_gate_bias)
        weights = [full(w) for w in (forget_weight, input_weight, candidate_weight)]
        smalls = [v.reshape(SLOTS, -1) for v in (gm, gl, gb)]
        up = full(full(up_weight, 0, "dp"), 1, "mp")
        down = full(full(down_weight, 1, "dp"), 0, "mp")

        def regroup(w):
            return w.reshape(8, width // 8, 4, width).transpose(0, 2, 1, 3).reshape(SLOTS, width // 8, width)

        both = [
            pack_feed(*v) for v in zip(regroup(up), regroup(down.T), full(output_weight).reshape(SLOTS, -1, width))
        ]

        def quarters(v):
            return tuple(jnp.stack([v[d] for d in order[k * 8 : (k + 1) * 8]]) for k in range(4))

        mixer = quarters(
            jnp.stack([pack(*[w[s * 16 : (s + 1) * 16] for w in weights], *[v[s] for v in smalls]) for s in range(SLOTS)])
        )
        feed1, feed2 = (quarters([v[k] for v in both]) for k in range(2))

    smem = pl.BlockSpec(memory_space=pltpu.SMEM)
    vmem = pl.BlockSpec(memory_space=pltpu.VMEM)
    part = 256

    def band(cols):
        return pl.BlockSpec((part, cols), lambda i: (i, 0))

    def shapes(*items):
        return [jax.ShapeDtypeStruct(shape, kind) for shape, kind in items]

    column = pl.BlockSpec((rows, LANES), lambda i: (0, i))
    block = pl.BlockSpec((None, rows, LANES), lambda i: (i, 0, 0))

    wide = pl.BlockSpec((width, 3 * LANES), lambda i: (0, i))
    hb, other, u1, u2, w3, xn1t, gains = pl.pallas_call(
        mixer_forward,
        grid=(blocks,),
        in_specs=[smem, whole((rows, width))] + [whole(mixer[0].shape)] * 4,
        out_specs=[column] + [block] * 3 + [wide, whole((width, rows)), whole((2, width))],
        out_shape=shapes(((rows, chans), BF), *[((blocks, rows, LANES), BF)] * 3,
                         ((width, 3 * chans), BF), ((width, rows), BF), ((2, width), F32)),
        scratch_shapes=[pltpu.VMEM((3, SLOTS, LANES), F32), pltpu.VMEM((1, chans), F32), pltpu.VMEM((rows, width), BF),
                        pltpu.VMEM((rows, 3 * LANES), F32), pltpu.VMEM((rows, LANES), F32),
                        pltpu.VMEM((rows, LANES), F32)],
        compiler_params=params(16),
        cost_estimate=pl.CostEstimate(flops=6 * rows * width * chans, bytes_accessed=32 << 20, transcendentals=0),
        name="mixer_forward",
    )(dev, xp, *mixer)
    if fast:
        core1 = send(eight1, CORE, "feed1_core")
        more1, got2, gains = after_all(more1, got2, gains)
        eight2 = jnp.concatenate([four2, got2])
        feed1 = (eight1, more1, core1, send(more1, CORE, "feed1_core_more"))

    size = width // 8

    def pieces(count):
        return [((slots, count, LANES), BF) for slots in (SLOTS // 4, SLOTS // 4, SLOTS // 2)]

    y1, xn2, xn2t, dyt, wo = pl.pallas_call(
        feed_prepare,
        in_specs=[smem] + [vmem] * 8,
        out_specs=[vmem] * 5,
        out_shape=shapes(((rows, width), F32), ((rows, width), BF), ((width, rows), BF), ((width, rows), BF), ((chans, width), BF)),
        compiler_params=params(16),
        cost_estimate=pl.CostEstimate(flops=2 * rows * width * chans, bytes_accessed=10 << 20, transcendentals=0),
        name="feed_prepare",
    )(dev, gains, *feed1, hb, xp, dyp)

    def feed(weights, *before):
        return pl.pallas_call(
            feed_half,
            in_specs=[smem] + [vmem] * (8 + len(before)),
            out_specs=[vmem] * 5,
            out_shape=shapes(((rows, width), F32), ((rows, width), F32), *pieces(2 * size)),
            scratch_shapes=[pltpu.VMEM((width, 2 * LANES), BF)] * 4,
            compiler_params=params(20),
            cost_estimate=pl.CostEstimate(flops=24 * rows * width * width, bytes_accessed=20 << 20, transcendentals=0),
            name="feed_last" if before else "feed_first",
        )(dev, *weights, xn2, xn2t, dyp, dyt, *before)

    if fast:
        more2 = send(eight2, SECOND, "feed2_second")
        core2 = send(eight2, CORE, "feed2_core")
    acc, dxn2, low1, high1, send1 = feed(feed1)
    if fast:
        half, quarter = SLOTS // 4, SLOTS // 8
        more2, core2, acc, dxn2, low1, high1, send1 = after_all(more2, core2, acc, dxn2, low1, high1, send1)
        feed2 = (eight2, more2, core2, send(more2, CORE, "feed2_core_more"))
        got1 = send(send1, CORE, "feed1_back_core")
        high1, acc, dxn2 = after_all(add(high1, got1[half:]), acc, dxn2)
        second1 = send(high1, SECOND, "feed1_back_second")
    acc, dxn2, low2, high2, send2 = feed(feed2, acc, dxn2)
    if fast:
        low1 = add(low1, got1[:half])
        second1, low1, acc, dxn2, low2, high2, send2 = after_all(second1, low1, acc, dxn2, low2, high2, send2)
        low1, high1 = add(low1[:quarter], second1[:quarter]), add(low1[quarter:], second1[quarter:])
        high1, acc, dxn2 = after_all(high1, acc, dxn2)
        first1 = send(high1, FIRST, "feed1_back_first")
        got2 = send(send2, CORE, "feed2_back_core")
    block_out, dmix, low_o, high_o, send_o, gmlp_small = pl.pallas_call(
        feed_finish,
        in_specs=[smem] + [vmem] * 6,
        out_specs=[vmem] * 6,
        out_shape=shapes(((rows, width), BF), ((rows, width), BF), *pieces(size), ((SLOTS, LANES), F32)),
        scratch_shapes=[pltpu.VMEM((chans, width), BF)],
        compiler_params=params(16),
        cost_estimate=pl.CostEstimate(flops=2 * rows * width * chans, bytes_accessed=10 << 20, transcendentals=0),
        name="feed_finish",
    )(dev, gains, hb, dyp, y1, acc, dxn2)
    if fast:
        first1, got2, dmix, low_o, high_o, send_o = after_all(first1, got2, dmix, low_o, high_o, send_o)
        got_o = send(send_o, CORE, "out_back_core")
        low1, high1 = add(low1[:2], first1[:2]), add(low1[2:], first1[2:])
        high2 = jnp.concatenate([add(high2, got2[half:]), add(high_o, got_o[half:])], axis=1)
        high1, high2, dmix = after_all(high1, high2, dmix)
        second2 = send(high2, SECOND, "feed2_back_second")
        near1 = send(high1, NEAR, "feed1_back_near")
    piece = (SLOTS // 2, 3 * blocks * 16 + 16, LANES)
    dk, keep3, send3 = pl.pallas_call(
        mixer_backward,
        grid=(blocks,),
        in_specs=[smem, whole((rows, width)), whole((width, rows)), whole((chans, width)), whole((SLOTS, LANES)),
                  block, block, block],
        out_specs=[pl.BlockSpec((None, rows, 3 * LANES), lambda i: (i, 0, 0))] + [whole(piece)] * 2,
        out_shape=shapes(((blocks, rows, 3 * LANES), BF), (piece, BF), (piece, BF)),
        scratch_shapes=[pltpu.VMEM((1, chans), F32), pltpu.VMEM((blocks, rows, LANES), F32),
                        pltpu.VMEM((width, 3 * LANES), BF)],
        compiler_params=params(16),
        cost_estimate=pl.CostEstimate(flops=8 * rows * width * chans, bytes_accessed=40 << 20, transcendentals=0),
        name="mixer_backward",
    )(dev, dmix, xn1t, wo, gmlp_small, other, u1, u2)

    def input_grad(dk_later):
        return pl.pallas_call(
            input_gradient,
            grid=(rows // part,),
            in_specs=[band(width), band(width), whole((2, width))] + [pl.BlockSpec((blocks, part, 3 * LANES), lambda i: (0, i, 0)), whole((width, 3 * chans))],
            out_specs=band(width),
            out_shape=jax.ShapeDtypeStruct((rows, width), F32),
            compiler_params=params(14),
            cost_estimate=pl.CostEstimate(flops=6 * rows * width * chans, bytes_accessed=24 << 20, transcendentals=0),
            name="input_gradient",
        )(xp, dmix, gains, dk_later, w3)

    def uncut(v):
        v = v[:, : 48 * blocks].reshape(-1, blocks, 3, 16, LANES)
        return [v[:, :, k].transpose(0, 2, 1, 3).reshape(-1, 16, chans) for k in range(3)]

    if fast:
        second2, near1, low1, low2, low_o, dk, send3, keep3 = after_all(second2, near1, low1, low2, low_o, dk, send3, keep3)
        low1, high1 = add(low1[0], near1[0]), add(low1[1], near1[1])
        low2 = jnp.concatenate([add(low2, got2[:half]), add(low_o, got_o[:half])], axis=1)
        low2, high2 = add(low2[:quarter], second2[:quarter]), add(low2[quarter:], second2[quarter:])
        high1, high2 = after_all(high1, high2)
        got = send(send3, CORE, "mixer_back_core")
        first2, far1 = send(high2, FIRST, "feed2_back_first"), send(high1, FAR, "feed1_back_far")
        mlow, mhigh = add(keep3[:half], got[:half]), add(keep3[half:], got[half:])
        first2, far1, mlow, mhigh, dk = after_all(first2, far1, mlow, mhigh, dk)
        first = low1.astype(F32) + far1.astype(F32)
        low2, high2 = add(low2[:2], first2[:2]), add(low2[2:], first2[2:])
        mhigh, high2 = after_all(mhigh, high2)
        got, near2, tokens_grad = after_all(
            send(mhigh, SECOND, "mixer_back_second"), send(high2, NEAR, "feed2_back_near"), input_grad(dk)
        )
        low2, high2 = add(low2[0], near2[0]), add(low2[1], near2[1])
        mlow, mhigh = add(mlow[:quarter], got[:quarter]), add(mlow[quarter:], got[quarter:])
        mlow, mhigh, low2, high2 = after_all(mlow, mhigh, low2, high2)
        got, far2 = after_all(send(mhigh, FIRST, "mixer_back_first"), send(high2, FAR, "feed2_back_far"))
        four = add(mlow, got)
        last = low2.astype(F32) + far2.astype(F32)
        parts = [send(four[k + 1], p, "mixer_back_z") for k, p in enumerate((FAR, NEAR, BOTH))]
        up_grad = jnp.concatenate([first[:size], last[:size]], axis=1)
        down_grad = jnp.concatenate([first[size:], last[size : 2 * size]], axis=1)
        out_grad = jnp.concatenate([last[2 * size : 2 * size + 32], last[2 * size + 32 :]], axis=1)
        down_grad = down_grad.T
        *grads, gmix_grad, gmlp_grad, bias_grad = pl.pallas_call(
            finish_mixer,
            out_shape=shapes(*[((16, chans), F32)] * 3, ((1, shard), F32), ((1, shard), F32), ((1, chans // SLOTS), F32)),
            compiler_params=params(16),
            name="finish",
        )(four[0], *parts, forget_weight, input_weight, candidate_weight, gain_mix[None])
        gmix_grad, gmlp_grad, bias_grad = gmix_grad[0], gmlp_grad[0], bias_grad[0]
    else:
        tokens_grad = input_grad(dk)
        first, last, out_grad, total = (
            jnp.stack([jnp.concatenate(v)[k] for k in np.argsort(order)]).astype(F32)
            for v in ((low1, high1, send1), (low2, high2, send2), (low_o, high_o, send_o), (keep3, send3))
        )

        def summed(v, axis=0, names=AXES):
            return lax.psum_scatter(v, names, scatter_dimension=axis, tiled=True)

        def joined(base):
            w = jnp.concatenate([first[:, base : base + size], last[:, base : base + size]], axis=2)
            return w.reshape(8, 4, size, width).transpose(0, 2, 1, 3).reshape(width, 4 * width)

        up_grad = summed(summed(joined(0), 0, "dp"), 1, "mp")
        down_grad = summed(summed(joined(size).T, 1, "dp"), 0, "mp")
        out_grad = jnp.concatenate([out_grad[:, :32], out_grad[:, 32:]], axis=2)
        out_grad = summed(out_grad.reshape(chans, width))
        grads = [summed(v.reshape(width, chans)) for v in uncut(total)]
        edge = total[:, 48 * blocks]
        gmlp_grad = summed(edge[:, :shard].reshape(-1))
        bias_grad = summed(edge[:, 2 * shard : 2 * shard + chans // SLOTS].reshape(-1))
        dots = sum(
            jnp.sum(w.astype(F32) * g, axis=1) for w, g in zip((forget_weight, input_weight, candidate_weight), grads)
        )
        gmix_grad = dots / gain_mix.astype(F32)

    return (restore(block_out), restore(tokens_grad), gmix_grad, gmlp_grad, grads[0], grads[1], grads[2], bias_grad,
            out_grad, up_grad, down_grad)


def solution(mesh):
    fast = mesh.shape["dp"] == 8 and mesh.shape["mp"] == 4
    every = P(AXES, None)
    in_specs = (every, P(AXES), P(AXES), every, every, every, P(AXES), every, P("dp", "mp"), P("mp", "dp"), every)
    out_specs = (every, every, P(AXES), P(AXES), every, every, every, P(AXES), every, P("dp", "mp"), P("mp", "dp"))
    return jax.shard_map(
        functools.partial(local, fast), mesh=mesh, in_specs=in_specs, out_specs=out_specs, check_vma=False
    )
```
